32 devices in a mesh: rows: 8 (over z, x), cols: 4 (over y, core).
Axes of the slice: x: 2, y: 2, z: 4, core: 2. Of those that a mesh axis runs over, the one named last changes fastest.
Arguments:
- field: bfloat16 [1, 18432, 18432], P(None, 'rows', 'cols'), may hold values from -48 to 48
Outputs:
- spectra: float32 [1, 1152, 2304], P(None, ('rows', 'cols'))
The draws below stay inside these ranges and needn't reach their ends.
All inputs are finite; a program needn't handle non-finite values.
Results may differ from the reference program's by a relative error of at most 0.0003.
The reference program's roundings to bfloat16 on the way (of `taps`) count: a program that leaves them out, or rounds other values in their place, can miss the bound.
Values may be sent and summed in bfloat16 or wider, within the bound.
No kernel may reach another device: no remote copies, remote signals or barrier semaphores. Data moves between devices by JAX's collectives and lax.ppermute only.
A program may use at most 64 MiB of HBM per device.

```python
import jax
import jax.numpy as jnp
from jax import lax

FIELDS = 1
NK = 2304
TAPS = 33
STRIDE = 8
NY = 18432
KH = 1152


def steps_of(stream_key, shape, shards, smallest, high):
    def one(dim, shards_of):
        draws = jax.random.uniform(jax.random.fold_in(jax.random.fold_in(stream_key, 6), dim), (shards_of,), jnp.float32, smallest / len(shards), high / len(shards))
        return jnp.repeat(jnp.exp(draws), shape[dim] // shards_of).reshape((-1,) + (1,) * (len(shape) - dim - 1))

    gain = one(*shards[0])
    for cut in shards[1:]:
        gain = gain * one(*cut)
    return gain


def normal_values(own_key, dims, width, limit, shards=(), kind=jnp.bfloat16):
    array = jax.random.normal(own_key, dims, jnp.float32) * width
    if len(shards) > 0:
        array = steps_of(own_key, dims, shards, -0.22, 0.18) * array
    return jnp.clip(array, min=-limit, max=limit).astype(kind)


def setup_inputs(seed: int = 0) -> dict:
    key_list = jax.random.split(jax.random.key(seed), 2)
    return {
        "field": normal_values(key_list[0], (FIELDS, NY, NY), 8.0, 48.0, ((1, 8), (2, 4))),
    }


def taps_table():
    tap_ids = jnp.arange(TAPS, dtype=jnp.float32)
    centre = TAPS // 2
    shaped = jnp.sinc((tap_ids - centre) / STRIDE) * (0.54 - 0.46 * jnp.cos(2 * jnp.pi * tap_ids / (TAPS - 1)))
    shaped = shaped / jnp.sum(shaped)
    rounded = lax.optimization_barrier(shaped.astype(jnp.bfloat16))
    return rounded.astype(jnp.float32)


def one_field(plane):
    taps = taps_table()
    tap_reach = TAPS // 2
    padded = jnp.pad(plane, ((tap_reach, tap_reach), (0, 0)))
    rowcut = jnp.zeros((NK, NY), jnp.float32)
    for tap_id in range(TAPS):
        rowcut = rowcut + taps[tap_id] * padded[tap_id:tap_id + STRIDE * NK:STRIDE, :].astype(jnp.float32)
    padded_cut = jnp.pad(rowcut, ((0, 0), (tap_reach, tap_reach)))
    cut = jnp.zeros((NK, NK), jnp.float32)
    for tap_id in range(TAPS):
        cut = cut + taps[tap_id] * padded_cut[:, tap_id:tap_id + STRIDE * NK:STRIDE]
    points = jnp.arange(NK, dtype=jnp.float32)
    window = 0.5 - 0.5 * jnp.cos(2 * jnp.pi * points / NK)
    tapered = cut * window[:, None] * window[None, :]
    transform = jnp.fft.rfft2(tapered)[:, :KH]
    power = (jnp.real(transform) * jnp.real(transform) + jnp.imag(transform) * jnp.imag(transform)) * (8.0 / (NK * NK))
    return power.T


def reference(field):
    return lax.map(one_field, field)
```

```python
import functools
import math

import jax
import jax.numpy as jnp
import ml_dtypes
import numpy as np
from jax import lax
from jax.experimental import pallas as pl
from jax.experimental.pallas import tpu as pltpu
from jax.sharding import PartitionSpec as P

TAPS = 33
STRIDE = 8
REACH = TAPS // 2
GROUP_COLS = 1536
GROUP_OUTS = GROUP_COLS // STRIDE
LANES = 128
INNER = 256
ROW_MARGIN = 8
HALO_OUTS = 2


def ceil_to(value, step):
    return -(-value // step) * step


def split_host(table):
    high = table.astype(ml_dtypes.bfloat16)
    low = (table - high.astype(np.float64)).astype(ml_dtypes.bfloat16)
    return high, low


def taps_host():
    ids = np.arange(TAPS, dtype=np.float64)
    shaped = np.sinc((ids - REACH) / STRIDE) * (0.54 - 0.46 * np.cos(2 * np.pi * ids / (TAPS - 1)))
    return (shaped / shaped.sum()).astype(ml_dtypes.bfloat16)


def band_host(span_in, span_out, first_out):
    tap_ids = np.arange(span_in)[:, None] - STRIDE * (np.arange(span_out)[None, :] - first_out) + REACH
    table = taps_host()
    inside = (tap_ids >= 0) & (tap_ids < TAPS)
    return np.where(inside, table[np.clip(tap_ids, 0, TAPS - 1)], 0).astype(ml_dtypes.bfloat16)


def angles_host(left, right, length):
    reduced = (np.asarray(left)[:, None] * np.asarray(right)[None, :]) % length
    return 2 * np.pi * reduced / length


def split(value):
    high = value.astype(jnp.bfloat16)
    low = (value - high.astype(jnp.float32)).astype(jnp.bfloat16)
    return high, low


def dot(left, right):
    return jnp.dot(left, right, preferred_element_type=jnp.float32)


def dot_nt(left, right):
    return lax.dot_general(left, right, (((1,), (1,)), ((), ())), preferred_element_type=jnp.float32)


def cut_kernel(shape, field, band_cols, band_rows, row_weight, col_weight, out, total, tapered):
    groups, block_outs, fold, owners, own_rows = shape
    step = pl.program_id(0)

    @pl.when(step == 0)
    def _():
        total[...] = jnp.zeros_like(total)

    begin = pl.multiple_of(step * block_outs, 8)
    for group in range(groups):
        raw = field[0, :, group * GROUP_COLS : (group + 1) * GROUP_COLS]
        high, low = split(dot(raw, band_cols[...]))
        term = dot(band_rows[...], high) + dot(band_rows[...], low)
        total[group, pl.ds(begin, band_rows.shape[0]), :] += term

    @pl.when(step == pl.num_programs(0) - 1)
    def _():
        rows = owners * own_rows + 2 * ROW_MARGIN
        middle = jnp.concatenate([total[1, :rows, :], jnp.zeros((rows, LANES), jnp.float32)], axis=1)
        middle = pltpu.roll(middle, 64, 1)
        joined = [
            total[0, :rows, :LANES],
            total[0, :rows, LANES:] + middle[:, :LANES],
            middle[:, LANES : 2 * LANES],
            middle[:, 2 * LANES :] + total[2, :rows, :LANES],
            total[2, :rows, LANES:],
        ]
        for place, piece in enumerate(joined):
            lanes = slice(place * LANES, (place + 1) * LANES)
            tapered[place] = piece * row_weight[...] * col_weight[:, lanes]
        sub = lax.broadcasted_iota(jnp.int32, (8, LANES), 0)
        ahead, behind = ROW_MARGIN - 8, ROW_MARGIN + owners * own_rows
        for place in range(len(joined)):
            lanes = slice(place * LANES, (place + 1) * LANES)
            for owner in range(owners):
                begin_at = ROW_MARGIN + owner * own_rows
                for part in range(fold):
                    count = own_rows // fold
                    out[owner, part * count : (part + 1) * count, lanes] = tapered[
                        pl.ds(place, 1), pl.ds(begin_at + part, count, stride=fold), :
                    ][0]
                edge = (6, 7, 0, 1)[owner]
                first = ahead if owner < 2 else behind
                block = tapered[place, first : first + 8, :]
                block = jnp.where(sub == edge, block, 0.0)
                out[owner, own_rows : own_rows + 8, lanes] = pltpu.roll(block, (8 - edge) % 8, 0)


def cut_filter(field, row_weight, col_weight, owners, fold):
    _, raw_rows, raw_cols = field.shape
    block_rows = next(size for size in (256, 192, 128, 64) if raw_rows % size == 0)
    groups = raw_cols // GROUP_COLS
    block_outs = block_rows // STRIDE
    own_rows = raw_rows // STRIDE // owners
    span = block_outs + 2 * ROW_MARGIN
    band_cols = band_host(GROUP_COLS, 2 * LANES, HALO_OUTS)
    band_rows = band_host(block_rows, span, ROW_MARGIN).T
    out_cols = col_weight.shape[1]
    shape = (groups, block_outs, fold, owners, own_rows)
    return pl.pallas_call(
        functools.partial(cut_kernel, shape),
        grid=(raw_rows // block_rows,),
        out_shape=jax.ShapeDtypeStruct((owners, own_rows + 8, out_cols), jnp.float32),
        in_specs=[
            pl.BlockSpec((1, block_rows, raw_cols), lambda i: (0, i, 0)),
            pl.BlockSpec(band_cols.shape, lambda i: (0, 0)),
            pl.BlockSpec(band_rows.shape, lambda i: (0, 0)),
            pl.BlockSpec(row_weight.shape, lambda i: (0, 0)),
            pl.BlockSpec(col_weight.shape, lambda i: (0, 0)),
        ],
        out_specs=pl.BlockSpec((owners, own_rows + 8, out_cols), lambda i: (0, 0, 0)),
        scratch_shapes=[
            pltpu.VMEM((groups, raw_rows // STRIDE + 2 * ROW_MARGIN, 2 * LANES), jnp.float32),
            pltpu.VMEM((out_cols // LANES, raw_rows // STRIDE + 2 * ROW_MARGIN, LANES), jnp.float32),
        ],
        compiler_params=pltpu.CompilerParams(vmem_limit_bytes=48 * 2**20),
    )(field, jnp.asarray(band_cols), jnp.asarray(band_rows), row_weight, col_weight)


def column_kernel(shape, blocks, twiddle, high_table, low_table, out, joined, high_rows, low_rows):
    owners, rows, own_cols, fold = shape
    joined[...] = jnp.zeros_like(joined)
    width = blocks.shape[2]
    for owner in range(owners):
        first = LANES + own_cols * owner - HALO_OUTS
        block = jnp.concatenate([blocks[owner], jnp.zeros((rows, LANES), jnp.float32)], axis=1)
        base = first // LANES * LANES
        joined[:, base : base + width + LANES] += pltpu.roll(block, first - base, 1)
    points = [joined[:, LANES + INNER * i : LANES + INNER * (i + 1)] for i in range(fold)]
    half = fold // 2
    sums = [points[j] + points[fold - j] for j in range(1, half + 1)]
    differences = [points[j] - points[fold - j] for j in range(1, half + 1)]
    used = rows * fold
    if high_rows.shape[0] > used:
        rest = jnp.zeros((high_rows.shape[0] - used, 2 * INNER), jnp.bfloat16)
        high_rows[used:, :] = rest
        low_rows[used:, :] = rest

    def keep(freq, real, imag):
        for side, value in enumerate((real, imag)):
            high, low = split(value)
            place = (slice(freq * rows, (freq + 1) * rows), slice(side * INNER, (side + 1) * INNER))
            high_rows[place] = high
            low_rows[place] = low

    def turned(freq, real, imag):
        tc = twiddle[freq : freq + 1, :INNER]
        ts = twiddle[freq : freq + 1, INNER:]
        keep(freq, real * tc + imag * ts, imag * tc - real * ts)

    keep(0, functools.reduce(jnp.add, sums, points[0]), jnp.zeros((rows, INNER), jnp.float32))
    for freq in range(1, half + 1):
        real, imag = points[0], None
        for j in range(1, half + 1):
            angle = 2 * math.pi * ((j * freq) % fold) / fold
            real = real + math.cos(angle) * sums[j - 1]
            term = -math.sin(angle) * differences[j - 1]
            imag = term if imag is None else imag + term
        turned(freq, real, imag)
        turned(fold - freq, real, -imag)
    result = dot_nt(high_table[...], high_rows[...])
    result += dot_nt(high_table[...], low_rows[...])
    result += dot_nt(low_table[...], high_rows[...])
    out[...] = result.reshape(out.shape)


def column_transform(blocks, length, devices):
    owners, rows, width = blocks.shape
    own_cols = length // owners
    fold = length // INNER
    kept = INNER // 2
    per_device = kept // devices
    angle = angles_host(np.arange(fold), np.arange(INNER), length)
    twiddle = np.concatenate([np.cos(angle), np.sin(angle)], axis=1).astype(np.float32)
    angle = angles_host(np.arange(kept), np.arange(INNER), INNER)
    table = np.stack(
        [
            np.concatenate([np.cos(angle), np.sin(angle)], axis=1),
            np.concatenate([-np.sin(angle), np.cos(angle)], axis=1),
        ]
    )
    table = table.reshape(2, devices, per_device, 2 * INNER).transpose(1, 0, 2, 3).reshape(INNER, 2 * INNER)
    high_table, low_table = split_host(table)
    lanes = ceil_to(fold * rows, LANES)
    return pl.pallas_call(
        functools.partial(column_kernel, (owners, rows, own_cols, fold)),
        out_shape=jax.ShapeDtypeStruct((devices, 2 * per_device, lanes), jnp.float32),
        scratch_shapes=[
            pltpu.VMEM((rows, length + 2 * LANES), jnp.float32),
            pltpu.VMEM((lanes, 2 * INNER), jnp.bfloat16),
            pltpu.VMEM((lanes, 2 * INNER), jnp.bfloat16),
        ],
        compiler_params=pltpu.CompilerParams(vmem_limit_bytes=48 * 2**20),
    )(blocks, jnp.asarray(twiddle), jnp.asarray(high_table), jnp.asarray(low_table))


def row_kernel(shape, arrived, twiddle, high_table, low_table, out, spread, folded):
    length, fold, step, parts, scale = shape
    devices, packed, width = arrived.shape
    per_device = packed // 2
    slots = LANES // step
    lane = lax.broadcasted_iota(jnp.int32, (packed, LANES), 1) // step
    sign = jnp.where(lax.broadcasted_iota(jnp.int32, (packed, INNER), 0) < per_device, 1.0, -1.0)

    for column in range(width // LANES):
        for half in range(devices // slots):
            tiles = [
                arrived[half * slots + g, :, column * LANES : (column + 1) * LANES] for g in range(slots)
            ]
            bit = 1
            while bit < slots:
                upper = (lane & bit) != 0
                for g in range(slots):
                    if g & bit:
                        continue
                    a, b = tiles[g], tiles[g + bit]
                    tiles[g] = jnp.where(upper, pltpu.roll(b, bit * step, 1), a)
                    tiles[g + bit] = jnp.where(upper, b, pltpu.roll(a, LANES - bit * step, 1))
                bit *= 2
            for g in range(slots):
                q = column * slots + g
                if q < fold * parts:
                    spread[q, :, half * LANES : (half + 1) * LANES] = tiles[g]

    def quarter(value):
        return pltpu.roll(value, per_device, 0) * sign

    place = lax.broadcasted_iota(jnp.int32, (packed, INNER), 1)
    for freq in range(fold):
        halo = spread[freq * parts + fold]
        run = 4 * step
        extra = {}
        for owner, (target, shift) in enumerate(
            ((fold - 2, -1), (fold - 1, -1 - step), (0, 2 * step), (1, step))
        ):
            only = jnp.where(place % run == owner * step, halo, 0.0)
            moved = pltpu.roll(only, shift % INNER, 1)
            extra[target] = extra[target] + moved if target in extra else moved
        for point in range(fold):
            value = spread[freq * parts + point]
            if point in extra:
                value = value + extra[point]
            folded[(point * fold + freq) * packed : (point * fold + freq + 1) * packed, :] = value

    high, low = split(folded[...])
    result = dot(high, high_table[...]) + dot(low, high_table[...]) + dot(high, low_table[...])
    for freq in range(fold):
        points = []
        for point in range(fold):
            begin = (point * fold + freq) * packed
            rows = slice(begin, begin + packed)
            value = result[rows, :INNER] + quarter(result[rows, INNER:])
            if point:
                tc = twiddle[point : point + 1, :INNER]
                ts = twiddle[point : point + 1, INNER:]
                value = value * tc + quarter(value) * ts
            points.append(value)
        half = fold // 2
        sums = [points[j] + points[fold - j] for j in range(1, half + 1)]
        differences = [quarter(points[j] - points[fold - j]) for j in range(1, half + 1)]

        def keep(index, value):
            power = value * value
            power = (power + pltpu.roll(power, per_device, 0)) * scale
            for own in range(per_device):
                row = own * fold + freq
                out[0, row : row + 1, index * INNER : (index + 1) * INNER] = power[own : own + 1]

        keep(0, functools.reduce(jnp.add, sums, points[0]))
        for index in range(1, half + 1):
            even, odd = points[0], None
            for j in range(1, half + 1):
                angle = 2 * math.pi * ((j * index) % fold) / fold
                even = even + math.cos(angle) * sums[j - 1]
                term = math.sin(angle) * differences[j - 1]
                odd = term if odd is None else odd + term
            keep(index, even + odd)
            keep(fold - index, even - odd)


def row_transform(arrived, length, rows):
    devices, packed, width = arrived.shape
    fold = length // INNER
    step = length // fold // devices
    angle = angles_host(np.arange(fold), np.arange(INNER), length)
    twiddle = np.concatenate([np.cos(angle), np.sin(angle)], axis=1).astype(np.float32)
    angle = angles_host(np.arange(INNER), np.arange(INNER), INNER)
    high_table, low_table = split_host(np.concatenate([np.cos(angle), np.sin(angle)], axis=1))
    parts = rows // step
    shape = (length, fold, step, parts, STRIDE / (length * length))
    return pl.pallas_call(
        functools.partial(row_kernel, shape),
        out_shape=jax.ShapeDtypeStruct((1, fold * packed // 2, length), jnp.float32),
        scratch_shapes=[
            pltpu.VMEM((fold * parts, packed, INNER), jnp.float32),
            pltpu.VMEM((fold * fold * packed, INNER), jnp.float32),
        ],
        compiler_params=pltpu.CompilerParams(vmem_limit_bytes=48 * 2**20),
    )(arrived, jnp.asarray(twiddle), jnp.asarray(high_table), jnp.asarray(low_table))


def taper(ids, length):
    weight = 0.5 - 0.5 * jnp.cos(2 * jnp.pi * ids.astype(jnp.float32) / length)
    return jnp.where((ids >= 0) & (ids < length), weight, 0.0)


def local(field):
    owners = lax.axis_size("cols")
    devices = lax.axis_size("rows") * owners
    own_rows = field.shape[1] // STRIDE
    own_cols = field.shape[2] // STRIDE
    length = own_rows * lax.axis_size("rows")
    fold = length // INNER
    lanes = ceil_to(own_cols + 2 * HALO_OUTS, LANES)
    row_ids = lax.axis_index("rows") * own_rows + jnp.arange(-ROW_MARGIN, own_rows + ROW_MARGIN)
    col_ids = lax.axis_index("cols") * own_cols + jnp.arange(-HALO_OUTS, lanes - HALO_OUTS)
    row_weight = taper(row_ids, length)[:, None]
    col_weight = taper(col_ids, length)[None, :]
    tapered = cut_filter(field, row_weight, col_weight, owners, fold)
    grouped = lax.all_to_all(tapered, "cols", split_axis=0, concat_axis=0, tiled=True)
    partial = column_transform(grouped, length, devices)
    arrived = lax.all_to_all(partial, ("rows", "cols"), split_axis=0, concat_axis=0, tiled=True)
    return row_transform(arrived, length, grouped.shape[1])


def solution(mesh):
    return jax.shard_map(
        local,
        mesh=mesh,
        in_specs=(P(None, "rows", "cols"),),
        out_specs=P(None, ("rows", "cols"), None),
        check_vma=False,
    )
```

```python
import functools
import math

import jax
import jax.numpy as jnp
import ml_dtypes
import numpy as np
from jax import lax
from jax.experimental import pallas as pl
from jax.experimental.pallas import tpu as pltpu
from jax.sharding import PartitionSpec as P

TAPS = 33
STRIDE = 8
REACH = TAPS // 2
GROUP_COLS = 1536
GROUP_OUTS = GROUP_COLS // STRIDE
LANES = 128
INNER = 256
COMPAND = 1023.0
LEVELS = 240
NONE_CODE = 2.0 ** -(LEVELS // 2)
ROW_MARGIN = 8
HALO_OUTS = 2


def ceil_to(value, step):
    return -(-value // step) * step


def split_host(table):
    high = table.astype(ml_dtypes.bfloat16)
    low = (table - high.astype(np.float64)).astype(ml_dtypes.bfloat16)
    return high, low


def taps_host():
    ids = np.arange(TAPS, dtype=np.float64)
    shaped = np.sinc((ids - REACH) / STRIDE) * (0.54 - 0.46 * np.cos(2 * np.pi * ids / (TAPS - 1)))
    return (shaped / shaped.sum()).astype(ml_dtypes.bfloat16)


def band(taps, tap_ids):
    table = jnp.zeros(tap_ids.shape, jnp.float32)
    for tap_id, tap in enumerate(taps):
        table = jnp.where(tap_ids == tap_id, tap, table)
    return table


def angles_host(left, right, length):
    reduced = (np.asarray(left)[:, None] * np.asarray(right)[None, :]) % length
    return 2 * np.pi * reduced / length


def taper_host(length):
    return (0.5 - 0.5 * np.cos(2 * np.pi * np.arange(length) / length)).astype(np.float32)


def split(value):
    high = value.astype(jnp.bfloat16)
    low = (value - high.astype(jnp.float32)).astype(jnp.bfloat16)
    return high, low


def row_scale(*arrays):
    peak = functools.reduce(jnp.maximum, [jnp.abs(array) for array in arrays])
    peak = jnp.max(peak, axis=-1, keepdims=True)
    return (peak * 1.01 + 1e-30).astype(jnp.bfloat16).astype(jnp.float32)


def encode(value, scale):
    level = jnp.log(1.0 + jnp.abs(value) * (COMPAND / scale)) * (LEVELS / math.log(1.001 * COMPAND))
    whole = jnp.floor(level)
    code = (1.0 + (level - whole)) * jnp.exp2(whole - LEVELS / 2)
    return jnp.where(value < 0, -code, code)


def decode(code, scale):
    size = jnp.abs(code)
    whole = jnp.floor(jnp.log2(size) + 0.0028)
    level = whole + (LEVELS / 2 - 1.0) + size * jnp.exp2(-whole)
    value = (jnp.exp(level * (math.log(1.001 * COMPAND) / LEVELS)) - 1.0) * (scale / COMPAND)
    return jnp.where(code < 0, -value, value)


def dot(left, right):
    return jnp.dot(left, right, preferred_element_type=jnp.float32)


def dot_nt(left, right):
    return lax.dot_general(left, right, (((1,), (1,)), ((), ())), preferred_element_type=jnp.float32)


def cut_kernel(shape, field, out, raw, arrived, band_rows, band_cols, total, cut, ordered):
    taps, chunks, groups, block_outs, fold, owners, own_rows = shape
    block_rows = raw.shape[1]

    def copy(chunk):
        rows = pl.ds(pl.multiple_of(chunk * block_rows, block_rows), block_rows)
        return pltpu.make_async_copy(field.at[0, rows, :], raw.at[chunk], arrived.at[chunk])

    for chunk in range(chunks):
        copy(chunk).start()
    total[...] = jnp.zeros_like(total)
    ids = lax.broadcasted_iota(jnp.int32, band_rows.shape, 1)
    ids = ids - STRIDE * (lax.broadcasted_iota(jnp.int32, band_rows.shape, 0) - ROW_MARGIN) + REACH
    band_rows[...] = band(taps, ids).astype(jnp.bfloat16)
    shape_8 = (8, band_cols.shape[1])
    ids = lax.broadcasted_iota(jnp.int32, shape_8, 0)
    ids = ids - STRIDE * (lax.broadcasted_iota(jnp.int32, shape_8, 1) - HALO_OUTS) + REACH
    initial = band(taps, ids)
    for pair in range(GROUP_COLS // 16):
        both = [pltpu.roll(initial, move, 1) if move else initial for move in (2 * pair, 2 * pair + 1)]
        band_cols[16 * pair : 16 * pair + 16, :] = jnp.concatenate(both, axis=0).astype(jnp.bfloat16)

    def step(chunk, carry):
        copy(chunk).wait()
        stacked = jnp.concatenate(
            [raw[chunk, :, group * GROUP_COLS : (group + 1) * GROUP_COLS] for group in range(groups)], axis=0
        )
        high, low = split(dot(stacked, band_cols[...]))
        rows = pl.ds(pl.multiple_of(chunk * block_outs, 8), band_rows.shape[0])
        for group in range(groups):
            own = slice(group * block_rows, (group + 1) * block_rows)
            term = dot(band_rows[...], high[own]) + dot(band_rows[...], low[own])
            total[group, rows, :] += term
        return carry

    lax.fori_loop(0, chunks, step, 0)
    count_rows = owners * own_rows + 2 * ROW_MARGIN
    middle = jnp.concatenate([total[1], jnp.zeros((count_rows, LANES), jnp.float32)], axis=1)
    middle = pltpu.roll(middle, 64, 1)
    cut[0] = total[0, :, :LANES]
    cut[1] = total[0, :, LANES:] + middle[:, :LANES]
    cut[2] = middle[:, LANES : 2 * LANES]
    cut[3] = middle[:, 2 * LANES :] + total[2, :, :LANES]
    cut[4] = total[2, :, LANES:]
    places = cut.shape[0]
    scale = row_scale(*[cut[place] for place in range(places)])
    last = lax.broadcasted_iota(jnp.int32, (count_rows, LANES), 1) == LANES - 1
    for place in range(places):
        code = encode(cut[place], scale)
        cut[place] = jnp.where(last, scale, code) if place == places - 1 else code
    used = own_rows + 8
    sub = lax.broadcasted_iota(jnp.int32, (8, LANES), 0)
    behind = ROW_MARGIN + owners * own_rows
    if ordered.shape[0] > used:
        ordered[used:, :] = jnp.full((ordered.shape[0] - used, ordered.shape[1]), NONE_CODE, jnp.float32)
    for owner in range(owners):
        begin_at = ROW_MARGIN + owner * own_rows
        count = own_rows // fold
        edge = (ROW_MARGIN - 2, ROW_MARGIN - 1, 0, 1)[owner]
        first = 0 if owner < 2 else behind
        for place in range(places):
            lanes = slice(place * LANES, (place + 1) * LANES)
            for part in range(fold):
                picked = cut[pl.ds(place, 1), pl.ds(begin_at + part, count, stride=fold), :]
                ordered[part * count : (part + 1) * count, lanes] = picked[0]
            block = pltpu.roll(cut[place, first : first + 8, :], (8 - edge) % 8, 0)
            ordered[own_rows:used, lanes] = jnp.where(sub == 0, block, NONE_CODE)
        out[owner] = ordered[...].astype(jnp.bfloat16)


def cut_filter(field, owners, fold):
    _, raw_rows, raw_cols = field.shape
    block_rows = next(size for size in (256, 192, 128, 64) if raw_rows % size == 0)
    chunks = raw_rows // block_rows
    groups = raw_cols // GROUP_COLS
    block_outs = block_rows // STRIDE
    own_rows = raw_rows // STRIDE // owners
    span = block_outs + 2 * ROW_MARGIN
    count_rows = raw_rows // STRIDE + 2 * ROW_MARGIN
    out_cols = ceil_to(raw_cols // STRIDE + 2 * HALO_OUTS, LANES)
    taps = [float(tap) for tap in taps_host()]
    shape = (taps, chunks, groups, block_outs, fold, owners, own_rows)
    out_rows = ceil_to(own_rows + 8, 16)
    return pl.pallas_call(
        functools.partial(cut_kernel, shape),
        out_shape=jax.ShapeDtypeStruct((owners, out_rows, out_cols), jnp.bfloat16),
        in_specs=[pl.BlockSpec(memory_space=pl.ANY)],
        out_specs=pl.BlockSpec(memory_space=pltpu.VMEM),
        scratch_shapes=[
            pltpu.VMEM((chunks, block_rows, raw_cols), jnp.bfloat16),
            pltpu.SemaphoreType.DMA((chunks,)),
            pltpu.VMEM((span, block_rows), jnp.bfloat16),
            pltpu.VMEM((GROUP_COLS, 2 * LANES), jnp.bfloat16),
            pltpu.VMEM((groups, count_rows, 2 * LANES), jnp.float32),
            pltpu.VMEM((out_cols // LANES, count_rows, LANES), jnp.float32),
            pltpu.VMEM((out_rows, out_cols), jnp.float32),
        ],
        compiler_params=pltpu.CompilerParams(vmem_limit_bytes=40 * 2**20),
    )(field)


def column_kernel(shape, blocks, weight, twiddle, high_table, low_table, out, joined, high_rows, low_rows):
    owners, rows, own_cols, fold = shape
    joined[...] = jnp.zeros_like(joined)
    width = blocks.shape[2]
    inside = lax.broadcasted_iota(jnp.int32, (rows, width), 1) < own_cols + 2 * HALO_OUTS
    for owner in range(owners):
        first = LANES + own_cols * owner - HALO_OUTS
        code = blocks[owner].astype(jnp.float32)
        value = decode(code, code[:, width - 1 :])
        value = jnp.where(inside, value, 0.0)
        block = jnp.concatenate([value, jnp.zeros((rows, LANES), jnp.float32)], axis=1)
        base = first // LANES * LANES
        joined[:, base : base + width + LANES] += pltpu.roll(block, first - base, 1)
    points = [
        joined[:, LANES + INNER * i : LANES + INNER * (i + 1)] * weight[:, INNER * i : INNER * (i + 1)]
        for i in range(fold)
    ]
    half = fold // 2
    sums = [points[j] + points[fold - j] for j in range(1, half + 1)]
    differences = [points[j] - points[fold - j] for j in range(1, half + 1)]
    used = rows * fold
    if high_rows.shape[0] > used:
        rest = jnp.zeros((high_rows.shape[0] - used, 2 * INNER), jnp.bfloat16)
        high_rows[used:, :] = rest
        low_rows[used:, :] = rest

    def keep(freq, real, imag):
        for side, value in enumerate((real, imag)):
            high, low = split(value)
            place = (slice(freq * rows, (freq + 1) * rows), slice(side * INNER, (side + 1) * INNER))
            high_rows[place] = high
            low_rows[place] = low

    def turned(freq, real, imag):
        tc = twiddle[freq : freq + 1, :INNER]
        ts = twiddle[freq : freq + 1, INNER:]
        keep(freq, real * tc + imag * ts, imag * tc - real * ts)

    keep(0, functools.reduce(jnp.add, sums, points[0]), jnp.zeros((rows, INNER), jnp.float32))
    for freq in range(1, half + 1):
        real, imag = points[0], None
        for j in range(1, half + 1):
            angle = 2 * math.pi * ((j * freq) % fold) / fold
            real = real + math.cos(angle) * sums[j - 1]
            term = -math.sin(angle) * differences[j - 1]
            imag = term if imag is None else imag + term
        turned(freq, real, imag)
        turned(fold - freq, real, -imag)
    result = dot_nt(high_table[...], high_rows[...])
    result += dot_nt(high_table[...], low_rows[...])
    result += dot_nt(low_table[...], high_rows[...])
    scale = row_scale(result)
    code = encode(result, scale)
    lane = lax.broadcasted_iota(jnp.int32, code.shape, 1)
    code = jnp.where(lane == code.shape[1] - 1, scale, code)
    devices, tall, wide = out.shape
    pieces = code.shape[1] // wide
    code = code.reshape(devices, tall // pieces, code.shape[1])
    code = [code[:, :, piece * wide : (piece + 1) * wide] for piece in range(pieces)]
    out[...] = jnp.concatenate(code, axis=1).astype(jnp.bfloat16)


def column_transform(blocks, length, devices):
    owners, rows, width = blocks.shape
    own_cols = length // owners
    fold = length // INNER
    kept = INNER // 2
    per_device = kept // devices
    angle = angles_host(np.arange(fold), np.arange(INNER), length)
    twiddle = np.concatenate([np.cos(angle), np.sin(angle)], axis=1).astype(np.float32)
    angle = angles_host(np.arange(kept), np.arange(INNER), INNER)
    table = np.stack(
        [
            np.concatenate([np.cos(angle), np.sin(angle)], axis=1),
            np.concatenate([-np.sin(angle), np.cos(angle)], axis=1),
        ]
    )
    table = table.reshape(2, devices, per_device, 2 * INNER).transpose(1, 0, 2, 3).reshape(INNER, 2 * INNER)
    high_table, low_table = split_host(table)
    pieces = max(16 // (2 * per_device), 1)
    lanes = ceil_to(fold * rows + 1, pieces * LANES)
    return pl.pallas_call(
        functools.partial(column_kernel, (owners, rows, own_cols, fold)),
        out_shape=jax.ShapeDtypeStruct((devices, pieces * 2 * per_device, lanes // pieces), jnp.bfloat16),
        scratch_shapes=[
            pltpu.VMEM((rows, length + 2 * LANES), jnp.float32),
            pltpu.VMEM((lanes, 2 * INNER), jnp.bfloat16),
            pltpu.VMEM((lanes, 2 * INNER), jnp.bfloat16),
        ],
        compiler_params=pltpu.CompilerParams(vmem_limit_bytes=48 * 2**20),
    )(blocks, jnp.asarray(taper_host(length)[None, :]), jnp.asarray(twiddle), jnp.asarray(high_table), jnp.asarray(low_table))


def row_kernel(shape, arrived, weight, twiddle, high_table, low_table, out, blocks, spread, folded):
    length, fold, step, parts, packed, factor = shape
    devices, tall, wide = arrived.shape
    per_device = packed // 2
    pieces = tall // packed
    code = arrived[...].astype(jnp.float32)
    scale = code[:, tall - packed :, wide - 1 :]
    value = decode(code, jnp.concatenate([scale] * pieces, axis=1))
    for piece in range(pieces):
        blocks[:, :, piece * wide : (piece + 1) * wide] = value[:, piece * packed : (piece + 1) * packed]
    width = blocks.shape[2]
    slots = LANES // step
    lane = lax.broadcasted_iota(jnp.int32, (packed, LANES), 1) // step
    sign = jnp.where(lax.broadcasted_iota(jnp.int32, (packed, INNER), 0) < per_device, 1.0, -1.0)

    for column in range(width // LANES):
        for half in range(devices // slots):
            tiles = [
                blocks[half * slots + g, :, column * LANES : (column + 1) * LANES] for g in range(slots)
            ]
            bit = 1
            while bit < slots:
                upper = (lane & bit) != 0
                for g in range(slots):
                    if g & bit:
                        continue
                    a, b = tiles[g], tiles[g + bit]
                    tiles[g] = jnp.where(upper, pltpu.roll(b, bit * step, 1), a)
                    tiles[g + bit] = jnp.where(upper, b, pltpu.roll(a, LANES - bit * step, 1))
                bit *= 2
            for g in range(slots):
                q = column * slots + g
                if q < fold * parts:
                    spread[q, :, half * LANES : (half + 1) * LANES] = tiles[g]

    def quarter(value):
        return pltpu.roll(value, per_device, 0) * sign

    place = lax.broadcasted_iota(jnp.int32, (packed, INNER), 1)
    for freq in range(fold):
        halo = spread[freq * parts + fold]
        run = 4 * step
        extra = {}
        for owner, (target, shift) in enumerate(
            ((fold - 2, -1), (fold - 1, -1 - step), (0, 2 * step), (1, step))
        ):
            inside = place != owner * step if owner < 2 else place != INNER - run + owner * step
            only = jnp.where((place % run == owner * step) & inside, halo, 0.0)
            moved = pltpu.roll(only, shift % INNER, 1)
            extra[target] = extra[target] + moved if target in extra else moved
        for point in range(fold):
            value = spread[freq * parts + point]
            if point in extra:
                value = value + extra[point]
            folded[(point * fold + freq) * packed : (point * fold + freq + 1) * packed, :] = (
                value * weight[point : point + 1, :]
            )

    high, low = split(folded[...])
    result = dot(high, high_table[...]) + dot(low, high_table[...]) + dot(high, low_table[...])
    for freq in range(fold):
        points = []
        for point in range(fold):
            begin = (point * fold + freq) * packed
            rows = slice(begin, begin + packed)
            value = result[rows, :INNER] + quarter(result[rows, INNER:])
            if point:
                tc = twiddle[point : point + 1, :INNER]
                ts = twiddle[point : point + 1, INNER:]
                value = value * tc + quarter(value) * ts
            points.append(value)
        half = fold // 2
        sums = [points[j] + points[fold - j] for j in range(1, half + 1)]
        differences = [quarter(points[j] - points[fold - j]) for j in range(1, half + 1)]

        def keep(index, value):
            power = value * value
            power = (power + pltpu.roll(power, per_device, 0)) * factor
            for side in range(INNER // LANES):
                row = (freq * length + index * INNER) // LANES + side
                rows = pl.ds(row, per_device, stride=fold * length // LANES)
                out[rows, :] = power[:per_device, side * LANES : (side + 1) * LANES]

        keep(0, functools.reduce(jnp.add, sums, points[0]))
        for index in range(1, half + 1):
            even, odd = points[0], None
            for j in range(1, half + 1):
                angle = 2 * math.pi * ((j * index) % fold) / fold
                even = even + math.cos(angle) * sums[j - 1]
                term = math.sin(angle) * differences[j - 1]
                odd = term if odd is None else odd + term
            keep(index, even + odd)
            keep(fold - index, even - odd)


def row_transform(arrived, length, rows):
    devices, tall, wide = arrived.shape
    packed = INNER // devices
    fold = length // INNER
    step = length // fold // devices
    angle = angles_host(np.arange(fold), np.arange(INNER), length)
    twiddle = np.concatenate([np.cos(angle), np.sin(angle)], axis=1).astype(np.float32)
    angle = angles_host(np.arange(INNER), np.arange(INNER), INNER)
    high_table, low_table = split_host(np.concatenate([np.cos(angle), np.sin(angle)], axis=1))
    parts = rows // step
    weight = np.ascontiguousarray(taper_host(length).reshape(INNER, fold).T)
    shape = (length, fold, step, parts, packed, STRIDE / (length * length))
    return pl.pallas_call(
        functools.partial(row_kernel, shape),
        out_shape=jax.ShapeDtypeStruct((fold * packed // 2 * length // LANES, LANES), jnp.float32),
        scratch_shapes=[
            pltpu.VMEM((devices, packed, tall * wide // packed), jnp.float32),
            pltpu.VMEM((fold * parts, packed, INNER), jnp.float32),
            pltpu.VMEM((fold * fold * packed, INNER), jnp.float32),
        ],
        compiler_params=pltpu.CompilerParams(vmem_limit_bytes=48 * 2**20),
    )(arrived, jnp.asarray(weight), jnp.asarray(twiddle), jnp.asarray(high_table), jnp.asarray(low_table))


def local(field):
    owners = lax.axis_size("cols")
    devices = lax.axis_size("rows") * owners
    length = field.shape[1] // STRIDE * lax.axis_size("rows")
    fold = length // INNER
    cut = cut_filter(field, owners, fold)
    grouped = lax.all_to_all(cut, "cols", split_axis=0, concat_axis=0, tiled=True)
    partial = column_transform(grouped, length, devices)
    arrived = lax.all_to_all(partial, ("rows", "cols"), split_axis=0, concat_axis=0, tiled=True)
    return row_transform(arrived, length, grouped.shape[1]).reshape(1, -1, length)


def solution(mesh):
    return jax.shard_map(
        local,
        mesh=mesh,
        in_specs=(P(None, "rows", "cols"),),
        out_specs=P(None, ("rows", "cols"), None),
        check_vma=False,
    )
```

```python
import functools
import math

import jax
import jax.numpy as jnp
import ml_dtypes
import numpy as np
from jax import lax
from jax.experimental import pallas as pl
from jax.experimental.pallas import tpu as pltpu
from jax.sharding import PartitionSpec as P

TAPS = 33
STRIDE = 8
REACH = TAPS // 2
GROUP_COLS = 1536
GROUP_OUTS = GROUP_COLS // STRIDE
LANES = 128
INNER = 256
COMPAND = 1023.0
LEVELS = 240
NONE_CODE = 2.0 ** -(LEVELS // 2)
ROW_MARGIN = 8
HALO_OUTS = 2


def ceil_to(value, step):
    return -(-value // step) * step


def split_host(table):
    high = table.astype(ml_dtypes.bfloat16)
    low = (table - high.astype(np.float64)).astype(ml_dtypes.bfloat16)
    return high, low


def taps_host():
    ids = np.arange(TAPS, dtype=np.float64)
    shaped = np.sinc((ids - REACH) / STRIDE) * (0.54 - 0.46 * np.cos(2 * np.pi * ids / (TAPS - 1)))
    return (shaped / shaped.sum()).astype(ml_dtypes.bfloat16)


def band(taps, tap_ids):
    table = jnp.zeros(tap_ids.shape, jnp.float32)
    for tap_id, tap in enumerate(taps):
        table = jnp.where(tap_ids == tap_id, tap, table)
    return table


def angles_host(left, right, length):
    reduced = (np.asarray(left)[:, None] * np.asarray(right)[None, :]) % length
    return 2 * np.pi * reduced / length


def taper_host(length):
    return (0.5 - 0.5 * np.cos(2 * np.pi * np.arange(length) / length)).astype(np.float32)


def split(value):
    high = value.astype(jnp.bfloat16)
    low = (value - high.astype(jnp.float32)).astype(jnp.bfloat16)
    return high, low


def row_scale(*arrays):
    peak = functools.reduce(jnp.maximum, [jnp.abs(array) for array in arrays])
    peak = jnp.max(peak, axis=-1, keepdims=True)
    return (peak * 1.01 + 1e-30).astype(jnp.bfloat16).astype(jnp.float32)


def encode(value, scale):
    level = jnp.log(1.0 + jnp.abs(value) * (COMPAND / scale)) * (LEVELS / math.log(1.001 * COMPAND))
    whole = jnp.floor(level)
    code = (1.0 + (level - whole)) * jnp.exp2(whole - LEVELS / 2)
    return jnp.where(value < 0, -code, code)


def decode(code, scale):
    size = jnp.abs(code)
    whole = jnp.floor(jnp.log2(size) + 0.0028)
    level = whole + (LEVELS / 2 - 1.0) + size * jnp.exp2(-whole)
    value = (jnp.exp(level * (math.log(1.001 * COMPAND) / LEVELS)) - 1.0) * (scale / COMPAND)
    return jnp.where(code < 0, -value, value)


def dot(left, right):
    return jnp.dot(left, right, preferred_element_type=jnp.float32)


def dot_nt(left, right):
    return lax.dot_general(left, right, (((1,), (1,)), ((), ())), preferred_element_type=jnp.float32)


def cut_kernel(shape, field, *refs):
    outs, refs = refs[: shape[-2]], refs[shape[-2] :]
    raw, arrived, band_rows, band_cols, sums_a, sums_b, total, cut, ordered = refs
    taps, chunks, groups, block_outs, fold, owners, own_rows = shape
    block_rows = raw.shape[1]

    def copy(chunk):
        rows = pl.ds(pl.multiple_of(chunk * block_rows, block_rows), block_rows)
        return pltpu.make_async_copy(field.at[0, rows, :], raw.at[chunk], arrived.at[chunk])

    for chunk in range(chunks):
        copy(chunk).start()
    total[...] = jnp.zeros_like(total)
    ids = lax.broadcasted_iota(jnp.int32, band_rows.shape, 1)
    ids = ids - STRIDE * (lax.broadcasted_iota(jnp.int32, band_rows.shape, 0) - ROW_MARGIN) + REACH
    band_rows[...] = band(taps, ids).astype(jnp.bfloat16)
    shape_8 = (8, band_cols.shape[1])
    ids = lax.broadcasted_iota(jnp.int32, shape_8, 0)
    ids = ids - STRIDE * (lax.broadcasted_iota(jnp.int32, shape_8, 1) - HALO_OUTS) + REACH
    initial = band(taps, ids)
    for pair in range(GROUP_COLS // 16):
        both = [pltpu.roll(initial, move, 1) if move else initial for move in (2 * pair, 2 * pair + 1)]
        band_cols[16 * pair : 16 * pair + 16, :] = jnp.concatenate(both, axis=0).astype(jnp.bfloat16)

    places = cut.shape[0]
    last = lax.broadcasted_iota(jnp.int32, (1, LANES), 1) == LANES - 1

    def filter_cols(chunk, sums):
        copy(chunk).wait()
        stacked = jnp.concatenate(
            [raw[chunk, :, group * GROUP_COLS : (group + 1) * GROUP_COLS] for group in range(groups)], axis=0
        )
        sums[...] = dot(stacked, band_cols[...])

    def finish(begin, count):
        rows = pl.ds(begin, count)
        middle = jnp.concatenate([total[1, rows, :], jnp.zeros((count, LANES), jnp.float32)], axis=1)
        middle = pltpu.roll(middle, 64, 1)
        joined = [
            total[0, rows, :LANES],
            total[0, rows, LANES:] + middle[:, :LANES],
            middle[:, LANES : 2 * LANES],
            middle[:, 2 * LANES :] + total[2, rows, :LANES],
            total[2, rows, LANES:],
        ]
        scale = row_scale(*joined)
        for place in range(places):
            code = encode(joined[place], scale)
            cut[place, rows, :] = jnp.where(last, scale, code) if place == places - 1 else code

    def filter_rows(chunk, sums):
        begin = pl.multiple_of(chunk * block_outs, 8)
        high, low = split(sums[...])
        rows = pl.ds(begin, band_rows.shape[0])
        for group in range(groups):
            own = slice(group * block_rows, (group + 1) * block_rows)
            term = dot(band_rows[...], high[own]) + dot(band_rows[...], low[own])
            total[group, rows, :] += term

    filter_cols(0, sums_a)

    def two(index, carry):
        filter_cols(2 * index + 1, sums_b)
        filter_rows(2 * index, sums_a)
        filter_cols(2 * index + 2, sums_a)
        filter_rows(2 * index + 1, sums_b)
        return carry

    lax.fori_loop(0, (chunks - 1) // 2, two, 0)
    if chunks % 2 == 0:
        filter_cols(chunks - 1, sums_b)
        filter_rows(chunks - 2, sums_a)
    filter_rows(chunks - 1, sums_a if chunks % 2 else sums_b)
    finish(0, owners * own_rows + 2 * ROW_MARGIN)
    used = own_rows + 8
    sub = lax.broadcasted_iota(jnp.int32, (8, LANES), 0)
    if ordered.shape[0] > used:
        ordered[used:, :] = jnp.full((ordered.shape[0] - used, ordered.shape[1]), NONE_CODE, jnp.float32)
    own_col = lax.axis_index("cols")
    for distance in range(owners):
        owner = own_col ^ distance
        count = own_rows // fold
        begin_at = ROW_MARGIN + owner * own_rows
        edge = jnp.where(owner < 2, ROW_MARGIN - 2 + owner, ROW_MARGIN + owners * own_rows + owner - 2)
        for place in range(places):
            lanes = slice(place * LANES, (place + 1) * LANES)
            for part in range(fold):
                picked = cut[pl.ds(place, 1), pl.ds(begin_at + part, count, stride=fold), :]
                ordered[part * count : (part + 1) * count, lanes] = picked[0]
            row = cut[pl.ds(place, 1), pl.ds(edge, 1), :][0]
            ordered[own_rows:used, lanes] = jnp.where(sub == 0, row, NONE_CODE)
        outs[distance][...] = ordered[...].astype(jnp.bfloat16)


def cut_filter(field, owners, fold):
    _, raw_rows, raw_cols = field.shape
    block_rows = next(size for size in (256, 192, 128, 64) if raw_rows % size == 0)
    chunks = raw_rows // block_rows
    groups = raw_cols // GROUP_COLS
    block_outs = block_rows // STRIDE
    own_rows = raw_rows // STRIDE // owners
    span = block_outs + 2 * ROW_MARGIN
    count_rows = raw_rows // STRIDE + 2 * ROW_MARGIN
    out_cols = ceil_to(raw_cols // STRIDE + 2 * HALO_OUTS, LANES)
    taps = [float(tap) for tap in taps_host()]
    shape = (taps, chunks, groups, block_outs, fold, owners, own_rows)
    out_rows = ceil_to(own_rows + 8, 16)
    return pl.pallas_call(
        functools.partial(cut_kernel, shape),
        out_shape=[jax.ShapeDtypeStruct((out_rows, out_cols), jnp.bfloat16)] * owners,
        in_specs=[pl.BlockSpec(memory_space=pl.ANY)],
        out_specs=[pl.BlockSpec(memory_space=pltpu.VMEM)] * owners,
        scratch_shapes=[
            pltpu.VMEM((chunks, block_rows, raw_cols), jnp.bfloat16),
            pltpu.SemaphoreType.DMA((chunks,)),
            pltpu.VMEM((span, block_rows), jnp.bfloat16),
            pltpu.VMEM((GROUP_COLS, 2 * LANES), jnp.bfloat16),
            pltpu.VMEM((groups * block_rows, 2 * LANES), jnp.float32),
            pltpu.VMEM((groups * block_rows, 2 * LANES), jnp.float32),
            pltpu.VMEM((groups, count_rows, 2 * LANES), jnp.float32),
            pltpu.VMEM((out_cols // LANES, count_rows, LANES), jnp.float32),
            pltpu.VMEM((out_rows, out_cols), jnp.float32),
        ],
        compiler_params=pltpu.CompilerParams(vmem_limit_bytes=40 * 2**20),
    )(field)


def column_kernel(shape, *refs):
    owners, rows, own_cols, fold = shape
    blocks, refs = refs[:owners], refs[owners:]
    weight, twiddle, high_table, low_table, out, joined, high_rows, low_rows = refs
    own_col = lax.axis_index("cols")
    joined[...] = jnp.zeros_like(joined)
    width = blocks[0].shape[1]
    inside = lax.broadcasted_iota(jnp.int32, (rows, width), 1) < own_cols + 2 * HALO_OUTS
    for distance in range(owners):
        first = LANES + own_cols * (own_col ^ distance) - HALO_OUTS
        code = blocks[distance][...].astype(jnp.float32)
        value = decode(code, code[:, width - 1 :])
        value = jnp.where(inside, value, 0.0)
        block = jnp.concatenate([value, jnp.zeros((rows, LANES), jnp.float32)], axis=1)
        base = pl.multiple_of(first // LANES * LANES, LANES)
        joined[:, pl.ds(base, width + LANES)] += pltpu.roll(block, first % LANES, 1)
    points = [
        joined[:, LANES + INNER * i : LANES + INNER * (i + 1)] * weight[:, INNER * i : INNER * (i + 1)]
        for i in range(fold)
    ]
    half = fold // 2
    sums = [points[j] + points[fold - j] for j in range(1, half + 1)]
    differences = [points[j] - points[fold - j] for j in range(1, half + 1)]
    used = rows * fold
    if high_rows.shape[0] > used:
        rest = jnp.zeros((high_rows.shape[0] - used, 2 * INNER), jnp.bfloat16)
        high_rows[used:, :] = rest
        low_rows[used:, :] = rest

    def keep(freq, real, imag):
        for side, value in enumerate((real, imag)):
            high, low = split(value)
            place = (slice(freq * rows, (freq + 1) * rows), slice(side * INNER, (side + 1) * INNER))
            high_rows[place] = high
            low_rows[place] = low

    def turned(freq, real, imag):
        tc = twiddle[freq : freq + 1, :INNER]
        ts = twiddle[freq : freq + 1, INNER:]
        keep(freq, real * tc + imag * ts, imag * tc - real * ts)

    keep(0, functools.reduce(jnp.add, sums, points[0]), jnp.zeros((rows, INNER), jnp.float32))
    for freq in range(1, half + 1):
        real, imag = points[0], None
        for j in range(1, half + 1):
            angle = 2 * math.pi * ((j * freq) % fold) / fold
            real = real + math.cos(angle) * sums[j - 1]
            term = -math.sin(angle) * differences[j - 1]
            imag = term if imag is None else imag + term
        turned(freq, real, imag)
        turned(fold - freq, real, -imag)
    result = dot_nt(high_table[...], high_rows[...])
    result += dot_nt(high_table[...], low_rows[...])
    result += dot_nt(low_table[...], high_rows[...])
    scale = row_scale(result)
    code = encode(result, scale)
    lane = lax.broadcasted_iota(jnp.int32, code.shape, 1)
    code = jnp.where(lane == code.shape[1] - 1, scale, code)
    devices, tall, wide = out.shape
    pieces = code.shape[1] // wide
    code = code.reshape(devices, tall // pieces, code.shape[1])
    code = [code[:, :, piece * wide : (piece + 1) * wide] for piece in range(pieces)]
    out[...] = jnp.concatenate(code, axis=1).astype(jnp.bfloat16)


def column_transform(blocks, length, devices):
    owners = len(blocks)
    rows, width = blocks[0].shape
    own_cols = length // owners
    fold = length // INNER
    kept = INNER // 2
    per_device = kept // devices
    angle = angles_host(np.arange(fold), np.arange(INNER), length)
    twiddle = np.concatenate([np.cos(angle), np.sin(angle)], axis=1).astype(np.float32)
    angle = angles_host(np.arange(kept), np.arange(INNER), INNER)
    table = np.stack(
        [
            np.concatenate([np.cos(angle), np.sin(angle)], axis=1),
            np.concatenate([-np.sin(angle), np.cos(angle)], axis=1),
        ]
    )
    table = table.reshape(2, devices, per_device, 2 * INNER).transpose(1, 0, 2, 3).reshape(INNER, 2 * INNER)
    high_table, low_table = split_host(table)
    pieces = max(16 // (2 * per_device), 1)
    lanes = ceil_to(fold * rows + 1, pieces * LANES)
    return pl.pallas_call(
        functools.partial(column_kernel, (owners, rows, own_cols, fold)),
        out_shape=jax.ShapeDtypeStruct((devices, pieces * 2 * per_device, lanes // pieces), jnp.bfloat16),
        scratch_shapes=[
            pltpu.VMEM((rows, length + 2 * LANES), jnp.float32),
            pltpu.VMEM((lanes, 2 * INNER), jnp.bfloat16),
            pltpu.VMEM((lanes, 2 * INNER), jnp.bfloat16),
        ],
        compiler_params=pltpu.CompilerParams(vmem_limit_bytes=48 * 2**20),
    )(*blocks, jnp.asarray(taper_host(length)[None, :]), jnp.asarray(twiddle), jnp.asarray(high_table), jnp.asarray(low_table))


def row_kernel(shape, arrived, weight, twiddle, high_table, low_table, out, blocks, spread, folded):
    length, fold, step, parts, packed, factor = shape
    devices, tall, wide = arrived.shape
    per_device = packed // 2
    pieces = tall // packed
    code = arrived[...].astype(jnp.float32)
    scale = code[:, tall - packed :, wide - 1 :]
    value = decode(code, jnp.concatenate([scale] * pieces, axis=1))
    for piece in range(pieces):
        blocks[:, :, piece * wide : (piece + 1) * wide] = value[:, piece * packed : (piece + 1) * packed]
    width = blocks.shape[2]
    slots = LANES // step
    lane = lax.broadcasted_iota(jnp.int32, (packed, LANES), 1) // step
    sign = jnp.where(lax.broadcasted_iota(jnp.int32, (packed, INNER), 0) < per_device, 1.0, -1.0)

    for column in range(width // LANES):
        for half in range(devices // slots):
            tiles = [
                blocks[half * slots + g, :, column * LANES : (column + 1) * LANES] for g in range(slots)
            ]
            bit = 1
            while bit < slots:
                upper = (lane & bit) != 0
                for g in range(slots):
                    if g & bit:
                        continue
                    a, b = tiles[g], tiles[g + bit]
                    tiles[g] = jnp.where(upper, pltpu.roll(b, bit * step, 1), a)
                    tiles[g + bit] = jnp.where(upper, b, pltpu.roll(a, LANES - bit * step, 1))
                bit *= 2
            for g in range(slots):
                q = column * slots + g
                if q < fold * parts:
                    spread[q, :, half * LANES : (half + 1) * LANES] = tiles[g]

    def quarter(value):
        return pltpu.roll(value, per_device, 0) * sign

    place = lax.broadcasted_iota(jnp.int32, (packed, INNER), 1)
    for freq in range(fold):
        halo = spread[freq * parts + fold]
        run = 4 * step
        extra = {}
        for owner, (target, shift) in enumerate(
            ((fold - 2, -1), (fold - 1, -1 - step), (0, 2 * step), (1, step))
        ):
            inside = place != owner * step if owner < 2 else place != INNER - run + owner * step
            only = jnp.where((place % run == owner * step) & inside, halo, 0.0)
            moved = pltpu.roll(only, shift % INNER, 1)
            extra[target] = extra[target] + moved if target in extra else moved
        for point in range(fold):
            value = spread[freq * parts + point]
            if point in extra:
                value = value + extra[point]
            folded[(point * fold + freq) * packed : (point * fold + freq + 1) * packed, :] = (
                value * weight[point : point + 1, :]
            )

    high, low = split(folded[...])
    result = dot(high, high_table[...]) + dot(low, high_table[...]) + dot(high, low_table[...])
    for freq in range(fold):
        points = []
        for point in range(fold):
            begin = (point * fold + freq) * packed
            rows = slice(begin, begin + packed)
            value = result[rows, :INNER] + quarter(result[rows, INNER:])
            if point:
                tc = twiddle[point : point + 1, :INNER]
                ts = twiddle[point : point + 1, INNER:]
                value = value * tc + quarter(value) * ts
            points.append(value)
        half = fold // 2
        sums = [points[j] + points[fold - j] for j in range(1, half + 1)]
        differences = [quarter(points[j] - points[fold - j]) for j in range(1, half + 1)]

        def keep(index, value):
            power = value * value
            power = (power + pltpu.roll(power, per_device, 0)) * factor
            for side in range(INNER // LANES):
                row = (freq * length + index * INNER) // LANES + side
                rows = pl.ds(row, per_device, stride=fold * length // LANES)
                out[rows, :] = power[:per_device, side * LANES : (side + 1) * LANES]

        keep(0, functools.reduce(jnp.add, sums, points[0]))
        for index in range(1, half + 1):
            even, odd = points[0], None
            for j in range(1, half + 1):
                angle = 2 * math.pi * ((j * index) % fold) / fold
                even = even + math.cos(angle) * sums[j - 1]
                term = math.sin(angle) * differences[j - 1]
                odd = term if odd is None else odd + term
            keep(index, even + odd)
            keep(fold - index, even - odd)


def row_transform(arrived, length, rows):
    devices, tall, wide = arrived.shape
    packed = INNER // devices
    fold = length // INNER
    step = length // fold // devices
    angle = angles_host(np.arange(fold), np.arange(INNER), length)
    twiddle = np.concatenate([np.cos(angle), np.sin(angle)], axis=1).astype(np.float32)
    angle = angles_host(np.arange(INNER), np.arange(INNER), INNER)
    high_table, low_table = split_host(np.concatenate([np.cos(angle), np.sin(angle)], axis=1))
    parts = rows // step
    weight = np.ascontiguousarray(taper_host(length).reshape(INNER, fold).T)
    shape = (length, fold, step, parts, packed, STRIDE / (length * length))
    return pl.pallas_call(
        functools.partial(row_kernel, shape),
        out_shape=jax.ShapeDtypeStruct((fold * packed // 2 * length // LANES, LANES), jnp.float32),
        scratch_shapes=[
            pltpu.VMEM((devices, packed, tall * wide // packed), jnp.float32),
            pltpu.VMEM((fold * parts, packed, INNER), jnp.float32),
            pltpu.VMEM((fold * fold * packed, INNER), jnp.float32),
        ],
        compiler_params=pltpu.CompilerParams(vmem_limit_bytes=48 * 2**20),
    )(arrived, jnp.asarray(weight), jnp.asarray(twiddle), jnp.asarray(high_table), jnp.asarray(low_table))


def local(field):
    owners = lax.axis_size("cols")
    devices = lax.axis_size("rows") * owners
    length = field.shape[1] // STRIDE * lax.axis_size("rows")
    fold = length // INNER
    cut = cut_filter(field, owners, fold)
    grouped = [cut[0]]
    for distance in range(1, owners):
        pairs = [(col, col ^ distance) for col in range(owners)]
        grouped.append(lax.ppermute(cut[distance], "cols", pairs))
    partial = column_transform(grouped, length, devices)
    arrived = lax.all_to_all(partial, ("rows", "cols"), split_axis=0, concat_axis=0, tiled=True)
    return row_transform(arrived, length, grouped[0].shape[0]).reshape(1, -1, length)


def solution(mesh):
    return jax.shard_map(
        local,
        mesh=mesh,
        in_specs=(P(None, "rows", "cols"),),
        out_specs=P(None, ("rows", "cols"), None),
        check_vma=False,
    )
```

```python
import functools
import math

import jax
import jax.numpy as jnp
import ml_dtypes
import numpy as np
from jax import lax
from jax.experimental import pallas as pl
from jax.experimental.pallas import tpu as pltpu
from jax.sharding import PartitionSpec as P

TAPS = 33
STRIDE = 8
REACH = TAPS // 2
GROUP_COLS = 1536
GROUP_OUTS = GROUP_COLS // STRIDE
LANES = 128
INNER = 256
COMPAND = 1023.0
LEVELS = 240
NONE_CODE = 2.0 ** -(LEVELS // 2)
ROW_MARGIN = 8
HALO_OUTS = 2


def ceil_to(value, step):
    return -(-value // step) * step


def split_host(table):
    high = table.astype(ml_dtypes.bfloat16)
    low = (table - high.astype(np.float64)).astype(ml_dtypes.bfloat16)
    return high, low


def taps_host():
    ids = np.arange(TAPS, dtype=np.float64)
    shaped = np.sinc((ids - REACH) / STRIDE) * (0.54 - 0.46 * np.cos(2 * np.pi * ids / (TAPS - 1)))
    return (shaped / shaped.sum()).astype(ml_dtypes.bfloat16)


def band(taps, tap_ids):
    table = jnp.zeros(tap_ids.shape, jnp.float32)
    for tap_id, tap in enumerate(taps):
        table = jnp.where(tap_ids == tap_id, tap, table)
    return table


def angles_host(left, right, length):
    reduced = (np.asarray(left)[:, None] * np.asarray(right)[None, :]) % length
    return 2 * np.pi * reduced / length


def taper_host(length):
    return (0.5 - 0.5 * np.cos(2 * np.pi * np.arange(length) / length)).astype(np.float32)


def split(value):
    high = value.astype(jnp.bfloat16)
    low = (value - high.astype(jnp.float32)).astype(jnp.bfloat16)
    return high, low


def row_scale(*arrays):
    peak = functools.reduce(jnp.maximum, [jnp.abs(array) for array in arrays])
    peak = jnp.max(peak, axis=-1, keepdims=True)
    return (peak * 1.01 + 1e-30).astype(jnp.bfloat16).astype(jnp.float32)


def encode(value, scale):
    level = jnp.log(1.0 + jnp.abs(value) * (COMPAND / scale)) * (LEVELS / math.log(1.001 * COMPAND))
    whole = jnp.floor(level)
    code = (1.0 + (level - whole)) * jnp.exp2(whole - LEVELS / 2)
    return jnp.where(value < 0, -code, code)


def decode(code, scale):
    size = jnp.abs(code)
    whole = jnp.floor(jnp.log2(size) + 0.0028)
    level = whole + (LEVELS / 2 - 1.0) + size * jnp.exp2(-whole)
    value = (jnp.exp(level * (math.log(1.001 * COMPAND) / LEVELS)) - 1.0) * (scale / COMPAND)
    return jnp.where(code < 0, -value, value)


def dot(left, right):
    return jnp.dot(left, right, preferred_element_type=jnp.float32)


def dot_nt(left, right):
    return lax.dot_general(left, right, (((1,), (1,)), ((), ())), preferred_element_type=jnp.float32)


def cut_kernel(shape, field, *refs):
    outs, refs = refs[: shape[-2]], refs[shape[-2] :]
    raw, arrived, band_rows, band_cols, sums_a, sums_b, total, cut, ordered, coded = refs
    taps, chunks, groups, block_outs, fold, owners, own_rows = shape
    block_rows = raw.shape[1]

    def copy(chunk):
        rows = pl.ds(pl.multiple_of(chunk * block_rows, block_rows), block_rows)
        return pltpu.make_async_copy(field.at[0, rows, :], raw.at[chunk], arrived.at[chunk])

    for chunk in range(chunks):
        copy(chunk).start()
    total[...] = jnp.zeros_like(total)
    ids = lax.broadcasted_iota(jnp.int32, band_rows.shape, 1)
    ids = ids - STRIDE * (lax.broadcasted_iota(jnp.int32, band_rows.shape, 0) - ROW_MARGIN) + REACH
    band_rows[...] = band(taps, ids).astype(jnp.bfloat16)
    shape_8 = (8, band_cols.shape[1])
    ids = lax.broadcasted_iota(jnp.int32, shape_8, 0)
    ids = ids - STRIDE * (lax.broadcasted_iota(jnp.int32, shape_8, 1) - HALO_OUTS) + REACH
    initial = band(taps, ids)
    for pair in range(GROUP_COLS // 16):
        both = [pltpu.roll(initial, move, 1) if move else initial for move in (2 * pair, 2 * pair + 1)]
        band_cols[16 * pair : 16 * pair + 16, :] = jnp.concatenate(both, axis=0).astype(jnp.bfloat16)

    places = cut.shape[0]
    last = lax.broadcasted_iota(jnp.int32, (1, LANES), 1) == LANES - 1

    def filter_cols(chunk, sums):
        copy(chunk).wait()
        stacked = jnp.concatenate(
            [raw[chunk, :, group * GROUP_COLS : (group + 1) * GROUP_COLS] for group in range(groups)], axis=0
        )
        sums[...] = dot(stacked, band_cols[...])

    def finish(begin, count):
        rows = pl.ds(begin, count)
        middle = jnp.concatenate([total[1, rows, :], jnp.zeros((count, LANES), jnp.float32)], axis=1)
        middle = pltpu.roll(middle, 64, 1)
        joined = [
            total[0, rows, :LANES],
            total[0, rows, LANES:] + middle[:, :LANES],
            middle[:, LANES : 2 * LANES],
            middle[:, 2 * LANES :] + total[2, rows, :LANES],
            total[2, rows, LANES:],
        ]
        scale = row_scale(*joined)
        for place in range(places):
            code = encode(joined[place], scale)
            cut[place, rows, :] = jnp.where(last, scale, code) if place == places - 1 else code

    def filter_rows(chunk, sums):
        begin = pl.multiple_of(chunk * block_outs, 8)
        high, low = split(sums[...])
        rows = pl.ds(begin, band_rows.shape[0])
        for group in range(groups):
            own = slice(group * block_rows, (group + 1) * block_rows)
            term = dot(band_rows[...], high[own]) + dot(band_rows[...], low[own])
            total[group, rows, :] += term
        finish(begin, block_outs)

    filter_cols(0, sums_a)

    def two(index, carry):
        filter_cols(2 * index + 1, sums_b)
        filter_rows(2 * index, sums_a)
        filter_cols(2 * index + 2, sums_a)
        filter_rows(2 * index + 1, sums_b)
        return carry

    lax.fori_loop(0, (chunks - 1) // 2, two, 0)
    if chunks % 2 == 0:
        filter_cols(chunks - 1, sums_b)
        filter_rows(chunks - 2, sums_a)
    filter_rows(chunks - 1, sums_a if chunks % 2 else sums_b)
    finish(owners * own_rows, 2 * ROW_MARGIN)
    used = own_rows + 8
    sub = lax.broadcasted_iota(jnp.int32, (8, LANES), 0)
    if ordered.shape[0] > used:
        ordered[used:, :] = jnp.full((ordered.shape[0] - used, ordered.shape[1]), NONE_CODE, jnp.float32)
    for owner in range(owners):
        count = own_rows // fold
        begin_at = ROW_MARGIN + owner * own_rows
        edge = (ROW_MARGIN - 2, ROW_MARGIN - 1, ROW_MARGIN + owners * own_rows, ROW_MARGIN + owners * own_rows + 1)[owner]
        for place in range(places):
            lanes = slice(place * LANES, (place + 1) * LANES)
            for part in range(fold):
                picked = cut[pl.ds(place, 1), pl.ds(begin_at + part, count, stride=fold), :]
                ordered[part * count : (part + 1) * count, lanes] = picked[0]
            row = cut[place, edge : edge + 1, :]
            ordered[own_rows:used, lanes] = jnp.where(sub == 0, row, NONE_CODE)
        coded[owner] = ordered[...].astype(jnp.bfloat16)
    own_col = lax.axis_index("cols")
    for distance in range(owners):
        outs[distance][...] = coded[own_col ^ distance]


def cut_filter(field, owners, fold):
    _, raw_rows, raw_cols = field.shape
    block_rows = next(size for size in (256, 192, 128, 64) if raw_rows % size == 0)
    chunks = raw_rows // block_rows
    groups = raw_cols // GROUP_COLS
    block_outs = block_rows // STRIDE
    own_rows = raw_rows // STRIDE // owners
    span = block_outs + 2 * ROW_MARGIN
    count_rows = raw_rows // STRIDE + 2 * ROW_MARGIN
    out_cols = ceil_to(raw_cols // STRIDE + 2 * HALO_OUTS, LANES)
    taps = [float(tap) for tap in taps_host()]
    shape = (taps, chunks, groups, block_outs, fold, owners, own_rows)
    out_rows = ceil_to(own_rows + 8, 16)
    return pl.pallas_call(
        functools.partial(cut_kernel, shape),
        out_shape=[jax.ShapeDtypeStruct((out_rows, out_cols), jnp.bfloat16)] * owners,
        in_specs=[pl.BlockSpec(memory_space=pl.ANY)],
        out_specs=[pl.BlockSpec(memory_space=pltpu.VMEM)] * owners,
        scratch_shapes=[
            pltpu.VMEM((chunks, block_rows, raw_cols), jnp.bfloat16),
            pltpu.SemaphoreType.DMA((chunks,)),
            pltpu.VMEM((span, block_rows), jnp.bfloat16),
            pltpu.VMEM((GROUP_COLS, 2 * LANES), jnp.bfloat16),
            pltpu.VMEM((groups * block_rows, 2 * LANES), jnp.float32),
            pltpu.VMEM((groups * block_rows, 2 * LANES), jnp.float32),
            pltpu.VMEM((groups, count_rows, 2 * LANES), jnp.float32),
            pltpu.VMEM((out_cols // LANES, count_rows, LANES), jnp.float32),
            pltpu.VMEM((out_rows, out_cols), jnp.float32),
            pltpu.VMEM((owners, out_rows, out_cols), jnp.bfloat16),
        ],
        compiler_params=pltpu.CompilerParams(vmem_limit_bytes=40 * 2**20),
    )(field)


def column_kernel(shape, *refs):
    owners, rows, own_cols, fold = shape
    blocks, refs = refs[:owners], refs[owners:]
    weight, twiddle, high_table, low_table, out, joined, high_rows, low_rows = refs
    own_col = lax.axis_index("cols")
    joined[...] = jnp.zeros_like(joined)
    width = blocks[0].shape[1]
    inside = lax.broadcasted_iota(jnp.int32, (rows, width), 1) < own_cols + 2 * HALO_OUTS
    for distance in range(owners):
        first = LANES + own_cols * (own_col ^ distance) - HALO_OUTS
        code = blocks[distance][...].astype(jnp.float32)
        value = decode(code, code[:, width - 1 :])
        value = jnp.where(inside, value, 0.0)
        block = jnp.concatenate([value, jnp.zeros((rows, LANES), jnp.float32)], axis=1)
        base = pl.multiple_of(first // LANES * LANES, LANES)
        joined[:, pl.ds(base, width + LANES)] += pltpu.roll(block, first % LANES, 1)
    points = [
        joined[:, LANES + INNER * i : LANES + INNER * (i + 1)] * weight[:, INNER * i : INNER * (i + 1)]
        for i in range(fold)
    ]
    half = fold // 2
    sums = [points[j] + points[fold - j] for j in range(1, half + 1)]
    differences = [points[j] - points[fold - j] for j in range(1, half + 1)]
    used = rows * fold
    if high_rows.shape[0] > used:
        rest = jnp.zeros((high_rows.shape[0] - used, 2 * INNER), jnp.bfloat16)
        high_rows[used:, :] = rest
        low_rows[used:, :] = rest

    def keep(freq, real, imag):
        for side, value in enumerate((real, imag)):
            high, low = split(value)
            place = (slice(freq * rows, (freq + 1) * rows), slice(side * INNER, (side + 1) * INNER))
            high_rows[place] = high
            low_rows[place] = low

    def turned(freq, real, imag):
        tc = twiddle[freq : freq + 1, :INNER]
        ts = twiddle[freq : freq + 1, INNER:]
        keep(freq, real * tc + imag * ts, imag * tc - real * ts)

    keep(0, functools.reduce(jnp.add, sums, points[0]), jnp.zeros((rows, INNER), jnp.float32))
    for freq in range(1, half + 1):
        real, imag = points[0], None
        for j in range(1, half + 1):
            angle = 2 * math.pi * ((j * freq) % fold) / fold
            real = real + math.cos(angle) * sums[j - 1]
            term = -math.sin(angle) * differences[j - 1]
            imag = term if imag is None else imag + term
        turned(freq, real, imag)
        turned(fold - freq, real, -imag)
    result = dot_nt(high_table[...], high_rows[...])
    result += dot_nt(high_table[...], low_rows[...])
    result += dot_nt(low_table[...], high_rows[...])
    scale = row_scale(result)
    code = encode(result, scale)
    lane = lax.broadcasted_iota(jnp.int32, code.shape, 1)
    code = jnp.where(lane == code.shape[1] - 1, scale, code)
    devices, tall, wide = out.shape
    pieces = code.shape[1] // wide
    code = code.reshape(devices, tall // pieces, code.shape[1])
    code = [code[:, :, piece * wide : (piece + 1) * wide] for piece in range(pieces)]
    out[...] = jnp.concatenate(code, axis=1).astype(jnp.bfloat16)


def column_transform(blocks, length, devices):
    owners = len(blocks)
    rows, width = blocks[0].shape
    own_cols = length // owners
    fold = length // INNER
    kept = INNER // 2
    per_device = kept // devices
    angle = angles_host(np.arange(fold), np.arange(INNER), length)
    twiddle = np.concatenate([np.cos(angle), np.sin(angle)], axis=1).astype(np.float32)
    angle = angles_host(np.arange(kept), np.arange(INNER), INNER)
    table = np.stack(
        [
            np.concatenate([np.cos(angle), np.sin(angle)], axis=1),
            np.concatenate([-np.sin(angle), np.cos(angle)], axis=1),
        ]
    )
    table = table.reshape(2, devices, per_device, 2 * INNER).transpose(1, 0, 2, 3).reshape(INNER, 2 * INNER)
    high_table, low_table = split_host(table)
    pieces = max(16 // (2 * per_device), 1)
    lanes = ceil_to(fold * rows + 1, pieces * LANES)
    return pl.pallas_call(
        functools.partial(column_kernel, (owners, rows, own_cols, fold)),
        out_shape=jax.ShapeDtypeStruct((devices, pieces * 2 * per_device, lanes // pieces), jnp.bfloat16),
        scratch_shapes=[
            pltpu.VMEM((rows, length + 2 * LANES), jnp.float32),
            pltpu.VMEM((lanes, 2 * INNER), jnp.bfloat16),
            pltpu.VMEM((lanes, 2 * INNER), jnp.bfloat16),
        ],
        compiler_params=pltpu.CompilerParams(vmem_limit_bytes=48 * 2**20),
    )(*blocks, jnp.asarray(taper_host(length)[None, :]), jnp.asarray(twiddle), jnp.asarray(high_table), jnp.asarray(low_table))


def row_kernel(shape, arrived, weight, twiddle, high_table, low_table, out, blocks, spread, folded):
    length, fold, step, parts, packed, factor = shape
    devices, tall, wide = arrived.shape
    per_device = packed // 2
    pieces = tall // packed
    code = arrived[...].astype(jnp.float32)
    scale = code[:, tall - packed :, wide - 1 :]
    value = decode(code, jnp.concatenate([scale] * pieces, axis=1))
    for piece in range(pieces):
        blocks[:, :, piece * wide : (piece + 1) * wide] = value[:, piece * packed : (piece + 1) * packed]
    width = blocks.shape[2]
    slots = LANES // step
    lane = lax.broadcasted_iota(jnp.int32, (packed, LANES), 1) // step
    sign = jnp.where(lax.broadcasted_iota(jnp.int32, (packed, INNER), 0) < per_device, 1.0, -1.0)

    for column in range(width // LANES):
        for half in range(devices // slots):
            tiles = [
                blocks[half * slots + g, :, column * LANES : (column + 1) * LANES] for g in range(slots)
            ]
            bit = 1
            while bit < slots:
                upper = (lane & bit) != 0
                for g in range(slots):
                    if g & bit:
                        continue
                    a, b = tiles[g], tiles[g + bit]
                    tiles[g] = jnp.where(upper, pltpu.roll(b, bit * step, 1), a)
                    tiles[g + bit] = jnp.where(upper, b, pltpu.roll(a, LANES - bit * step, 1))
                bit *= 2
            for g in range(slots):
                q = column * slots + g
                if q < fold * parts:
                    spread[q, :, half * LANES : (half + 1) * LANES] = tiles[g]

    def quarter(value):
        return pltpu.roll(value, per_device, 0) * sign

    place = lax.broadcasted_iota(jnp.int32, (packed, INNER), 1)
    for freq in range(fold):
        halo = spread[freq * parts + fold]
        run = 4 * step
        extra = {}
        for owner, (target, shift) in enumerate(
            ((fold - 2, -1), (fold - 1, -1 - step), (0, 2 * step), (1, step))
        ):
            inside = place != owner * step if owner < 2 else place != INNER - run + owner * step
            only = jnp.where((place % run == owner * step) & inside, halo, 0.0)
            moved = pltpu.roll(only, shift % INNER, 1)
            extra[target] = extra[target] + moved if target in extra else moved
        for point in range(fold):
            value = spread[freq * parts + point]
            if point in extra:
                value = value + extra[point]
            folded[(point * fold + freq) * packed : (point * fold + freq + 1) * packed, :] = (
                value * weight[point : point + 1, :]
            )

    high, low = split(folded[...])
    result = dot(high, high_table[...]) + dot(low, high_table[...]) + dot(high, low_table[...])
    for freq in range(fold):
        points = []
        for point in range(fold):
            begin = (point * fold + freq) * packed
            rows = slice(begin, begin + packed)
            value = result[rows, :INNER] + quarter(result[rows, INNER:])
            if point:
                tc = twiddle[point : point + 1, :INNER]
                ts = twiddle[point : point + 1, INNER:]
                value = value * tc + quarter(value) * ts
            points.append(value)
        half = fold // 2
        sums = [points[j] + points[fold - j] for j in range(1, half + 1)]
        differences = [quarter(points[j] - points[fold - j]) for j in range(1, half + 1)]

        def keep(index, value):
            power = value * value
            power = (power + pltpu.roll(power, per_device, 0)) * factor
            for side in range(INNER // LANES):
                row = (freq * length + index * INNER) // LANES + side
                rows = pl.ds(row, per_device, stride=fold * length // LANES)
                out[rows, :] = power[:per_device, side * LANES : (side + 1) * LANES]

        keep(0, functools.reduce(jnp.add, sums, points[0]))
        for index in range(1, half + 1):
            even, odd = points[0], None
            for j in range(1, half + 1):
                angle = 2 * math.pi * ((j * index) % fold) / fold
                even = even + math.cos(angle) * sums[j - 1]
                term = math.sin(angle) * differences[j - 1]
                odd = term if odd is None else odd + term
            keep(index, even + odd)
            keep(fold - index, even - odd)


def row_transform(arrived, length, rows):
    devices, tall, wide = arrived.shape
    packed = INNER // devices
    fold = length // INNER
    step = length // fold // devices
    angle = angles_host(np.arange(fold), np.arange(INNER), length)
    twiddle = np.concatenate([np.cos(angle), np.sin(angle)], axis=1).astype(np.float32)
    angle = angles_host(np.arange(INNER), np.arange(INNER), INNER)
    high_table, low_table = split_host(np.concatenate([np.cos(angle), np.sin(angle)], axis=1))
    parts = rows // step
    weight = np.ascontiguousarray(taper_host(length).reshape(INNER, fold).T)
    shape = (length, fold, step, parts, packed, STRIDE / (length * length))
    return pl.pallas_call(
        functools.partial(row_kernel, shape),
        out_shape=jax.ShapeDtypeStruct((fold * packed // 2 * length // LANES, LANES), jnp.float32),
        scratch_shapes=[
            pltpu.VMEM((devices, packed, tall * wide // packed), jnp.float32),
            pltpu.VMEM((fold * parts, packed, INNER), jnp.float32),
            pltpu.VMEM((fold * fold * packed, INNER), jnp.float32),
        ],
        compiler_params=pltpu.CompilerParams(vmem_limit_bytes=48 * 2**20),
    )(arrived, jnp.asarray(weight), jnp.asarray(twiddle), jnp.asarray(high_table), jnp.asarray(low_table))


def local(field):
    owners = lax.axis_size("cols")
    devices = lax.axis_size("rows") * owners
    length = field.shape[1] // STRIDE * lax.axis_size("rows")
    fold = length // INNER
    cut = cut_filter(field, owners, fold)
    grouped = [cut[0]]
    for distance in range(1, owners):
        pairs = [(col, col ^ distance) for col in range(owners)]
        grouped.append(lax.ppermute(cut[distance], "cols", pairs))
    partial = column_transform(grouped, length, devices)
    arrived = lax.all_to_all(partial, ("rows", "cols"), split_axis=0, concat_axis=0, tiled=True)
    return row_transform(arrived, length, grouped[0].shape[0]).reshape(1, -1, length)


def solution(mesh):
    return jax.shard_map(
        local,
        mesh=mesh,
        in_specs=(P(None, "rows", "cols"),),
        out_specs=P(None, ("rows", "cols"), None),
        check_vma=False,
    )
```

```python
import functools
import math

import jax
import jax.numpy as jnp
import ml_dtypes
import numpy as np
from jax import lax
from jax.experimental import pallas as pl
from jax.experimental.pallas import tpu as pltpu
from jax.sharding import PartitionSpec as P

TAPS = 33
STRIDE = 8
REACH = TAPS // 2
GROUP_COLS = 1536
GROUP_OUTS = GROUP_COLS // STRIDE
LANES = 128
INNER = 256
COMPAND = 1023.0
LEVELS = 240
NONE_CODE = 2.0 ** -(LEVELS // 2)
ROW_MARGIN = 8
HALO_OUTS = 2


def ceil_to(value, step):
    return -(-value // step) * step


def split_host(table):
    high = table.astype(ml_dtypes.bfloat16)
    low = (table - high.astype(np.float64)).astype(ml_dtypes.bfloat16)
    return high, low


def taps_host():
    ids = np.arange(TAPS, dtype=np.float64)
    shaped = np.sinc((ids - REACH) / STRIDE) * (0.54 - 0.46 * np.cos(2 * np.pi * ids / (TAPS - 1)))
    return (shaped / shaped.sum()).astype(ml_dtypes.bfloat16)


def band(taps, tap_ids):
    table = jnp.zeros(tap_ids.shape, jnp.float32)
    for tap_id, tap in enumerate(taps):
        table = jnp.where(tap_ids == tap_id, tap, table)
    return table


def angles_host(left, right, length):
    reduced = (np.asarray(left)[:, None] * np.asarray(right)[None, :]) % length
    return 2 * np.pi * reduced / length


def taper_host(length):
    return (0.5 - 0.5 * np.cos(2 * np.pi * np.arange(length) / length)).astype(np.float32)


def split(value):
    high = value.astype(jnp.bfloat16)
    low = (value - high.astype(jnp.float32)).astype(jnp.bfloat16)
    return high, low


def row_scale(*arrays):
    peak = functools.reduce(jnp.maximum, [jnp.abs(array) for array in arrays])
    peak = jnp.max(peak, axis=-1, keepdims=True)
    return (peak * 1.01 + 1e-30).astype(jnp.bfloat16).astype(jnp.float32)


def encode(value, scale):
    level = jnp.log(1.0 + jnp.abs(value) * (COMPAND / scale)) * (LEVELS / math.log(1.001 * COMPAND))
    whole = jnp.floor(level)
    code = (1.0 + (level - whole)) * jnp.exp2(whole - LEVELS / 2)
    return jnp.where(value < 0, -code, code)


def decode(code, scale):
    size = jnp.abs(code)
    whole = jnp.floor(jnp.log2(size) + 0.0028)
    level = whole + (LEVELS / 2 - 1.0) + size * jnp.exp2(-whole)
    value = (jnp.exp(level * (math.log(1.001 * COMPAND) / LEVELS)) - 1.0) * (scale / COMPAND)
    return jnp.where(code < 0, -value, value)


def dot(left, right):
    return jnp.dot(left, right, preferred_element_type=jnp.float32)


def dot_nt(left, right):
    return lax.dot_general(left, right, (((1,), (1,)), ((), ())), preferred_element_type=jnp.float32)


def cut_kernel(shape, field, *refs):
    outs, refs = refs[: shape[-2]], refs[shape[-2] :]
    raw, arrived, band_rows, band_cols, total, cut, ordered, coded = refs
    taps, chunks, groups, block_outs, fold, owners, own_rows = shape
    block_rows = raw.shape[1]

    def copy(chunk):
        rows = pl.ds(pl.multiple_of(chunk * block_rows, block_rows), block_rows)
        return pltpu.make_async_copy(field.at[0, rows, :], raw.at[chunk], arrived.at[chunk])

    for chunk in range(chunks):
        copy(chunk).start()
    total[...] = jnp.zeros_like(total)
    shape_rows = (band_rows.shape[0], block_rows)
    ids = lax.broadcasted_iota(jnp.int32, shape_rows, 1)
    ids = ids - STRIDE * (lax.broadcasted_iota(jnp.int32, shape_rows, 0) - ROW_MARGIN) + REACH
    rows_band = band(taps, ids).astype(jnp.bfloat16)
    band_rows[...] = jnp.concatenate([rows_band, rows_band], axis=1)
    shape_8 = (8, band_cols.shape[1])
    ids = lax.broadcasted_iota(jnp.int32, shape_8, 0)
    ids = ids - STRIDE * (lax.broadcasted_iota(jnp.int32, shape_8, 1) - HALO_OUTS) + REACH
    initial = band(taps, ids)
    for pair in range(GROUP_COLS // 16):
        both = [pltpu.roll(initial, move, 1) if move else initial for move in (2 * pair, 2 * pair + 1)]
        band_cols[16 * pair : 16 * pair + 16, :] = jnp.concatenate(both, axis=0).astype(jnp.bfloat16)

    places = cut.shape[0]
    last = lax.broadcasted_iota(jnp.int32, (1, LANES), 1) == LANES - 1

    def finish(begin, count):
        rows = pl.ds(begin, count)
        middle = jnp.concatenate([total[1, rows, :], jnp.zeros((count, LANES), jnp.float32)], axis=1)
        middle = pltpu.roll(middle, 64, 1)
        joined = [
            total[0, rows, :LANES],
            total[0, rows, LANES:] + middle[:, :LANES],
            middle[:, LANES : 2 * LANES],
            middle[:, 2 * LANES :] + total[2, rows, :LANES],
            total[2, rows, LANES:],
        ]
        scale = row_scale(*joined)
        for place in range(places):
            code = encode(joined[place], scale)
            cut[place, rows, :] = jnp.where(last, scale, code) if place == places - 1 else code

    def step(chunk, carry):
        copy(chunk).wait()
        begin = pl.multiple_of(chunk * block_outs, 8)
        rows = pl.ds(begin, band_rows.shape[0])
        for group in range(groups):
            high, low = split(dot(raw[chunk, :, group * GROUP_COLS : (group + 1) * GROUP_COLS], band_cols[...]))
            total[group, rows, :] += dot(band_rows[...], jnp.concatenate([high, low], axis=0))
        return carry

    lax.fori_loop(0, chunks, step, 0)
    finish(0, owners * own_rows + 2 * ROW_MARGIN)
    used = own_rows + 8
    sub = lax.broadcasted_iota(jnp.int32, (8, LANES), 0)
    if ordered.shape[0] > used:
        ordered[used:, :] = jnp.full((ordered.shape[0] - used, ordered.shape[1]), NONE_CODE, jnp.float32)
    for owner in range(owners):
        count = own_rows // fold
        begin_at = ROW_MARGIN + owner * own_rows
        edge = (ROW_MARGIN - 2, ROW_MARGIN - 1, ROW_MARGIN + owners * own_rows, ROW_MARGIN + owners * own_rows + 1)[owner]
        for place in range(places):
            lanes = slice(place * LANES, (place + 1) * LANES)
            for part in range(fold):
                picked = cut[pl.ds(place, 1), pl.ds(begin_at + part, count, stride=fold), :]
                ordered[part * count : (part + 1) * count, lanes] = picked[0]
            row = cut[place, edge : edge + 1, :]
            ordered[own_rows:used, lanes] = jnp.where(sub == 0, row, NONE_CODE)
        coded[owner] = ordered[...].astype(jnp.bfloat16)
    own_col = lax.axis_index("cols")
    for distance in range(owners):
        outs[distance][...] = coded[own_col ^ distance]


def cut_filter(field, owners, fold):
    _, raw_rows, raw_cols = field.shape
    block_rows = next(size for size in (256, 192, 128, 64) if raw_rows % size == 0)
    chunks = raw_rows // block_rows
    groups = raw_cols // GROUP_COLS
    block_outs = block_rows // STRIDE
    own_rows = raw_rows // STRIDE // owners
    span = block_outs + 2 * ROW_MARGIN
    count_rows = raw_rows // STRIDE + 2 * ROW_MARGIN
    out_cols = ceil_to(raw_cols // STRIDE + 2 * HALO_OUTS, LANES)
    taps = [float(tap) for tap in taps_host()]
    shape = (taps, chunks, groups, block_outs, fold, owners, own_rows)
    out_rows = ceil_to(own_rows + 8, 16)
    return pl.pallas_call(
        functools.partial(cut_kernel, shape),
        out_shape=[jax.ShapeDtypeStruct((out_rows, out_cols), jnp.bfloat16)] * owners,
        in_specs=[pl.BlockSpec(memory_space=pl.ANY)],
        out_specs=[pl.BlockSpec(memory_space=pltpu.VMEM)] * owners,
        scratch_shapes=[
            pltpu.VMEM((chunks, block_rows, raw_cols), jnp.bfloat16),
            pltpu.SemaphoreType.DMA((chunks,)),
            pltpu.VMEM((span, 2 * block_rows), jnp.bfloat16),
            pltpu.VMEM((GROUP_COLS, 2 * LANES), jnp.bfloat16),
            pltpu.VMEM((groups, count_rows, 2 * LANES), jnp.float32),
            pltpu.VMEM((out_cols // LANES, count_rows, LANES), jnp.float32),
            pltpu.VMEM((out_rows, out_cols), jnp.float32),
            pltpu.VMEM((owners, out_rows, out_cols), jnp.bfloat16),
        ],
        compiler_params=pltpu.CompilerParams(vmem_limit_bytes=40 * 2**20),
    )(field)


def column_kernel(shape, *refs):
    owners, rows, own_cols, fold = shape
    blocks, refs = refs[:owners], refs[owners:]
    weight, twiddle, high_table, low_table, out, joined, high_rows, low_rows = refs
    own_col = lax.axis_index("cols")
    joined[...] = jnp.zeros_like(joined)
    width = blocks[0].shape[1]
    inside = lax.broadcasted_iota(jnp.int32, (rows, width), 1) < own_cols + 2 * HALO_OUTS
    for distance in range(owners):
        first = LANES + own_cols * (own_col ^ distance) - HALO_OUTS
        code = blocks[distance][...].astype(jnp.float32)
        value = decode(code, code[:, width - 1 :])
        value = jnp.where(inside, value, 0.0)
        block = jnp.concatenate([value, jnp.zeros((rows, LANES), jnp.float32)], axis=1)
        base = pl.multiple_of(first // LANES * LANES, LANES)
        joined[:, pl.ds(base, width + LANES)] += pltpu.roll(block, first % LANES, 1)
    points = [
        joined[:, LANES + INNER * i : LANES + INNER * (i + 1)] * weight[:, INNER * i : INNER * (i + 1)]
        for i in range(fold)
    ]
    half = fold // 2
    sums = [points[j] + points[fold - j] for j in range(1, half + 1)]
    differences = [points[j] - points[fold - j] for j in range(1, half + 1)]
    used = rows * fold
    if high_rows.shape[0] > used:
        rest = jnp.zeros((high_rows.shape[0] - used, 2 * INNER), jnp.bfloat16)
        high_rows[used:, :] = rest
        low_rows[used:, :] = rest

    def keep(freq, real, imag):
        for side, value in enumerate((real, imag)):
            high, low = split(value)
            place = (slice(freq * rows, (freq + 1) * rows), slice(side * INNER, (side + 1) * INNER))
            high_rows[place] = high
            low_rows[place] = low

    def turned(freq, real, imag):
        tc = twiddle[freq : freq + 1, :INNER]
        ts = twiddle[freq : freq + 1, INNER:]
        keep(freq, real * tc + imag * ts, imag * tc - real * ts)

    keep(0, functools.reduce(jnp.add, sums, points[0]), jnp.zeros((rows, INNER), jnp.float32))
    for freq in range(1, half + 1):
        real, imag = points[0], None
        for j in range(1, half + 1):
            angle = 2 * math.pi * ((j * freq) % fold) / fold
            real = real + math.cos(angle) * sums[j - 1]
            term = -math.sin(angle) * differences[j - 1]
            imag = term if imag is None else imag + term
        turned(freq, real, imag)
        turned(fold - freq, real, -imag)
    result = dot_nt(high_table[...], high_rows[...])
    result += dot_nt(high_table[...], low_rows[...])
    result += dot_nt(low_table[...], high_rows[...])
    scale = row_scale(result)
    code = encode(result, scale)
    lane = lax.broadcasted_iota(jnp.int32, code.shape, 1)
    code = jnp.where(lane == code.shape[1] - 1, scale, code)
    devices, tall, wide = out.shape
    pieces = code.shape[1] // wide
    code = code.reshape(devices, tall // pieces, code.shape[1])
    code = [code[:, :, piece * wide : (piece + 1) * wide] for piece in range(pieces)]
    out[...] = jnp.concatenate(code, axis=1).astype(jnp.bfloat16)


def column_transform(blocks, length, devices):
    owners = len(blocks)
    rows, width = blocks[0].shape
    own_cols = length // owners
    fold = length // INNER
    kept = INNER // 2
    per_device = kept // devices
    angle = angles_host(np.arange(fold), np.arange(INNER), length)
    twiddle = np.concatenate([np.cos(angle), np.sin(angle)], axis=1).astype(np.float32)
    angle = angles_host(np.arange(kept), np.arange(INNER), INNER)
    table = np.stack(
        [
            np.concatenate([np.cos(angle), np.sin(angle)], axis=1),
            np.concatenate([-np.sin(angle), np.cos(angle)], axis=1),
        ]
    )
    table = table.reshape(2, devices, per_device, 2 * INNER).transpose(1, 0, 2, 3).reshape(INNER, 2 * INNER)
    high_table, low_table = split_host(table)
    pieces = max(16 // (2 * per_device), 1)
    lanes = ceil_to(fold * rows + 1, pieces * LANES)
    return pl.pallas_call(
        functools.partial(column_kernel, (owners, rows, own_cols, fold)),
        out_shape=jax.ShapeDtypeStruct((devices, pieces * 2 * per_device, lanes // pieces), jnp.bfloat16),
        scratch_shapes=[
            pltpu.VMEM((rows, length + 2 * LANES), jnp.float32),
            pltpu.VMEM((lanes, 2 * INNER), jnp.bfloat16),
            pltpu.VMEM((lanes, 2 * INNER), jnp.bfloat16),
        ],
        compiler_params=pltpu.CompilerParams(vmem_limit_bytes=48 * 2**20),
    )(*blocks, jnp.asarray(taper_host(length)[None, :]), jnp.asarray(twiddle), jnp.asarray(high_table), jnp.asarray(low_table))


def row_kernel(shape, arrived, weight, twiddle, high_table, low_table, out, blocks, spread, folded):
    length, fold, step, parts, packed, factor = shape
    devices, tall, wide = arrived.shape
    per_device = packed // 2
    pieces = tall // packed
    code = arrived[...].astype(jnp.float32)
    scale = code[:, tall - packed :, wide - 1 :]
    value = decode(code, jnp.concatenate([scale] * pieces, axis=1))
    for piece in range(pieces):
        blocks[:, :, piece * wide : (piece + 1) * wide] = value[:, piece * packed : (piece + 1) * packed]
    width = blocks.shape[2]
    slots = LANES // step
    lane = lax.broadcasted_iota(jnp.int32, (packed, LANES), 1) // step
    sign = jnp.where(lax.broadcasted_iota(jnp.int32, (packed, INNER), 0) < per_device, 1.0, -1.0)

    for column in range(width // LANES):
        for half in range(devices // slots):
            tiles = [
                blocks[half * slots + g, :, column * LANES : (column + 1) * LANES] for g in range(slots)
            ]
            bit = 1
            while bit < slots:
                upper = (lane & bit) != 0
                for g in range(slots):
                    if g & bit:
                        continue
                    a, b = tiles[g], tiles[g + bit]
                    tiles[g] = jnp.where(upper, pltpu.roll(b, bit * step, 1), a)
                    tiles[g + bit] = jnp.where(upper, b, pltpu.roll(a, LANES - bit * step, 1))
                bit *= 2
            for g in range(slots):
                q = column * slots + g
                if q < fold * parts:
                    spread[q, :, half * LANES : (half + 1) * LANES] = tiles[g]

    def quarter(value):
        return pltpu.roll(value, per_device, 0) * sign

    place = lax.broadcasted_iota(jnp.int32, (packed, INNER), 1)
    for freq in range(fold):
        halo = spread[freq * parts + fold]
        run = 4 * step
        extra = {}
        for owner, (target, shift) in enumerate(
            ((fold - 2, -1), (fold - 1, -1 - step), (0, 2 * step), (1, step))
        ):
            inside = place != owner * step if owner < 2 else place != INNER - run + owner * step
            only = jnp.where((place % run == owner * step) & inside, halo, 0.0)
            moved = pltpu.roll(only, shift % INNER, 1)
            extra[target] = extra[target] + moved if target in extra else moved
        for point in range(fold):
            value = spread[freq * parts + point]
            if point in extra:
                value = value + extra[point]
            folded[(point * fold + freq) * packed : (point * fold + freq + 1) * packed, :] = (
                value * weight[point : point + 1, :]
            )

    high, low = split(folded[...])
    result = dot(high, high_table[...]) + dot(low, high_table[...]) + dot(high, low_table[...])
    for freq in range(fold):
        points = []
        for point in range(fold):
            begin = (point * fold + freq) * packed
            rows = slice(begin, begin + packed)
            value = result[rows, :INNER] + quarter(result[rows, INNER:])
            if point:
                tc = twiddle[point : point + 1, :INNER]
                ts = twiddle[point : point + 1, INNER:]
                value = value * tc + quarter(value) * ts
            points.append(value)
        half = fold // 2
        sums = [points[j] + points[fold - j] for j in range(1, half + 1)]
        differences = [quarter(points[j] - points[fold - j]) for j in range(1, half + 1)]

        def keep(index, value):
            power = value * value
            power = (power + pltpu.roll(power, per_device, 0)) * factor
            for side in range(INNER // LANES):
                row = (freq * length + index * INNER) // LANES + side
                rows = pl.ds(row, per_device, stride=fold * length // LANES)
                out[rows, :] = power[:per_device, side * LANES : (side + 1) * LANES]

        keep(0, functools.reduce(jnp.add, sums, points[0]))
        for index in range(1, half + 1):
            even, odd = points[0], None
            for j in range(1, half + 1):
                angle = 2 * math.pi * ((j * index) % fold) / fold
                even = even + math.cos(angle) * sums[j - 1]
                term = math.sin(angle) * differences[j - 1]
                odd = term if odd is None else odd + term
            keep(index, even + odd)
            keep(fold - index, even - odd)


def row_transform(arrived, length, rows):
    devices, tall, wide = arrived.shape
    packed = INNER // devices
    fold = length // INNER
    step = length // fold // devices
    angle = angles_host(np.arange(fold), np.arange(INNER), length)
    twiddle = np.concatenate([np.cos(angle), np.sin(angle)], axis=1).astype(np.float32)
    angle = angles_host(np.arange(INNER), np.arange(INNER), INNER)
    high_table, low_table = split_host(np.concatenate([np.cos(angle), np.sin(angle)], axis=1))
    parts = rows // step
    weight = np.ascontiguousarray(taper_host(length).reshape(INNER, fold).T)
    shape = (length, fold, step, parts, packed, STRIDE / (length * length))
    return pl.pallas_call(
        functools.partial(row_kernel, shape),
        out_shape=jax.ShapeDtypeStruct((fold * packed // 2 * length // LANES, LANES), jnp.float32),
        scratch_shapes=[
            pltpu.VMEM((devices, packed, tall * wide // packed), jnp.float32),
            pltpu.VMEM((fold * parts, packed, INNER), jnp.float32),
            pltpu.VMEM((fold * fold * packed, INNER), jnp.float32),
        ],
        compiler_params=pltpu.CompilerParams(vmem_limit_bytes=48 * 2**20),
    )(arrived, jnp.asarray(weight), jnp.asarray(twiddle), jnp.asarray(high_table), jnp.asarray(low_table))


def local(field):
    owners = lax.axis_size("cols")
    devices = lax.axis_size("rows") * owners
    length = field.shape[1] // STRIDE * lax.axis_size("rows")
    fold = length // INNER
    cut = cut_filter(field, owners, fold)
    grouped = [cut[0]]
    for distance in range(1, owners):
        pairs = [(col, col ^ distance) for col in range(owners)]
        grouped.append(lax.ppermute(cut[distance], "cols", pairs))
    partial = column_transform(grouped, length, devices)
    arrived = lax.all_to_all(partial, ("rows", "cols"), split_axis=0, concat_axis=0, tiled=True)
    return row_transform(arrived, length, grouped[0].shape[0]).reshape(1, -1, length)


def solution(mesh):
    return jax.shard_map(
        local,
        mesh=mesh,
        in_specs=(P(None, "rows", "cols"),),
        out_specs=P(None, ("rows", "cols"), None),
        check_vma=False,
    )
```

```python
import functools
import math

import jax
import jax.numpy as jnp
import ml_dtypes
import numpy as np
from jax import lax
from jax.experimental import pallas as pl
from jax.experimental.pallas import tpu as pltpu
from jax.sharding import PartitionSpec as P

TAPS = 33
STRIDE = 8
REACH = TAPS // 2
GROUP_COLS = 1536
GROUP_OUTS = GROUP_COLS // STRIDE
LANES = 128
INNER = 256
COMPAND = 1023.0
LEVELS = 240
NONE_CODE = 2.0 ** -(LEVELS // 2)
ROW_MARGIN = 8
HALO_OUTS = 2


def ceil_to(value, step):
    return -(-value // step) * step


def split_host(table):
    high = table.astype(ml_dtypes.bfloat16)
    low = (table - high.astype(np.float64)).astype(ml_dtypes.bfloat16)
    return high, low


def taps_host():
    ids = np.arange(TAPS, dtype=np.float64)
    shaped = np.sinc((ids - REACH) / STRIDE) * (0.54 - 0.46 * np.cos(2 * np.pi * ids / (TAPS - 1)))
    return (shaped / shaped.sum()).astype(ml_dtypes.bfloat16)


def band(taps, tap_ids):
    table = jnp.zeros(tap_ids.shape, jnp.float32)
    for tap_id, tap in enumerate(taps):
        table = jnp.where(tap_ids == tap_id, tap, table)
    return table


def angles_host(left, right, length):
    reduced = (np.asarray(left)[:, None] * np.asarray(right)[None, :]) % length
    return 2 * np.pi * reduced / length


def taper_host(length):
    return (0.5 - 0.5 * np.cos(2 * np.pi * np.arange(length) / length)).astype(np.float32)


def split(value):
    high = value.astype(jnp.bfloat16)
    low = (value - high.astype(jnp.float32)).astype(jnp.bfloat16)
    return high, low


def row_scale(*arrays):
    peak = functools.reduce(jnp.maximum, [jnp.abs(array) for array in arrays])
    peak = jnp.max(peak, axis=-1, keepdims=True)
    return (peak * 1.01 + 1e-30).astype(jnp.bfloat16).astype(jnp.float32)


def encode(value, scale):
    level = jnp.log(1.0 + jnp.abs(value) * (COMPAND / scale)) * (LEVELS / math.log(1.001 * COMPAND))
    whole = jnp.floor(level)
    code = (1.0 + (level - whole)) * jnp.exp2(whole - LEVELS / 2)
    return jnp.where(value < 0, -code, code)


def decode(code, scale):
    size = jnp.abs(code)
    whole = jnp.floor(jnp.log2(size) + 0.0028)
    level = whole + (LEVELS / 2 - 1.0) + size * jnp.exp2(-whole)
    value = (jnp.exp(level * (math.log(1.001 * COMPAND) / LEVELS)) - 1.0) * (scale / COMPAND)
    return jnp.where(code < 0, -value, value)


def dot(left, right):
    return jnp.dot(left, right, preferred_element_type=jnp.float32)


def dot_nt(left, right):
    return lax.dot_general(left, right, (((1,), (1,)), ((), ())), preferred_element_type=jnp.float32)


def cut_kernel(shape, field, *refs):
    outs, refs = refs[: shape[-2]], refs[shape[-2] :]
    raw, arrived, band_rows, band_cols, total, cut, ordered, coded = refs
    taps, chunks, merged, groups, block_outs, fold, owners, own_rows = shape
    block_rows = raw.shape[1]

    def copy(chunk):
        rows = pl.ds(pl.multiple_of(chunk * block_rows, block_rows), block_rows)
        return pltpu.make_async_copy(field.at[0, rows, :], raw.at[chunk], arrived.at[chunk])

    for chunk in range(chunks):
        copy(chunk).start()
    total[...] = jnp.zeros_like(total)
    ids = lax.broadcasted_iota(jnp.int32, band_rows.shape, 1)
    ids = ids - STRIDE * (lax.broadcasted_iota(jnp.int32, band_rows.shape, 0) - ROW_MARGIN) + REACH
    band_rows[...] = band(taps, ids).astype(jnp.bfloat16)
    shape_8 = (8, band_cols.shape[1])
    ids = lax.broadcasted_iota(jnp.int32, shape_8, 0)
    ids = ids - STRIDE * (lax.broadcasted_iota(jnp.int32, shape_8, 1) - HALO_OUTS) + REACH
    initial = band(taps, ids)
    for pair in range(GROUP_COLS // 16):
        both = [pltpu.roll(initial, move, 1) if move else initial for move in (2 * pair, 2 * pair + 1)]
        band_cols[16 * pair : 16 * pair + 16, :] = jnp.concatenate(both, axis=0).astype(jnp.bfloat16)

    places = cut.shape[0]
    last = lax.broadcasted_iota(jnp.int32, (1, LANES), 1) == LANES - 1

    def finish(begin, count):
        rows = pl.ds(begin, count)
        middle = jnp.concatenate([total[1, rows, :], jnp.zeros((count, LANES), jnp.float32)], axis=1)
        middle = pltpu.roll(middle, 64, 1)
        joined = [
            total[0, rows, :LANES],
            total[0, rows, LANES:] + middle[:, :LANES],
            middle[:, LANES : 2 * LANES],
            middle[:, 2 * LANES :] + total[2, rows, :LANES],
            total[2, rows, LANES:],
        ]
        scale = row_scale(*joined)
        for place in range(places):
            code = encode(joined[place], scale)
            cut[place, rows, :] = jnp.where(last, scale, code) if place == places - 1 else code

    def step(turn, carry):
        for part in range(merged):
            copy(turn * merged + part).wait()
        stacked = [
            raw[turn * merged + part, :, group * GROUP_COLS : (group + 1) * GROUP_COLS]
            for group in range(groups)
            for part in range(merged)
        ]
        high, low = split(dot(jnp.concatenate(stacked, axis=0), band_cols[...]))
        rows = pl.ds(pl.multiple_of(turn * merged * block_outs, 8), band_rows.shape[0])
        for group in range(groups):
            own = slice(group * merged * block_rows, (group + 1) * merged * block_rows)
            total[group, rows, :] += dot(band_rows[...], high[own]) + dot(band_rows[...], low[own])
        return carry

    lax.fori_loop(0, chunks // merged, step, 0)
    finish(0, owners * own_rows + 2 * ROW_MARGIN)
    used = own_rows + 8
    sub = lax.broadcasted_iota(jnp.int32, (8, LANES), 0)
    if ordered.shape[0] > used:
        ordered[used:, :] = jnp.full((ordered.shape[0] - used, ordered.shape[1]), NONE_CODE, jnp.float32)
    for owner in range(owners):
        count = own_rows // fold
        begin_at = ROW_MARGIN + owner * own_rows
        edge = (ROW_MARGIN - 2, ROW_MARGIN - 1, ROW_MARGIN + owners * own_rows, ROW_MARGIN + owners * own_rows + 1)[owner]
        for place in range(places):
            lanes = slice(place * LANES, (place + 1) * LANES)
            for part in range(fold):
                picked = cut[pl.ds(place, 1), pl.ds(begin_at + part, count, stride=fold), :]
                ordered[part * count : (part + 1) * count, lanes] = picked[0]
            row = cut[place, edge : edge + 1, :]
            ordered[own_rows:used, lanes] = jnp.where(sub == 0, row, NONE_CODE)
        coded[owner] = ordered[...].astype(jnp.bfloat16)
    own_col = lax.axis_index("cols")
    for distance in range(owners):
        outs[distance][...] = coded[own_col ^ distance]


def cut_filter(field, owners, fold):
    _, raw_rows, raw_cols = field.shape
    block_rows = next(size for size in (256, 192, 128, 64) if raw_rows % size == 0)
    chunks = raw_rows // block_rows
    merged = 3 if chunks % 3 == 0 else 1
    groups = raw_cols // GROUP_COLS
    block_outs = block_rows // STRIDE
    own_rows = raw_rows // STRIDE // owners
    span = merged * block_outs + 2 * ROW_MARGIN
    count_rows = raw_rows // STRIDE + 2 * ROW_MARGIN
    out_cols = ceil_to(raw_cols // STRIDE + 2 * HALO_OUTS, LANES)
    taps = [float(tap) for tap in taps_host()]
    shape = (taps, chunks, merged, groups, block_outs, fold, owners, own_rows)
    out_rows = ceil_to(own_rows + 8, 16)
    return pl.pallas_call(
        functools.partial(cut_kernel, shape),
        out_shape=[jax.ShapeDtypeStruct((out_rows, out_cols), jnp.bfloat16)] * owners,
        in_specs=[pl.BlockSpec(memory_space=pl.ANY)],
        out_specs=[pl.BlockSpec(memory_space=pltpu.VMEM)] * owners,
        scratch_shapes=[
            pltpu.VMEM((chunks, block_rows, raw_cols), jnp.bfloat16),
            pltpu.SemaphoreType.DMA((chunks,)),
            pltpu.VMEM((span, merged * block_rows), jnp.bfloat16),
            pltpu.VMEM((GROUP_COLS, 2 * LANES), jnp.bfloat16),
            pltpu.VMEM((groups, count_rows, 2 * LANES), jnp.float32),
            pltpu.VMEM((out_cols // LANES, count_rows, LANES), jnp.float32),
            pltpu.VMEM((out_rows, out_cols), jnp.float32),
            pltpu.VMEM((owners, out_rows, out_cols), jnp.bfloat16),
        ],
        compiler_params=pltpu.CompilerParams(vmem_limit_bytes=40 * 2**20),
    )(field)


def column_kernel(shape, *refs):
    owners, rows, own_cols, fold = shape
    blocks, refs = refs[:owners], refs[owners:]
    weight, twiddle, high_table, low_table, out, joined, high_rows, low_rows = refs
    own_col = lax.axis_index("cols")
    joined[...] = jnp.zeros_like(joined)
    width = blocks[0].shape[1]
    inside = lax.broadcasted_iota(jnp.int32, (rows, width), 1) < own_cols + 2 * HALO_OUTS
    for distance in range(owners):
        first = LANES + own_cols * (own_col ^ distance) - HALO_OUTS
        code = blocks[distance][...].astype(jnp.float32)
        value = decode(code, code[:, width - 1 :])
        value = jnp.where(inside, value, 0.0)
        block = jnp.concatenate([value, jnp.zeros((rows, LANES), jnp.float32)], axis=1)
        base = pl.multiple_of(first // LANES * LANES, LANES)
        joined[:, pl.ds(base, width + LANES)] += pltpu.roll(block, first % LANES, 1)
    points = [
        joined[:, LANES + INNER * i : LANES + INNER * (i + 1)] * weight[:, INNER * i : INNER * (i + 1)]
        for i in range(fold)
    ]
    half = fold // 2
    sums = [points[j] + points[fold - j] for j in range(1, half + 1)]
    differences = [points[j] - points[fold - j] for j in range(1, half + 1)]
    used = rows * fold
    if high_rows.shape[0] > used:
        rest = jnp.zeros((high_rows.shape[0] - used, 2 * INNER), jnp.bfloat16)
        high_rows[used:, :] = rest
        low_rows[used:, :] = rest

    def keep(freq, real, imag):
        for side, value in enumerate((real, imag)):
            high, low = split(value)
            place = (slice(freq * rows, (freq + 1) * rows), slice(side * INNER, (side + 1) * INNER))
            high_rows[place] = high
            low_rows[place] = low

    def turned(freq, real, imag):
        tc = twiddle[freq : freq + 1, :INNER]
        ts = twiddle[freq : freq + 1, INNER:]
        keep(freq, real * tc + imag * ts, imag * tc - real * ts)

    keep(0, functools.reduce(jnp.add, sums, points[0]), jnp.zeros((rows, INNER), jnp.float32))
    for freq in range(1, half + 1):
        real, imag = points[0], None
        for j in range(1, half + 1):
            angle = 2 * math.pi * ((j * freq) % fold) / fold
            real = real + math.cos(angle) * sums[j - 1]
            term = -math.sin(angle) * differences[j - 1]
            imag = term if imag is None else imag + term
        turned(freq, real, imag)
        turned(fold - freq, real, -imag)
    result = dot_nt(high_table[...], high_rows[...])
    result += dot_nt(high_table[...], low_rows[...])
    result += dot_nt(low_table[...], high_rows[...])
    scale = row_scale(result)
    code = encode(result, scale)
    lane = lax.broadcasted_iota(jnp.int32, code.shape, 1)
    code = jnp.where(lane == code.shape[1] - 1, scale, code)
    devices, tall, wide = out.shape
    pieces = code.shape[1] // wide
    code = code.reshape(devices, tall // pieces, code.shape[1])
    code = [code[:, :, piece * wide : (piece + 1) * wide] for piece in range(pieces)]
    out[...] = jnp.concatenate(code, axis=1).astype(jnp.bfloat16)


def column_transform(blocks, length, devices):
    owners = len(blocks)
    rows, width = blocks[0].shape
    own_cols = length // owners
    fold = length // INNER
    kept = INNER // 2
    per_device = kept // devices
    angle = angles_host(np.arange(fold), np.arange(INNER), length)
    twiddle = np.concatenate([np.cos(angle), np.sin(angle)], axis=1).astype(np.float32)
    angle = angles_host(np.arange(kept), np.arange(INNER), INNER)
    table = np.stack(
        [
            np.concatenate([np.cos(angle), np.sin(angle)], axis=1),
            np.concatenate([-np.sin(angle), np.cos(angle)], axis=1),
        ]
    )
    table = table.reshape(2, devices, per_device, 2 * INNER).transpose(1, 0, 2, 3).reshape(INNER, 2 * INNER)
    high_table, low_table = split_host(table)
    pieces = max(16 // (2 * per_device), 1)
    lanes = ceil_to(fold * rows + 1, pieces * LANES)
    return pl.pallas_call(
        functools.partial(column_kernel, (owners, rows, own_cols, fold)),
        out_shape=jax.ShapeDtypeStruct((devices, pieces * 2 * per_device, lanes // pieces), jnp.bfloat16),
        scratch_shapes=[
            pltpu.VMEM((rows, length + 2 * LANES), jnp.float32),
            pltpu.VMEM((lanes, 2 * INNER), jnp.bfloat16),
            pltpu.VMEM((lanes, 2 * INNER), jnp.bfloat16),
        ],
        compiler_params=pltpu.CompilerParams(vmem_limit_bytes=48 * 2**20),
    )(*blocks, jnp.asarray(taper_host(length)[None, :]), jnp.asarray(twiddle), jnp.asarray(high_table), jnp.asarray(low_table))


def row_kernel(shape, arrived, weight, twiddle, high_table, low_table, out, blocks, spread, folded):
    length, fold, step, parts, packed, factor = shape
    devices, tall, wide = arrived.shape
    per_device = packed // 2
    pieces = tall // packed
    code = arrived[...].astype(jnp.float32)
    scale = code[:, tall - packed :, wide - 1 :]
    value = decode(code, jnp.concatenate([scale] * pieces, axis=1))
    for piece in range(pieces):
        blocks[:, :, piece * wide : (piece + 1) * wide] = value[:, piece * packed : (piece + 1) * packed]
    width = blocks.shape[2]
    slots = LANES // step
    lane = lax.broadcasted_iota(jnp.int32, (packed, LANES), 1) // step
    sign = jnp.where(lax.broadcasted_iota(jnp.int32, (packed, INNER), 0) < per_device, 1.0, -1.0)

    for column in range(width // LANES):
        for half in range(devices // slots):
            tiles = [
                blocks[half * slots + g, :, column * LANES : (column + 1) * LANES] for g in range(slots)
            ]
            bit = 1
            while bit < slots:
                upper = (lane & bit) != 0
                for g in range(slots):
                    if g & bit:
                        continue
                    a, b = tiles[g], tiles[g + bit]
                    tiles[g] = jnp.where(upper, pltpu.roll(b, bit * step, 1), a)
                    tiles[g + bit] = jnp.where(upper, b, pltpu.roll(a, LANES - bit * step, 1))
                bit *= 2
            for g in range(slots):
                q = column * slots + g
                if q < fold * parts:
                    spread[q, :, half * LANES : (half + 1) * LANES] = tiles[g]

    def quarter(value):
        return pltpu.roll(value, per_device, 0) * sign

    place = lax.broadcasted_iota(jnp.int32, (packed, INNER), 1)
    for freq in range(fold):
        halo = spread[freq * parts + fold]
        run = 4 * step
        extra = {}
        for owner, (target, shift) in enumerate(
            ((fold - 2, -1), (fold - 1, -1 - step), (0, 2 * step), (1, step))
        ):
            inside = place != owner * step if owner < 2 else place != INNER - run + owner * step
            only = jnp.where((place % run == owner * step) & inside, halo, 0.0)
            moved = pltpu.roll(only, shift % INNER, 1)
            extra[target] = extra[target] + moved if target in extra else moved
        for point in range(fold):
            value = spread[freq * parts + point]
            if point in extra:
                value = value + extra[point]
            folded[(point * fold + freq) * packed : (point * fold + freq + 1) * packed, :] = (
                value * weight[point : point + 1, :]
            )

    high, low = split(folded[...])
    result = dot(high, high_table[...]) + dot(low, high_table[...]) + dot(high, low_table[...])
    for freq in range(fold):
        points = []
        for point in range(fold):
            begin = (point * fold + freq) * packed
            rows = slice(begin, begin + packed)
            value = result[rows, :INNER] + quarter(result[rows, INNER:])
            if point:
                tc = twiddle[point : point + 1, :INNER]
                ts = twiddle[point : point + 1, INNER:]
                value = value * tc + quarter(value) * ts
            points.append(value)
        half = fold // 2
        sums = [points[j] + points[fold - j] for j in range(1, half + 1)]
        differences = [quarter(points[j] - points[fold - j]) for j in range(1, half + 1)]

        def keep(index, value):
            power = value * value
            power = (power + pltpu.roll(power, per_device, 0)) * factor
            for side in range(INNER // LANES):
                row = (freq * length + index * INNER) // LANES + side
                rows = pl.ds(row, per_device, stride=fold * length // LANES)
                out[rows, :] = power[:per_device, side * LANES : (side + 1) * LANES]

        keep(0, functools.reduce(jnp.add, sums, points[0]))
        for index in range(1, half + 1):
            even, odd = points[0], None
            for j in range(1, half + 1):
                angle = 2 * math.pi * ((j * index) % fold) / fold
                even = even + math.cos(angle) * sums[j - 1]
                term = math.sin(angle) * differences[j - 1]
                odd = term if odd is None else odd + term
            keep(index, even + odd)
            keep(fold - index, even - odd)


def row_transform(arrived, length, rows):
    devices, tall, wide = arrived.shape
    packed = INNER // devices
    fold = length // INNER
    step = length // fold // devices
    angle = angles_host(np.arange(fold), np.arange(INNER), length)
    twiddle = np.concatenate([np.cos(angle), np.sin(angle)], axis=1).astype(np.float32)
    angle = angles_host(np.arange(INNER), np.arange(INNER), INNER)
    high_table, low_table = split_host(np.concatenate([np.cos(angle), np.sin(angle)], axis=1))
    parts = rows // step
    weight = np.ascontiguousarray(taper_host(length).reshape(INNER, fold).T)
    shape = (length, fold, step, parts, packed, STRIDE / (length * length))
    return pl.pallas_call(
        functools.partial(row_kernel, shape),
        out_shape=jax.ShapeDtypeStruct((fold * packed // 2 * length // LANES, LANES), jnp.float32),
        scratch_shapes=[
            pltpu.VMEM((devices, packed, tall * wide // packed), jnp.float32),
            pltpu.VMEM((fold * parts, packed, INNER), jnp.float32),
            pltpu.VMEM((fold * fold * packed, INNER), jnp.float32),
        ],
        compiler_params=pltpu.CompilerParams(vmem_limit_bytes=48 * 2**20),
    )(arrived, jnp.asarray(weight), jnp.asarray(twiddle), jnp.asarray(high_table), jnp.asarray(low_table))


def local(field):
    owners = lax.axis_size("cols")
    devices = lax.axis_size("rows") * owners
    length = field.shape[1] // STRIDE * lax.axis_size("rows")
    fold = length // INNER
    cut = cut_filter(field, owners, fold)
    grouped = [cut[0]]
    for distance in range(1, owners):
        pairs = [(col, col ^ distance) for col in range(owners)]
        grouped.append(lax.ppermute(cut[distance], "cols", pairs))
    partial = column_transform(grouped, length, devices)
    arrived = lax.all_to_all(partial, ("rows", "cols"), split_axis=0, concat_axis=0, tiled=True)
    return row_transform(arrived, length, grouped[0].shape[0]).reshape(1, -1, length)


def solution(mesh):
    return jax.shard_map(
        local,
        mesh=mesh,
        in_specs=(P(None, "rows", "cols"),),
        out_specs=P(None, ("rows", "cols"), None),
        check_vma=False,
    )
```

```python
import functools
import math

import jax
import jax.numpy as jnp
import ml_dtypes
import numpy as np
from jax import lax
from jax.experimental import pallas as pl
from jax.experimental.pallas import tpu as pltpu
from jax.sharding import PartitionSpec as P

TAPS = 33
STRIDE = 8
REACH = TAPS // 2
GROUP_COLS = 1536
GROUP_OUTS = GROUP_COLS // STRIDE
LANES = 128
INNER = 256
COMPAND = 1023.0
LEVELS = 240
NONE_CODE = 2.0 ** -(LEVELS // 2)
ROW_MARGIN = 8
HALO_OUTS = 2


def ceil_to(value, step):
    return -(-value // step) * step


def split_host(table):
    high = table.astype(ml_dtypes.bfloat16)
    low = (table - high.astype(np.float64)).astype(ml_dtypes.bfloat16)
    return high, low


def taps_host():
    ids = np.arange(TAPS, dtype=np.float64)
    shaped = np.sinc((ids - REACH) / STRIDE) * (0.54 - 0.46 * np.cos(2 * np.pi * ids / (TAPS - 1)))
    return (shaped / shaped.sum()).astype(ml_dtypes.bfloat16)


def band(taps, tap_ids):
    table = jnp.zeros(tap_ids.shape, jnp.float32)
    for tap_id, tap in enumerate(taps):
        table = jnp.where(tap_ids == tap_id, tap, table)
    return table


def angles_host(left, right, length):
    reduced = (np.asarray(left)[:, None] * np.asarray(right)[None, :]) % length
    return 2 * np.pi * reduced / length


def taper_host(length):
    return (0.5 - 0.5 * np.cos(2 * np.pi * np.arange(length) / length)).astype(np.float32)


def split(value):
    high = value.astype(jnp.bfloat16)
    low = (value - high.astype(jnp.float32)).astype(jnp.bfloat16)
    return high, low


def row_scale(*arrays):
    peak = functools.reduce(jnp.maximum, [jnp.abs(array) for array in arrays])
    peak = jnp.max(peak, axis=-1, keepdims=True)
    return (peak * 1.01 + 1e-30).astype(jnp.bfloat16).astype(jnp.float32)


def encode(value, scale):
    level = jnp.log(1.0 + jnp.abs(value) * (COMPAND / scale)) * (LEVELS / math.log(1.001 * COMPAND))
    whole = jnp.floor(level)
    code = (1.0 + (level - whole)) * jnp.exp2(whole - LEVELS / 2)
    return jnp.where(value < 0, -code, code)


def decode(code, scale):
    size = jnp.abs(code)
    whole = jnp.floor(jnp.log2(size) + 0.0028)
    level = whole + (LEVELS / 2 - 1.0) + size * jnp.exp2(-whole)
    value = (jnp.exp(level * (math.log(1.001 * COMPAND) / LEVELS)) - 1.0) * (scale / COMPAND)
    return jnp.where(code < 0, -value, value)


def dot(left, right):
    return jnp.dot(left, right, preferred_element_type=jnp.float32)


def dot_nt(left, right):
    return lax.dot_general(left, right, (((1,), (1,)), ((), ())), preferred_element_type=jnp.float32)


def cut_kernel(shape, field, *refs):
    outs, refs = refs[: shape[-2]], refs[shape[-2] :]
    raw, arrived, band_rows, band_cols, total, cut, ordered, coded = refs
    taps, chunks, merged, groups, block_outs, fold, owners, own_rows = shape
    block_rows = raw.shape[1]

    def copy(chunk):
        rows = pl.ds(pl.multiple_of(chunk * block_rows, block_rows), block_rows)
        return pltpu.make_async_copy(field.at[0, rows, :], raw.at[chunk], arrived.at[chunk])

    for chunk in range(chunks):
        copy(chunk).start()
    total[...] = jnp.zeros_like(total)
    ids = lax.broadcasted_iota(jnp.int32, band_rows.shape, 1)
    ids = ids - STRIDE * (lax.broadcasted_iota(jnp.int32, band_rows.shape, 0) - ROW_MARGIN) + REACH
    band_rows[...] = band(taps, ids).astype(jnp.bfloat16)
    shape_8 = (8, band_cols.shape[1])
    ids = lax.broadcasted_iota(jnp.int32, shape_8, 0)
    ids = ids - STRIDE * (lax.broadcasted_iota(jnp.int32, shape_8, 1) - HALO_OUTS) + REACH
    initial = band(taps, ids)
    for pair in range(GROUP_COLS // 16):
        both = [pltpu.roll(initial, move, 1) if move else initial for move in (2 * pair, 2 * pair + 1)]
        band_cols[16 * pair : 16 * pair + 16, :] = jnp.concatenate(both, axis=0).astype(jnp.bfloat16)

    places = cut.shape[0]
    last = lax.broadcasted_iota(jnp.int32, (1, LANES), 1) == LANES - 1

    def finish(begin, count):
        rows = pl.ds(begin, count)
        middle = jnp.concatenate([total[1, rows, :], jnp.zeros((count, LANES), jnp.float32)], axis=1)
        middle = pltpu.roll(middle, 64, 1)
        joined = [
            total[0, rows, :LANES],
            total[0, rows, LANES:] + middle[:, :LANES],
            middle[:, LANES : 2 * LANES],
            middle[:, 2 * LANES :] + total[2, rows, :LANES],
            total[2, rows, LANES:],
        ]
        scale = row_scale(*joined)
        for place in range(places):
            code = encode(joined[place], scale)
            cut[place, rows, :] = jnp.where(last, scale, code) if place == places - 1 else code

    def step(turn, carry):
        for part in range(merged):
            copy(turn * merged + part).wait()
        stacked = [
            raw[turn * merged + part, :, group * GROUP_COLS : (group + 1) * GROUP_COLS]
            for group in range(groups)
            for part in range(merged)
        ]
        high, low = split(dot(jnp.concatenate(stacked, axis=0), band_cols[...]))
        rows = pl.ds(pl.multiple_of(turn * merged * block_outs, 8), band_rows.shape[0])
        for group in range(groups):
            own = slice(group * merged * block_rows, (group + 1) * merged * block_rows)
            total[group, rows, :] += dot(band_rows[...], high[own]) + dot(band_rows[...], low[own])
        return carry

    lax.fori_loop(0, chunks // merged, step, 0)
    finish(0, owners * own_rows + 2 * ROW_MARGIN)
    used = own_rows + 8
    sub = lax.broadcasted_iota(jnp.int32, (8, LANES), 0)
    if ordered.shape[0] > used:
        ordered[used:, :] = jnp.full((ordered.shape[0] - used, ordered.shape[1]), NONE_CODE, jnp.float32)
    for owner in range(owners):
        count = own_rows // fold
        begin_at = ROW_MARGIN + owner * own_rows
        edge = (ROW_MARGIN - 2, ROW_MARGIN - 1, ROW_MARGIN + owners * own_rows, ROW_MARGIN + owners * own_rows + 1)[owner]
        for place in range(places):
            lanes = slice(place * LANES, (place + 1) * LANES)
            for part in range(fold):
                picked = cut[pl.ds(place, 1), pl.ds(begin_at + part, count, stride=fold), :]
                ordered[part * count : (part + 1) * count, lanes] = picked[0]
            row = cut[place, edge : edge + 1, :]
            ordered[own_rows:used, lanes] = jnp.where(sub == 0, row, NONE_CODE)
        coded[owner] = ordered[...].astype(jnp.bfloat16)
    own_col = lax.axis_index("cols")
    for distance in range(owners):
        outs[distance][...] = coded[own_col ^ distance]


def cut_filter(field, owners, fold):
    _, raw_rows, raw_cols = field.shape
    block_rows = next(size for size in (256, 192, 128, 64) if raw_rows % size == 0)
    chunks = raw_rows // block_rows
    merged = 1
    groups = raw_cols // GROUP_COLS
    block_outs = block_rows // STRIDE
    own_rows = raw_rows // STRIDE // owners
    span = merged * block_outs + 2 * ROW_MARGIN
    count_rows = raw_rows // STRIDE + 2 * ROW_MARGIN
    out_cols = ceil_to(raw_cols // STRIDE + 2 * HALO_OUTS, LANES)
    taps = [float(tap) for tap in taps_host()]
    shape = (taps, chunks, merged, groups, block_outs, fold, owners, own_rows)
    out_rows = ceil_to(own_rows + 8, 16)
    return pl.pallas_call(
        functools.partial(cut_kernel, shape),
        out_shape=[jax.ShapeDtypeStruct((out_rows, out_cols), jnp.bfloat16)] * owners,
        in_specs=[pl.BlockSpec(memory_space=pl.ANY)],
        out_specs=[pl.BlockSpec(memory_space=pltpu.VMEM)] * owners,
        scratch_shapes=[
            pltpu.VMEM((chunks, block_rows, raw_cols), jnp.bfloat16),
            pltpu.SemaphoreType.DMA((chunks,)),
            pltpu.VMEM((span, merged * block_rows), jnp.bfloat16),
            pltpu.VMEM((GROUP_COLS, 2 * LANES), jnp.bfloat16),
            pltpu.VMEM((groups, count_rows, 2 * LANES), jnp.float32),
            pltpu.VMEM((out_cols // LANES, count_rows, LANES), jnp.float32),
            pltpu.VMEM((out_rows, out_cols), jnp.float32),
            pltpu.VMEM((owners, out_rows, out_cols), jnp.bfloat16),
        ],
        compiler_params=pltpu.CompilerParams(vmem_limit_bytes=40 * 2**20),
    )(field)


def column_kernel(shape, *refs):
    owners, rows, own_cols, fold = shape
    blocks, refs = refs[:owners], refs[owners:]
    weight, twiddle, high_table, low_table, out, joined, high_rows, low_rows = refs
    own_col = lax.axis_index("cols")
    joined[...] = jnp.zeros_like(joined)
    width = blocks[0].shape[1]
    inside = lax.broadcasted_iota(jnp.int32, (rows, width), 1) < own_cols + 2 * HALO_OUTS
    for distance in range(owners):
        first = LANES + own_cols * (own_col ^ distance) - HALO_OUTS
        code = blocks[distance][...].astype(jnp.float32)
        value = decode(code, code[:, width - 1 :])
        value = jnp.where(inside, value, 0.0)
        block = jnp.concatenate([value, jnp.zeros((rows, LANES), jnp.float32)], axis=1)
        base = pl.multiple_of(first // LANES * LANES, LANES)
        joined[:, pl.ds(base, width + LANES)] += pltpu.roll(block, first % LANES, 1)
    points = [
        joined[:, LANES + INNER * i : LANES + INNER * (i + 1)] * weight[:, INNER * i : INNER * (i + 1)]
        for i in range(fold)
    ]
    half = fold // 2
    sums = [points[j] + points[fold - j] for j in range(1, half + 1)]
    differences = [points[j] - points[fold - j] for j in range(1, half + 1)]
    used = rows * fold
    if high_rows.shape[0] > used:
        rest = jnp.zeros((high_rows.shape[0] - used, 2 * INNER), jnp.bfloat16)
        high_rows[used:, :] = rest
        low_rows[used:, :] = rest

    def keep(freq, real, imag):
        for side, value in enumerate((real, imag)):
            high, low = split(value)
            place = (slice(freq * rows, (freq + 1) * rows), slice(side * INNER, (side + 1) * INNER))
            high_rows[place] = high
            low_rows[place] = low

    def turned(freq, real, imag):
        tc = twiddle[freq : freq + 1, :INNER]
        ts = twiddle[freq : freq + 1, INNER:]
        keep(freq, real * tc + imag * ts, imag * tc - real * ts)

    keep(0, functools.reduce(jnp.add, sums, points[0]), jnp.zeros((rows, INNER), jnp.float32))
    for freq in range(1, half + 1):
        real, imag = points[0], None
        for j in range(1, half + 1):
            angle = 2 * math.pi * ((j * freq) % fold) / fold
            real = real + math.cos(angle) * sums[j - 1]
            term = -math.sin(angle) * differences[j - 1]
            imag = term if imag is None else imag + term
        turned(freq, real, imag)
        turned(fold - freq, real, -imag)
    result = dot_nt(high_table[...], high_rows[...])
    result += dot_nt(high_table[...], low_rows[...])
    result += dot_nt(low_table[...], high_rows[...])
    scale = row_scale(result)
    code = encode(result, scale)
    lane = lax.broadcasted_iota(jnp.int32, code.shape, 1)
    code = jnp.where(lane == code.shape[1] - 1, scale, code)
    devices, tall, wide = out.shape
    pieces = code.shape[1] // wide
    code = code.reshape(devices, tall // pieces, code.shape[1])
    code = [code[:, :, piece * wide : (piece + 1) * wide] for piece in range(pieces)]
    out[...] = jnp.concatenate(code, axis=1).astype(jnp.bfloat16)


def column_transform(blocks, length, devices):
    owners = len(blocks)
    rows, width = blocks[0].shape
    own_cols = length // owners
    fold = length // INNER
    kept = INNER // 2
    per_device = kept // devices
    angle = angles_host(np.arange(fold), np.arange(INNER), length)
    twiddle = np.concatenate([np.cos(angle), np.sin(angle)], axis=1).astype(np.float32)
    angle = angles_host(np.arange(kept), np.arange(INNER), INNER)
    table = np.stack(
        [
            np.concatenate([np.cos(angle), np.sin(angle)], axis=1),
            np.concatenate([-np.sin(angle), np.cos(angle)], axis=1),
        ]
    )
    table = table.reshape(2, devices, per_device, 2 * INNER).transpose(1, 0, 2, 3).reshape(INNER, 2 * INNER)
    high_table, low_table = split_host(table)
    pieces = max(16 // (2 * per_device), 1)
    lanes = ceil_to(fold * rows + 1, pieces * LANES)
    return pl.pallas_call(
        functools.partial(column_kernel, (owners, rows, own_cols, fold)),
        out_shape=jax.ShapeDtypeStruct((devices, pieces * 2 * per_device, lanes // pieces), jnp.bfloat16),
        scratch_shapes=[
            pltpu.VMEM((rows, length + 2 * LANES), jnp.float32),
            pltpu.VMEM((lanes, 2 * INNER), jnp.bfloat16),
            pltpu.VMEM((lanes, 2 * INNER), jnp.bfloat16),
        ],
        compiler_params=pltpu.CompilerParams(vmem_limit_bytes=48 * 2**20),
    )(*blocks, jnp.asarray(taper_host(length)[None, :]), jnp.asarray(twiddle), jnp.asarray(high_table), jnp.asarray(low_table))


def row_kernel(shape, arrived, weight, twiddle, high_table, low_table, out, blocks, spread, folded):
    length, fold, step, parts, packed, factor = shape
    devices, tall, wide = arrived.shape
    per_device = packed // 2
    pieces = tall // packed
    code = arrived[...].astype(jnp.float32)
    scale = code[:, tall - packed :, wide - 1 :]
    value = decode(code, jnp.concatenate([scale] * pieces, axis=1))
    for piece in range(pieces):
        blocks[:, :, piece * wide : (piece + 1) * wide] = value[:, piece * packed : (piece + 1) * packed]
    width = blocks.shape[2]
    slots = LANES // step
    lane = lax.broadcasted_iota(jnp.int32, (packed, LANES), 1) // step
    sign = jnp.where(lax.broadcasted_iota(jnp.int32, (packed, INNER), 0) < per_device, 1.0, -1.0)

    for column in range(width // LANES):
        for half in range(devices // slots):
            tiles = [
                blocks[half * slots + g, :, column * LANES : (column + 1) * LANES] for g in range(slots)
            ]
            bit = 1
            while bit < slots:
                upper = (lane & bit) != 0
                for g in range(slots):
                    if g & bit:
                        continue
                    a, b = tiles[g], tiles[g + bit]
                    tiles[g] = jnp.where(upper, pltpu.roll(b, bit * step, 1), a)
                    tiles[g + bit] = jnp.where(upper, b, pltpu.roll(a, LANES - bit * step, 1))
                bit *= 2
            for g in range(slots):
                q = column * slots + g
                if q < fold * parts:
                    spread[q, :, half * LANES : (half + 1) * LANES] = tiles[g]

    def quarter(value):
        return pltpu.roll(value, per_device, 0) * sign

    place = lax.broadcasted_iota(jnp.int32, (packed, INNER), 1)
    for freq in range(fold):
        halo = spread[freq * parts + fold]
        run = 4 * step
        extra = {}
        for owner, (target, shift) in enumerate(
            ((fold - 2, -1), (fold - 1, -1 - step), (0, 2 * step), (1, step))
        ):
            inside = place != owner * step if owner < 2 else place != INNER - run + owner * step
            only = jnp.where((place % run == owner * step) & inside, halo, 0.0)
            moved = pltpu.roll(only, shift % INNER, 1)
            extra[target] = extra[target] + moved if target in extra else moved
        for point in range(fold):
            value = spread[freq * parts + point]
            if point in extra:
                value = value + extra[point]
            folded[(point * fold + freq) * packed : (point * fold + freq + 1) * packed, :] = (
                value * weight[point : point + 1, :]
            )

    high, low = split(folded[...])
    result = dot(high, high_table[...]) + dot(low, high_table[...]) + dot(high, low_table[...])
    for freq in range(fold):
        points = []
        for point in range(fold):
            begin = (point * fold + freq) * packed
            rows = slice(begin, begin + packed)
            value = result[rows, :INNER] + quarter(result[rows, INNER:])
            if point:
                tc = twiddle[point : point + 1, :INNER]
                ts = twiddle[point : point + 1, INNER:]
                value = value * tc + quarter(value) * ts
            points.append(value)
        half = fold // 2
        sums = [points[j] + points[fold - j] for j in range(1, half + 1)]
        differences = [quarter(points[j] - points[fold - j]) for j in range(1, half + 1)]

        def keep(index, value):
            power = value * value
            power = (power + pltpu.roll(power, per_device, 0)) * factor
            for side in range(INNER // LANES):
                row = (freq * length + index * INNER) // LANES + side
                rows = pl.ds(row, per_device, stride=fold * length // LANES)
                out[rows, :] = power[:per_device, side * LANES : (side + 1) * LANES]

        keep(0, functools.reduce(jnp.add, sums, points[0]))
        for index in range(1, half + 1):
            even, odd = points[0], None
            for j in range(1, half + 1):
                angle = 2 * math.pi * ((j * index) % fold) / fold
                even = even + math.cos(angle) * sums[j - 1]
                term = math.sin(angle) * differences[j - 1]
                odd = term if odd is None else odd + term
            keep(index, even + odd)
            keep(fold - index, even - odd)


def row_transform(arrived, length, rows):
    devices, tall, wide = arrived.shape
    packed = INNER // devices
    fold = length // INNER
    step = length // fold // devices
    angle = angles_host(np.arange(fold), np.arange(INNER), length)
    twiddle = np.concatenate([np.cos(angle), np.sin(angle)], axis=1).astype(np.float32)
    angle = angles_host(np.arange(INNER), np.arange(INNER), INNER)
    high_table, low_table = split_host(np.concatenate([np.cos(angle), np.sin(angle)], axis=1))
    parts = rows // step
    weight = np.ascontiguousarray(taper_host(length).reshape(INNER, fold).T)
    shape = (length, fold, step, parts, packed, STRIDE / (length * length))
    return pl.pallas_call(
        functools.partial(row_kernel, shape),
        out_shape=jax.ShapeDtypeStruct((fold * packed // 2 * length // LANES, LANES), jnp.float32),
        scratch_shapes=[
            pltpu.VMEM((devices, packed, tall * wide // packed), jnp.float32),
            pltpu.VMEM((fold * parts, packed, INNER), jnp.float32),
            pltpu.VMEM((fold * fold * packed, INNER), jnp.float32),
        ],
        compiler_params=pltpu.CompilerParams(vmem_limit_bytes=48 * 2**20),
    )(arrived, jnp.asarray(weight), jnp.asarray(twiddle), jnp.asarray(high_table), jnp.asarray(low_table))


def local(field):
    owners = lax.axis_size("cols")
    devices = lax.axis_size("rows") * owners
    length = field.shape[1] // STRIDE * lax.axis_size("rows")
    fold = length // INNER
    cut = cut_filter(field, owners, fold)
    grouped = [cut[0]]
    for distance in range(1, owners):
        pairs = [(col, col ^ distance) for col in range(owners)]
        grouped.append(lax.ppermute(cut[distance], "cols", pairs))
    partial = column_transform(grouped, length, devices)
    arrived = lax.all_to_all(partial, ("rows", "cols"), split_axis=0, concat_axis=0, tiled=True)
    return row_transform(arrived, length, grouped[0].shape[0]).reshape(1, -1, length)


def solution(mesh):
    return jax.shard_map(
        local,
        mesh=mesh,
        in_specs=(P(None, "rows", "cols"),),
        out_specs=P(None, ("rows", "cols"), None),
        check_vma=False,
    )
```

```python
import functools
import math

import jax
import jax.numpy as jnp
import ml_dtypes
import numpy as np
from jax import lax
from jax.experimental import pallas as pl
from jax.experimental.pallas import tpu as pltpu
from jax.sharding import PartitionSpec as P

TAPS = 33
STRIDE = 8
REACH = TAPS // 2
GROUP_COLS = 1536
GROUP_OUTS = GROUP_COLS // STRIDE
LANES = 128
INNER = 256
COMPAND = 1023.0
LEVELS = 240
NONE_CODE = 2.0 ** -(LEVELS // 2)
ROW_MARGIN = 8
HALO_OUTS = 2


def ceil_to(value, step):
    return -(-value // step) * step


def split_host(table):
    high = table.astype(ml_dtypes.bfloat16)
    low = (table - high.astype(np.float64)).astype(ml_dtypes.bfloat16)
    return high, low


def taps_host():
    ids = np.arange(TAPS, dtype=np.float64)
    shaped = np.sinc((ids - REACH) / STRIDE) * (0.54 - 0.46 * np.cos(2 * np.pi * ids / (TAPS - 1)))
    return (shaped / shaped.sum()).astype(ml_dtypes.bfloat16)


def band(taps, tap_ids):
    table = jnp.zeros(tap_ids.shape, jnp.float32)
    for tap_id, tap in enumerate(taps):
        table = jnp.where(tap_ids == tap_id, tap, table)
    return table


def angles_host(left, right, length):
    reduced = (np.asarray(left)[:, None] * np.asarray(right)[None, :]) % length
    return 2 * np.pi * reduced / length


def taper_host(length):
    return (0.5 - 0.5 * np.cos(2 * np.pi * np.arange(length) / length)).astype(np.float32)


def split(value):
    high = value.astype(jnp.bfloat16)
    low = (value - high.astype(jnp.float32)).astype(jnp.bfloat16)
    return high, low


def row_scale(*arrays):
    peak = functools.reduce(jnp.maximum, [jnp.abs(array) for array in arrays])
    peak = jnp.max(peak, axis=-1, keepdims=True)
    return (peak * 1.01 + 1e-30).astype(jnp.bfloat16).astype(jnp.float32)


def encode(value, scale):
    level = jnp.log(1.0 + jnp.abs(value) * (COMPAND / scale)) * (LEVELS / math.log(1.001 * COMPAND))
    whole = jnp.floor(level)
    code = (1.0 + (level - whole)) * jnp.exp2(whole - LEVELS / 2)
    return jnp.where(value < 0, -code, code)


def decode(code, scale):
    size = jnp.abs(code)
    whole = jnp.floor(jnp.log2(size) + 0.0028)
    level = whole + (LEVELS / 2 - 1.0) + size * jnp.exp2(-whole)
    value = (jnp.exp(level * (math.log(1.001 * COMPAND) / LEVELS)) - 1.0) * (scale / COMPAND)
    return jnp.where(code < 0, -value, value)


def dot(left, right):
    return jnp.dot(left, right, preferred_element_type=jnp.float32)


def dot_nt(left, right):
    return lax.dot_general(left, right, (((1,), (1,)), ((), ())), preferred_element_type=jnp.float32)


def cut_kernel(shape, field, *refs):
    outs, refs = refs[: shape[-2]], refs[shape[-2] :]
    raw, arrived, band_rows, band_cols, total, cut, ordered, coded = refs
    taps, chunks, merged, groups, block_outs, fold, owners, own_rows = shape
    block_rows = raw.shape[1]

    def copy(chunk):
        rows = pl.ds(pl.multiple_of(chunk * block_rows, block_rows), block_rows)
        return pltpu.make_async_copy(field.at[0, rows, :], raw.at[chunk], arrived.at[chunk])

    for chunk in range(chunks):
        copy(chunk).start()
    total[...] = jnp.zeros_like(total)
    ids = lax.broadcasted_iota(jnp.int32, band_rows.shape, 1)
    ids = ids - STRIDE * (lax.broadcasted_iota(jnp.int32, band_rows.shape, 0) - ROW_MARGIN) + REACH
    band_rows[...] = band(taps, ids).astype(jnp.bfloat16)
    shape_8 = (8, band_cols.shape[1])
    ids = lax.broadcasted_iota(jnp.int32, shape_8, 0)
    ids = ids - STRIDE * (lax.broadcasted_iota(jnp.int32, shape_8, 1) - HALO_OUTS) + REACH
    initial = band(taps, ids)
    for pair in range(GROUP_COLS // 16):
        both = [pltpu.roll(initial, move, 1) if move else initial for move in (2 * pair, 2 * pair + 1)]
        band_cols[16 * pair : 16 * pair + 16, :] = jnp.concatenate(both, axis=0).astype(jnp.bfloat16)

    places = cut.shape[0]
    last = lax.broadcasted_iota(jnp.int32, (1, LANES), 1) == LANES - 1

    def finish(begin, count):
        rows = pl.ds(begin, count)
        middle = jnp.concatenate([total[1, rows, :], jnp.zeros((count, LANES), jnp.float32)], axis=1)
        middle = pltpu.roll(middle, 64, 1)
        joined = [
            total[0, rows, :LANES],
            total[0, rows, LANES:] + middle[:, :LANES],
            middle[:, LANES : 2 * LANES],
            middle[:, 2 * LANES :] + total[2, rows, :LANES],
            total[2, rows, LANES:],
        ]
        scale = row_scale(*joined)
        for place in range(places):
            code = encode(joined[place], scale)
            cut[place, rows, :] = jnp.where(last, scale, code) if place == places - 1 else code

    def step(turn, carry):
        for part in range(merged):
            copy(turn * merged + part).wait()
        stacked = [
            raw[turn * merged + part, :, group * GROUP_COLS : (group + 1) * GROUP_COLS]
            for group in range(groups)
            for part in range(merged)
        ]
        high, low = split(dot(jnp.concatenate(stacked, axis=0), band_cols[...]))
        rows = pl.ds(pl.multiple_of(turn * merged * block_outs, 8), band_rows.shape[0])
        for group in range(groups):
            own = slice(group * merged * block_rows, (group + 1) * merged * block_rows)
            total[group, rows, :] += dot(band_rows[...], high[own]) + dot(band_rows[...], low[own])
        return carry

    lax.fori_loop(0, chunks // merged, step, 0)
    finish(0, owners * own_rows + 2 * ROW_MARGIN)
    used = own_rows + 8
    sub = lax.broadcasted_iota(jnp.int32, (8, LANES), 0)
    if ordered.shape[0] > used:
        ordered[used:, :] = jnp.full((ordered.shape[0] - used, ordered.shape[1]), NONE_CODE, jnp.float32)
    for owner in range(owners):
        count = own_rows // fold
        begin_at = ROW_MARGIN + owner * own_rows
        edge = (ROW_MARGIN - 2, ROW_MARGIN - 1, ROW_MARGIN + owners * own_rows, ROW_MARGIN + owners * own_rows + 1)[owner]
        for place in range(places):
            lanes = slice(place * LANES, (place + 1) * LANES)
            for part in range(fold):
                picked = cut[pl.ds(place, 1), pl.ds(begin_at + part, count, stride=fold), :]
                ordered[part * count : (part + 1) * count, lanes] = picked[0]
            row = cut[place, edge : edge + 1, :]
            ordered[own_rows:used, lanes] = jnp.where(sub == 0, row, NONE_CODE)
        coded[owner] = ordered[...].astype(jnp.bfloat16)
    own_col = lax.axis_index("cols")
    for distance in range(owners):
        outs[distance][...] = coded[own_col ^ distance]


def cut_filter(field, owners, fold):
    _, raw_rows, raw_cols = field.shape
    block_rows = next(size for size in (256, 192, 128, 64) if raw_rows % size == 0)
    chunks = raw_rows // block_rows
    merged = 1
    groups = raw_cols // GROUP_COLS
    block_outs = block_rows // STRIDE
    own_rows = raw_rows // STRIDE // owners
    span = merged * block_outs + 2 * ROW_MARGIN
    count_rows = raw_rows // STRIDE + 2 * ROW_MARGIN
    out_cols = ceil_to(raw_cols // STRIDE + 2 * HALO_OUTS, LANES)
    taps = [float(tap) for tap in taps_host()]
    shape = (taps, chunks, merged, groups, block_outs, fold, owners, own_rows)
    out_rows = ceil_to(own_rows + 8, 16)
    return pl.pallas_call(
        functools.partial(cut_kernel, shape),
        out_shape=[jax.ShapeDtypeStruct((out_rows, out_cols), jnp.bfloat16)] * owners,
        in_specs=[pl.BlockSpec(memory_space=pl.ANY)],
        out_specs=[pl.BlockSpec(memory_space=pltpu.VMEM)] * owners,
        scratch_shapes=[
            pltpu.VMEM((chunks, block_rows, raw_cols), jnp.bfloat16),
            pltpu.SemaphoreType.DMA((chunks,)),
            pltpu.VMEM((span, merged * block_rows), jnp.bfloat16),
            pltpu.VMEM((GROUP_COLS, 2 * LANES), jnp.bfloat16),
            pltpu.VMEM((groups, count_rows, 2 * LANES), jnp.float32),
            pltpu.VMEM((out_cols // LANES, count_rows, LANES), jnp.float32),
            pltpu.VMEM((out_rows, out_cols), jnp.float32),
            pltpu.VMEM((owners, out_rows, out_cols), jnp.bfloat16),
        ],
        compiler_params=pltpu.CompilerParams(vmem_limit_bytes=40 * 2**20),
    )(field)


def column_kernel(shape, *refs):
    owners, rows, own_cols, fold = shape
    blocks, refs = refs[:owners], refs[owners:]
    weight, twiddle, table, out, held, joined, high_rows, low_rows = refs
    own_col = lax.axis_index("cols")
    joined[...] = jnp.zeros_like(joined)
    width = blocks[0].shape[1]
    inside = lax.broadcasted_iota(jnp.int32, (rows, width), 1) < own_cols + 2 * HALO_OUTS
    for distance in range(owners):
        code = blocks[distance][...].astype(jnp.float32)
        value = decode(code, code[:, width - 1 :])
        held[own_col ^ distance] = jnp.where(inside, value, 0.0)
    for owner in range(owners):
        first = LANES + own_cols * owner - HALO_OUTS
        block = jnp.concatenate([held[owner], jnp.zeros((rows, LANES), jnp.float32)], axis=1)
        base = first // LANES * LANES
        joined[:, base : base + width + LANES] += pltpu.roll(block, first - base, 1)
    points = [
        joined[:, LANES + INNER * i : LANES + INNER * (i + 1)] * weight[:, INNER * i : INNER * (i + 1)]
        for i in range(fold)
    ]
    half = fold // 2
    sums = [points[j] + points[fold - j] for j in range(1, half + 1)]
    differences = [points[j] - points[fold - j] for j in range(1, half + 1)]
    used = rows * fold
    if high_rows.shape[0] > used:
        rest = jnp.zeros((high_rows.shape[0] - used, 2 * INNER), jnp.bfloat16)
        high_rows[used:, :] = rest
        low_rows[used:, :] = rest

    def keep(freq, real, imag):
        for side, value in enumerate((real, imag)):
            high, low = split(value)
            place = (slice(freq * rows, (freq + 1) * rows), slice(side * INNER, (side + 1) * INNER))
            high_rows[place] = high
            low_rows[place] = low

    def turned(freq, real, imag):
        tc = twiddle[freq : freq + 1, :INNER]
        ts = twiddle[freq : freq + 1, INNER:]
        keep(freq, real * tc + imag * ts, imag * tc - real * ts)

    keep(0, functools.reduce(jnp.add, sums, points[0]), jnp.zeros((rows, INNER), jnp.float32))
    for freq in range(1, half + 1):
        real, imag = points[0], None
        for j in range(1, half + 1):
            angle = 2 * math.pi * ((j * freq) % fold) / fold
            real = real + math.cos(angle) * sums[j - 1]
            term = -math.sin(angle) * differences[j - 1]
            imag = term if imag is None else imag + term
        turned(freq, real, imag)
        turned(fold - freq, real, -imag)
    both = dot_nt(table[...], high_rows[...])
    result = both[:INNER] + both[INNER:] + dot_nt(table[:INNER, :], low_rows[...])
    scale = row_scale(result)
    code = encode(result, scale)
    lane = lax.broadcasted_iota(jnp.int32, code.shape, 1)
    code = jnp.where(lane == code.shape[1] - 1, scale, code)
    devices, tall, wide = out.shape
    pieces = code.shape[1] // wide
    code = code.reshape(devices, tall // pieces, code.shape[1])
    code = [code[:, :, piece * wide : (piece + 1) * wide] for piece in range(pieces)]
    out[...] = jnp.concatenate(code, axis=1).astype(jnp.bfloat16)


def column_transform(blocks, length, devices):
    owners = len(blocks)
    rows, width = blocks[0].shape
    own_cols = length // owners
    fold = length // INNER
    kept = INNER // 2
    per_device = kept // devices
    angle = angles_host(np.arange(fold), np.arange(INNER), length)
    twiddle = np.concatenate([np.cos(angle), np.sin(angle)], axis=1).astype(np.float32)
    angle = angles_host(np.arange(kept), np.arange(INNER), INNER)
    table = np.stack(
        [
            np.concatenate([np.cos(angle), np.sin(angle)], axis=1),
            np.concatenate([-np.sin(angle), np.cos(angle)], axis=1),
        ]
    )
    table = table.reshape(2, devices, per_device, 2 * INNER).transpose(1, 0, 2, 3).reshape(INNER, 2 * INNER)
    table = np.concatenate(split_host(table), axis=0)
    pieces = max(16 // (2 * per_device), 1)
    lanes = ceil_to(fold * rows + 1, pieces * LANES)
    return pl.pallas_call(
        functools.partial(column_kernel, (owners, rows, own_cols, fold)),
        out_shape=jax.ShapeDtypeStruct((devices, pieces * 2 * per_device, lanes // pieces), jnp.bfloat16),
        scratch_shapes=[
            pltpu.VMEM((owners, rows, width), jnp.float32),
            pltpu.VMEM((rows, length + 2 * LANES), jnp.float32),
            pltpu.VMEM((lanes, 2 * INNER), jnp.bfloat16),
            pltpu.VMEM((lanes, 2 * INNER), jnp.bfloat16),
        ],
        compiler_params=pltpu.CompilerParams(vmem_limit_bytes=48 * 2**20),
    )(*blocks, jnp.asarray(taper_host(length)[None, :]), jnp.asarray(twiddle), jnp.asarray(table))


def row_kernel(shape, arrived, weight, twiddle, high_table, low_table, out, blocks, spread, folded):
    length, fold, step, parts, packed, factor = shape
    devices, tall, wide = arrived.shape
    per_device = packed // 2
    pieces = tall // packed
    code = arrived[...].astype(jnp.float32)
    scale = code[:, tall - packed :, wide - 1 :]
    value = decode(code, jnp.concatenate([scale] * pieces, axis=1))
    for piece in range(pieces):
        blocks[:, :, piece * wide : (piece + 1) * wide] = value[:, piece * packed : (piece + 1) * packed]
    width = blocks.shape[2]
    slots = LANES // step
    lane = lax.broadcasted_iota(jnp.int32, (packed, LANES), 1) // step
    sign = jnp.where(lax.broadcasted_iota(jnp.int32, (packed, INNER), 0) < per_device, 1.0, -1.0)

    for column in range(width // LANES):
        for half in range(devices // slots):
            tiles = [
                blocks[half * slots + g, :, column * LANES : (column + 1) * LANES] for g in range(slots)
            ]
            bit = 1
            while bit < slots:
                upper = (lane & bit) != 0
                for g in range(slots):
                    if g & bit:
                        continue
                    a, b = tiles[g], tiles[g + bit]
                    tiles[g] = jnp.where(upper, pltpu.roll(b, bit * step, 1), a)
                    tiles[g + bit] = jnp.where(upper, b, pltpu.roll(a, LANES - bit * step, 1))
                bit *= 2
            for g in range(slots):
                q = column * slots + g
                if q < fold * parts:
                    spread[q, :, half * LANES : (half + 1) * LANES] = tiles[g]

    def quarter(value):
        return pltpu.roll(value, per_device, 0) * sign

    place = lax.broadcasted_iota(jnp.int32, (packed, INNER), 1)
    for freq in range(fold):
        halo = spread[freq * parts + fold]
        run = 4 * step
        extra = {}
        for owner, (target, shift) in enumerate(
            ((fold - 2, -1), (fold - 1, -1 - step), (0, 2 * step), (1, step))
        ):
            inside = place != owner * step if owner < 2 else place != INNER - run + owner * step
            only = jnp.where((place % run == owner * step) & inside, halo, 0.0)
            moved = pltpu.roll(only, shift % INNER, 1)
            extra[target] = extra[target] + moved if target in extra else moved
        for point in range(fold):
            value = spread[freq * parts + point]
            if point in extra:
                value = value + extra[point]
            folded[(point * fold + freq) * packed : (point * fold + freq + 1) * packed, :] = (
                value * weight[point : point + 1, :]
            )

    high, low = split(folded[...])
    both = dot(jnp.concatenate([high, low], axis=0), high_table[...])
    result = both[: high.shape[0]] + both[high.shape[0] :] + dot(high, low_table[...])
    for freq in range(fold):
        points = []
        for point in range(fold):
            begin = (point * fold + freq) * packed
            rows = slice(begin, begin + packed)
            value = result[rows, :INNER] + quarter(result[rows, INNER:])
            if point:
                tc = twiddle[point : point + 1, :INNER]
                ts = twiddle[point : point + 1, INNER:]
                value = value * tc + quarter(value) * ts
            points.append(value)
        half = fold // 2
        sums = [points[j] + points[fold - j] for j in range(1, half + 1)]
        differences = [quarter(points[j] - points[fold - j]) for j in range(1, half + 1)]

        def keep(index, value):
            power = value * value
            power = (power + pltpu.roll(power, per_device, 0)) * factor
            for side in range(INNER // LANES):
                row = (freq * length + index * INNER) // LANES + side
                rows = pl.ds(row, per_device, stride=fold * length // LANES)
                out[rows, :] = power[:per_device, side * LANES : (side + 1) * LANES]

        keep(0, functools.reduce(jnp.add, sums, points[0]))
        for index in range(1, half + 1):
            even, odd = points[0], None
            for j in range(1, half + 1):
                angle = 2 * math.pi * ((j * index) % fold) / fold
                even = even + math.cos(angle) * sums[j - 1]
                term = math.sin(angle) * differences[j - 1]
                odd = term if odd is None else odd + term
            keep(index, even + odd)
            keep(fold - index, even - odd)


def row_transform(arrived, length, rows):
    devices, tall, wide = arrived.shape
    packed = INNER // devices
    fold = length // INNER
    step = length // fold // devices
    angle = angles_host(np.arange(fold), np.arange(INNER), length)
    twiddle = np.concatenate([np.cos(angle), np.sin(angle)], axis=1).astype(np.float32)
    angle = angles_host(np.arange(INNER), np.arange(INNER), INNER)
    high_table, low_table = split_host(np.concatenate([np.cos(angle), np.sin(angle)], axis=1))
    parts = rows // step
    weight = np.ascontiguousarray(taper_host(length).reshape(INNER, fold).T)
    shape = (length, fold, step, parts, packed, STRIDE / (length * length))
    return pl.pallas_call(
        functools.partial(row_kernel, shape),
        out_shape=jax.ShapeDtypeStruct((fold * packed // 2 * length // LANES, LANES), jnp.float32),
        scratch_shapes=[
            pltpu.VMEM((devices, packed, tall * wide // packed), jnp.float32),
            pltpu.VMEM((fold * parts, packed, INNER), jnp.float32),
            pltpu.VMEM((fold * fold * packed, INNER), jnp.float32),
        ],
        compiler_params=pltpu.CompilerParams(vmem_limit_bytes=48 * 2**20),
    )(arrived, jnp.asarray(weight), jnp.asarray(twiddle), jnp.asarray(high_table), jnp.asarray(low_table))


def local(field):
    owners = lax.axis_size("cols")
    devices = lax.axis_size("rows") * owners
    length = field.shape[1] // STRIDE * lax.axis_size("rows")
    fold = length // INNER
    cut = cut_filter(field, owners, fold)
    grouped = [cut[0]] * owners
    for distance in reversed(range(1, owners)):
        pairs = [(col, col ^ distance) for col in range(owners)]
        grouped[distance] = lax.ppermute(cut[distance], "cols", pairs)
    partial = column_transform(grouped, length, devices)
    arrived = lax.all_to_all(partial, ("rows", "cols"), split_axis=0, concat_axis=0, tiled=True)
    return row_transform(arrived, length, grouped[0].shape[0]).reshape(1, -1, length)


def solution(mesh):
    return jax.shard_map(
        local,
        mesh=mesh,
        in_specs=(P(None, "rows", "cols"),),
        out_specs=P(None, ("rows", "cols"), None),
        check_vma=False,
    )
```

```python
import functools
import math

import jax
import jax.numpy as jnp
import ml_dtypes
import numpy as np
from jax import lax
from jax.experimental import pallas as pl
from jax.experimental.pallas import tpu as pltpu
from jax.sharding import PartitionSpec as P

TAPS = 33
STRIDE = 8
REACH = TAPS // 2
GROUP_COLS = 1536
GROUP_OUTS = GROUP_COLS // STRIDE
LANES = 128
INNER = 256
COMPAND = 1023.0
LEVELS = 240
NONE_CODE = 2.0 ** -(LEVELS // 2)
ROW_MARGIN = 8
HALO_OUTS = 2


def ceil_to(value, step):
    return -(-value // step) * step


def split_host(table):
    high = table.astype(ml_dtypes.bfloat16)
    low = (table - high.astype(np.float64)).astype(ml_dtypes.bfloat16)
    return high, low


def taps_host():
    ids = np.arange(TAPS, dtype=np.float64)
    shaped = np.sinc((ids - REACH) / STRIDE) * (0.54 - 0.46 * np.cos(2 * np.pi * ids / (TAPS - 1)))
    return (shaped / shaped.sum()).astype(ml_dtypes.bfloat16)


def band(taps, tap_ids):
    table = jnp.zeros(tap_ids.shape, jnp.float32)
    for tap_id, tap in enumerate(taps):
        table = jnp.where(tap_ids == tap_id, tap, table)
    return table


def angles_host(left, right, length):
    reduced = (np.asarray(left)[:, None] * np.asarray(right)[None, :]) % length
    return 2 * np.pi * reduced / length


def taper_host(length):
    return (0.5 - 0.5 * np.cos(2 * np.pi * np.arange(length) / length)).astype(np.float32)


def split(value):
    high = value.astype(jnp.bfloat16)
    low = (value - high.astype(jnp.float32)).astype(jnp.bfloat16)
    return high, low


def row_scale(*arrays):
    peak = functools.reduce(jnp.maximum, [jnp.abs(array) for array in arrays])
    peak = jnp.max(peak, axis=-1, keepdims=True)
    return (peak * 1.01 + 1e-30).astype(jnp.bfloat16).astype(jnp.float32)


def encode(value, scale):
    level = jnp.log(1.0 + jnp.abs(value) * (COMPAND / scale)) * (LEVELS / math.log(1.001 * COMPAND))
    whole = jnp.floor(level)
    code = (1.0 + (level - whole)) * jnp.exp2(whole - LEVELS / 2)
    return jnp.where(value < 0, -code, code)


def decode(code, scale):
    size = jnp.abs(code)
    whole = jnp.floor(jnp.log2(size) + 0.0028)
    level = whole + (LEVELS / 2 - 1.0) + size * jnp.exp2(-whole)
    value = (jnp.exp(level * (math.log(1.001 * COMPAND) / LEVELS)) - 1.0) * (scale / COMPAND)
    return jnp.where(code < 0, -value, value)


def dot(left, right):
    return jnp.dot(left, right, preferred_element_type=jnp.float32)


def dot_nt(left, right):
    return lax.dot_general(left, right, (((1,), (1,)), ((), ())), preferred_element_type=jnp.float32)


def distance_of(index, owners):
    return (owners - index) % owners


def cut_kernel(shape, field, *refs):
    outs, refs = refs[: shape[-2]], refs[shape[-2] :]
    raw, arrived, band_rows, band_cols, total, cut, ordered, coded = refs
    taps, chunks, merged, groups, block_outs, fold, owners, own_rows = shape
    block_rows = raw.shape[1]

    def copy(chunk):
        rows = pl.ds(pl.multiple_of(chunk * block_rows, block_rows), block_rows)
        return pltpu.make_async_copy(field.at[0, rows, :], raw.at[chunk], arrived.at[chunk])

    for chunk in range(chunks):
        copy(chunk).start()
    total[...] = jnp.zeros_like(total)
    ids = lax.broadcasted_iota(jnp.int32, band_rows.shape, 1)
    ids = ids - STRIDE * (lax.broadcasted_iota(jnp.int32, band_rows.shape, 0) - ROW_MARGIN) + REACH
    band_rows[...] = band(taps, ids).astype(jnp.bfloat16)
    shape_8 = (8, band_cols.shape[1])
    ids = lax.broadcasted_iota(jnp.int32, shape_8, 0)
    ids = ids - STRIDE * (lax.broadcasted_iota(jnp.int32, shape_8, 1) - HALO_OUTS) + REACH
    initial = band(taps, ids)
    for pair in range(GROUP_COLS // 16):
        both = [pltpu.roll(initial, move, 1) if move else initial for move in (2 * pair, 2 * pair + 1)]
        band_cols[16 * pair : 16 * pair + 16, :] = jnp.concatenate(both, axis=0).astype(jnp.bfloat16)

    places = cut.shape[0]
    last = lax.broadcasted_iota(jnp.int32, (1, LANES), 1) == LANES - 1

    def finish(begin, count):
        rows = pl.ds(begin, count)
        middle = jnp.concatenate([total[1, rows, :], jnp.zeros((count, LANES), jnp.float32)], axis=1)
        middle = pltpu.roll(middle, 64, 1)
        joined = [
            total[0, rows, :LANES],
            total[0, rows, LANES:] + middle[:, :LANES],
            middle[:, LANES : 2 * LANES],
            middle[:, 2 * LANES :] + total[2, rows, :LANES],
            total[2, rows, LANES:],
        ]
        scale = row_scale(*joined)
        for place in range(places):
            code = encode(joined[place], scale)
            cut[place, rows, :] = jnp.where(last, scale, code) if place == places - 1 else code

    def step(turn, carry):
        for part in range(merged):
            copy(turn * merged + part).wait()
        stacked = [
            raw[turn * merged + part, :, group * GROUP_COLS : (group + 1) * GROUP_COLS]
            for group in range(groups)
            for part in range(merged)
        ]
        high, low = split(dot(jnp.concatenate(stacked, axis=0), band_cols[...]))
        rows = pl.ds(pl.multiple_of(turn * merged * block_outs, 8), band_rows.shape[0])
        for group in range(groups):
            own = slice(group * merged * block_rows, (group + 1) * merged * block_rows)
            total[group, rows, :] += dot(band_rows[...], high[own]) + dot(band_rows[...], low[own])
        finish(pl.multiple_of(turn * merged * block_outs, 8), merged * block_outs)
        return carry

    lax.fori_loop(0, chunks // merged, step, 0)
    finish(owners * own_rows, 2 * ROW_MARGIN)
    used = own_rows + 8
    sub = lax.broadcasted_iota(jnp.int32, (8, LANES), 0)
    if ordered.shape[0] > used:
        ordered[used:, :] = jnp.full((ordered.shape[0] - used, ordered.shape[1]), NONE_CODE, jnp.float32)
    for owner in range(owners):
        count = own_rows // fold
        begin_at = ROW_MARGIN + owner * own_rows
        edge = (ROW_MARGIN - 2, ROW_MARGIN - 1, ROW_MARGIN + owners * own_rows, ROW_MARGIN + owners * own_rows + 1)[owner]
        for place in range(places):
            lanes = slice(place * LANES, (place + 1) * LANES)
            for part in range(fold):
                picked = cut[pl.ds(place, 1), pl.ds(begin_at + part, count, stride=fold), :]
                ordered[part * count : (part + 1) * count, lanes] = picked[0]
            row = cut[place, edge : edge + 1, :]
            ordered[own_rows:used, lanes] = jnp.where(sub == 0, row, NONE_CODE)
        coded[owner] = ordered[...].astype(jnp.bfloat16)
    own_col = lax.axis_index("cols")
    for index, out in enumerate(outs):
        out[...] = coded[own_col ^ distance_of(index, owners)]


def cut_filter(field, owners, fold):
    _, raw_rows, raw_cols = field.shape
    block_rows = next(size for size in (256, 192, 128, 64) if raw_rows % size == 0)
    chunks = raw_rows // block_rows
    merged = 1
    groups = raw_cols // GROUP_COLS
    block_outs = block_rows // STRIDE
    own_rows = raw_rows // STRIDE // owners
    span = merged * block_outs + 2 * ROW_MARGIN
    count_rows = raw_rows // STRIDE + 2 * ROW_MARGIN
    out_cols = ceil_to(raw_cols // STRIDE + 2 * HALO_OUTS, LANES)
    taps = [float(tap) for tap in taps_host()]
    shape = (taps, chunks, merged, groups, block_outs, fold, owners, own_rows)
    out_rows = ceil_to(own_rows + 8, 16)
    return pl.pallas_call(
        functools.partial(cut_kernel, shape),
        out_shape=[jax.ShapeDtypeStruct((out_rows, out_cols), jnp.bfloat16)] * owners,
        in_specs=[pl.BlockSpec(memory_space=pl.ANY)],
        out_specs=[pl.BlockSpec(memory_space=pltpu.VMEM)] * owners,
        scratch_shapes=[
            pltpu.VMEM((chunks, block_rows, raw_cols), jnp.bfloat16),
            pltpu.SemaphoreType.DMA((chunks,)),
            pltpu.VMEM((span, merged * block_rows), jnp.bfloat16),
            pltpu.VMEM((GROUP_COLS, 2 * LANES), jnp.bfloat16),
            pltpu.VMEM((groups, count_rows, 2 * LANES), jnp.float32),
            pltpu.VMEM((out_cols // LANES, count_rows, LANES), jnp.float32),
            pltpu.VMEM((out_rows, out_cols), jnp.float32),
            pltpu.VMEM((owners, out_rows, out_cols), jnp.bfloat16),
        ],
        compiler_params=pltpu.CompilerParams(vmem_limit_bytes=40 * 2**20),
    )(field)


def column_kernel(shape, *refs):
    owners, rows, own_cols, fold = shape
    blocks, refs = refs[:owners], refs[owners:]
    weight, twiddle, table, out, held, joined, high_rows, low_rows = refs
    own_col = lax.axis_index("cols")
    joined[...] = jnp.zeros_like(joined)
    width = blocks[0].shape[1]
    inside = lax.broadcasted_iota(jnp.int32, (rows, width), 1) < own_cols + 2 * HALO_OUTS
    for index, block in enumerate(blocks):
        code = block[...].astype(jnp.float32)
        value = decode(code, code[:, width - 1 :])
        held[own_col ^ distance_of(index, owners)] = jnp.where(inside, value, 0.0)
    for owner in range(owners):
        first = LANES + own_cols * owner - HALO_OUTS
        block = jnp.concatenate([held[owner], jnp.zeros((rows, LANES), jnp.float32)], axis=1)
        base = first // LANES * LANES
        joined[:, base : base + width + LANES] += pltpu.roll(block, first - base, 1)
    points = [
        joined[:, LANES + INNER * i : LANES + INNER * (i + 1)] * weight[:, INNER * i : INNER * (i + 1)]
        for i in range(fold)
    ]
    half = fold // 2
    sums = [points[j] + points[fold - j] for j in range(1, half + 1)]
    differences = [points[j] - points[fold - j] for j in range(1, half + 1)]
    used = rows * fold
    if high_rows.shape[0] > used:
        rest = jnp.zeros((high_rows.shape[0] - used, 2 * INNER), jnp.bfloat16)
        high_rows[used:, :] = rest
        low_rows[used:, :] = rest

    def keep(freq, real, imag):
        for side, value in enumerate((real, imag)):
            high, low = split(value)
            place = (slice(freq * rows, (freq + 1) * rows), slice(side * INNER, (side + 1) * INNER))
            high_rows[place] = high
            low_rows[place] = low

    def turned(freq, real, imag):
        tc = twiddle[freq : freq + 1, :INNER]
        ts = twiddle[freq : freq + 1, INNER:]
        keep(freq, real * tc + imag * ts, imag * tc - real * ts)

    keep(0, functools.reduce(jnp.add, sums, points[0]), jnp.zeros((rows, INNER), jnp.float32))
    for freq in range(1, half + 1):
        real, imag = points[0], None
        for j in range(1, half + 1):
            angle = 2 * math.pi * ((j * freq) % fold) / fold
            real = real + math.cos(angle) * sums[j - 1]
            term = -math.sin(angle) * differences[j - 1]
            imag = term if imag is None else imag + term
        turned(freq, real, imag)
        turned(fold - freq, real, -imag)
    both = dot_nt(table[...], high_rows[...])
    result = both[:INNER] + both[INNER:] + dot_nt(table[:INNER, :], low_rows[...])
    scale = row_scale(result)
    code = encode(result, scale)
    lane = lax.broadcasted_iota(jnp.int32, code.shape, 1)
    code = jnp.where(lane == code.shape[1] - 1, scale, code)
    devices, tall, wide = out.shape
    pieces = code.shape[1] // wide
    code = code.reshape(devices, tall // pieces, code.shape[1])
    code = [code[:, :, piece * wide : (piece + 1) * wide] for piece in range(pieces)]
    out[...] = jnp.concatenate(code, axis=1).astype(jnp.bfloat16)


def column_transform(blocks, length, devices):
    owners = len(blocks)
    rows, width = blocks[0].shape
    own_cols = length // owners
    fold = length // INNER
    kept = INNER // 2
    per_device = kept // devices
    angle = angles_host(np.arange(fold), np.arange(INNER), length)
    twiddle = np.concatenate([np.cos(angle), np.sin(angle)], axis=1).astype(np.float32)
    angle = angles_host(np.arange(kept), np.arange(INNER), INNER)
    table = np.stack(
        [
            np.concatenate([np.cos(angle), np.sin(angle)], axis=1),
            np.concatenate([-np.sin(angle), np.cos(angle)], axis=1),
        ]
    )
    table = table.reshape(2, devices, per_device, 2 * INNER).transpose(1, 0, 2, 3).reshape(INNER, 2 * INNER)
    table = np.concatenate(split_host(table), axis=0)
    pieces = max(16 // (2 * per_device), 1)
    lanes = ceil_to(fold * rows + 1, pieces * LANES)
    return pl.pallas_call(
        functools.partial(column_kernel, (owners, rows, own_cols, fold)),
        out_shape=jax.ShapeDtypeStruct((devices, pieces * 2 * per_device, lanes // pieces), jnp.bfloat16),
        scratch_shapes=[
            pltpu.VMEM((owners, rows, width), jnp.float32),
            pltpu.VMEM((rows, length + 2 * LANES), jnp.float32),
            pltpu.VMEM((lanes, 2 * INNER), jnp.bfloat16),
            pltpu.VMEM((lanes, 2 * INNER), jnp.bfloat16),
        ],
        compiler_params=pltpu.CompilerParams(vmem_limit_bytes=48 * 2**20),
    )(*blocks, jnp.asarray(taper_host(length)[None, :]), jnp.asarray(twiddle), jnp.asarray(table))


def row_kernel(shape, arrived, weight, twiddle, high_table, low_table, out, blocks, spread, folded):
    length, fold, step, parts, packed, factor = shape
    devices, tall, wide = arrived.shape
    per_device = packed // 2
    pieces = tall // packed
    code = arrived[...].astype(jnp.float32)
    scale = code[:, tall - packed :, wide - 1 :]
    value = decode(code, jnp.concatenate([scale] * pieces, axis=1))
    for piece in range(pieces):
        blocks[:, :, piece * wide : (piece + 1) * wide] = value[:, piece * packed : (piece + 1) * packed]
    width = blocks.shape[2]
    slots = LANES // step
    lane = lax.broadcasted_iota(jnp.int32, (packed, LANES), 1) // step
    sign = jnp.where(lax.broadcasted_iota(jnp.int32, (packed, INNER), 0) < per_device, 1.0, -1.0)

    for column in range(width // LANES):
        for half in range(devices // slots):
            tiles = [
                blocks[half * slots + g, :, column * LANES : (column + 1) * LANES] for g in range(slots)
            ]
            bit = 1
            while bit < slots:
                upper = (lane & bit) != 0
                for g in range(slots):
                    if g & bit:
                        continue
                    a, b = tiles[g], tiles[g + bit]
                    tiles[g] = jnp.where(upper, pltpu.roll(b, bit * step, 1), a)
                    tiles[g + bit] = jnp.where(upper, b, pltpu.roll(a, LANES - bit * step, 1))
                bit *= 2
            for g in range(slots):
                q = column * slots + g
                if q < fold * parts:
                    spread[q, :, half * LANES : (half + 1) * LANES] = tiles[g]

    def quarter(value):
        return pltpu.roll(value, per_device, 0) * sign

    place = lax.broadcasted_iota(jnp.int32, (packed, INNER), 1)
    for freq in range(fold):
        halo = spread[freq * parts + fold]
        run = 4 * step
        extra = {}
        for owner, (target, shift) in enumerate(
            ((fold - 2, -1), (fold - 1, -1 - step), (0, 2 * step), (1, step))
        ):
            inside = place != owner * step if owner < 2 else place != INNER - run + owner * step
            only = jnp.where((place % run == owner * step) & inside, halo, 0.0)
            moved = pltpu.roll(only, shift % INNER, 1)
            extra[target] = extra[target] + moved if target in extra else moved
        for point in range(fold):
            value = spread[freq * parts + point]
            if point in extra:
                value = value + extra[point]
            folded[(point * fold + freq) * packed : (point * fold + freq + 1) * packed, :] = (
                value * weight[point : point + 1, :]
            )

    high, low = split(folded[...])
    both = dot(jnp.concatenate([high, low], axis=0), high_table[...])
    result = both[: high.shape[0]] + both[high.shape[0] :] + dot(high, low_table[...])
    for freq in range(fold):
        points = []
        for point in range(fold):
            begin = (point * fold + freq) * packed
            rows = slice(begin, begin + packed)
            value = result[rows, :INNER] + quarter(result[rows, INNER:])
            if point:
                tc = twiddle[point : point + 1, :INNER]
                ts = twiddle[point : point + 1, INNER:]
                value = value * tc + quarter(value) * ts
            points.append(value)
        half = fold // 2
        sums = [points[j] + points[fold - j] for j in range(1, half + 1)]
        differences = [quarter(points[j] - points[fold - j]) for j in range(1, half + 1)]

        def keep(index, value):
            power = value * value
            power = (power + pltpu.roll(power, per_device, 0)) * factor
            for side in range(INNER // LANES):
                row = (freq * length + index * INNER) // LANES + side
                rows = pl.ds(row, per_device, stride=fold * length // LANES)
                out[rows, :] = power[:per_device, side * LANES : (side + 1) * LANES]

        keep(0, functools.reduce(jnp.add, sums, points[0]))
        for index in range(1, half + 1):
            even, odd = points[0], None
            for j in range(1, half + 1):
                angle = 2 * math.pi * ((j * index) % fold) / fold
                even = even + math.cos(angle) * sums[j - 1]
                term = math.sin(angle) * differences[j - 1]
                odd = term if odd is None else odd + term
            keep(index, even + odd)
            keep(fold - index, even - odd)


def row_transform(arrived, length, rows):
    devices, tall, wide = arrived.shape
    packed = INNER // devices
    fold = length // INNER
    step = length // fold // devices
    angle = angles_host(np.arange(fold), np.arange(INNER), length)
    twiddle = np.concatenate([np.cos(angle), np.sin(angle)], axis=1).astype(np.float32)
    angle = angles_host(np.arange(INNER), np.arange(INNER), INNER)
    high_table, low_table = split_host(np.concatenate([np.cos(angle), np.sin(angle)], axis=1))
    parts = rows // step
    weight = np.ascontiguousarray(taper_host(length).reshape(INNER, fold).T)
    shape = (length, fold, step, parts, packed, STRIDE / (length * length))
    return pl.pallas_call(
        functools.partial(row_kernel, shape),
        out_shape=jax.ShapeDtypeStruct((fold * packed // 2 * length // LANES, LANES), jnp.float32),
        scratch_shapes=[
            pltpu.VMEM((devices, packed, tall * wide // packed), jnp.float32),
            pltpu.VMEM((fold * parts, packed, INNER), jnp.float32),
            pltpu.VMEM((fold * fold * packed, INNER), jnp.float32),
        ],
        compiler_params=pltpu.CompilerParams(vmem_limit_bytes=48 * 2**20),
    )(arrived, jnp.asarray(weight), jnp.asarray(twiddle), jnp.asarray(high_table), jnp.asarray(low_table))


def local(field):
    owners = lax.axis_size("cols")
    devices = lax.axis_size("rows") * owners
    length = field.shape[1] // STRIDE * lax.axis_size("rows")
    fold = length // INNER
    cut = cut_filter(field, owners, fold)
    grouped = [cut[0]]
    for index in range(1, owners):
        pairs = [(col, col ^ distance_of(index, owners)) for col in range(owners)]
        grouped.append(lax.ppermute(cut[index], "cols", pairs))
    partial = column_transform(grouped, length, devices)
    arrived = lax.all_to_all(partial, ("rows", "cols"), split_axis=0, concat_axis=0, tiled=True)
    return row_transform(arrived, length, grouped[0].shape[0]).reshape(1, -1, length)


def solution(mesh):
    return jax.shard_map(
        local,
        mesh=mesh,
        in_specs=(P(None, "rows", "cols"),),
        out_specs=P(None, ("rows", "cols"), None),
        check_vma=False,
    )
```

```python
import functools
import math

import jax
import jax.numpy as jnp
import ml_dtypes
import numpy as np
from jax import lax
from jax.experimental import pallas as pl
from jax.experimental.pallas import tpu as pltpu
from jax.sharding import PartitionSpec as P

TAPS = 33
STRIDE = 8
REACH = TAPS // 2
GROUP_COLS = 1536
GROUP_OUTS = GROUP_COLS // STRIDE
LANES = 128
INNER = 256
COMPAND = 1023.0
LEVELS = 240
NONE_CODE = 2.0 ** -(LEVELS // 2)
ROW_MARGIN = 8
HALO_OUTS = 2


def ceil_to(value, step):
    return -(-value // step) * step


def split_host(table):
    high = table.astype(ml_dtypes.bfloat16)
    low = (table - high.astype(np.float64)).astype(ml_dtypes.bfloat16)
    return high, low


def taps_host():
    ids = np.arange(TAPS, dtype=np.float64)
    shaped = np.sinc((ids - REACH) / STRIDE) * (0.54 - 0.46 * np.cos(2 * np.pi * ids / (TAPS - 1)))
    return (shaped / shaped.sum()).astype(ml_dtypes.bfloat16)


def band(taps, tap_ids):
    table = jnp.zeros(tap_ids.shape, jnp.float32)
    for tap_id, tap in enumerate(taps):
        table = jnp.where(tap_ids == tap_id, tap, table)
    return table


def angles_host(left, right, length):
    reduced = (np.asarray(left)[:, None] * np.asarray(right)[None, :]) % length
    return 2 * np.pi * reduced / length


def taper_host(length):
    return (0.5 - 0.5 * np.cos(2 * np.pi * np.arange(length) / length)).astype(np.float32)


def split(value):
    high = value.astype(jnp.bfloat16)
    low = (value - high.astype(jnp.float32)).astype(jnp.bfloat16)
    return high, low


def row_scale(*arrays):
    peak = functools.reduce(jnp.maximum, [jnp.abs(array) for array in arrays])
    peak = jnp.max(peak, axis=-1, keepdims=True)
    return (peak * 1.01 + 1e-30).astype(jnp.bfloat16).astype(jnp.float32)


def encode(value, scale):
    level = jnp.log(1.0 + jnp.abs(value) * (COMPAND / scale)) * (LEVELS / math.log(1.001 * COMPAND))
    whole = jnp.floor(level)
    code = (1.0 + (level - whole)) * jnp.exp2(whole - LEVELS / 2)
    return jnp.where(value < 0, -code, code)


def decode(code, scale):
    size = jnp.abs(code)
    whole = jnp.floor(jnp.log2(size) + 0.0028)
    level = whole + (LEVELS / 2 - 1.0) + size * jnp.exp2(-whole)
    value = (jnp.exp(level * (math.log(1.001 * COMPAND) / LEVELS)) - 1.0) * (scale / COMPAND)
    return jnp.where(code < 0, -value, value)


def dot(left, right):
    return jnp.dot(left, right, preferred_element_type=jnp.float32)


def dot_nt(left, right):
    return lax.dot_general(left, right, (((1,), (1,)), ((), ())), preferred_element_type=jnp.float32)


def cut_kernel(shape, field, *refs):
    outs, refs = refs[: shape[-2]], refs[shape[-2] :]
    raw, arrived, band_rows, band_cols, total, cut, ordered, coded = refs
    taps, chunks, merged, groups, block_outs, fold, owners, own_rows = shape
    block_rows = raw.shape[1]

    def copy(chunk):
        rows = pl.ds(pl.multiple_of(chunk * block_rows, block_rows), block_rows)
        return pltpu.make_async_copy(field.at[0, rows, :], raw.at[chunk], arrived.at[chunk])

    for chunk in range(chunks):
        copy(chunk).start()
    total[...] = jnp.zeros_like(total)
    ids = lax.broadcasted_iota(jnp.int32, band_rows.shape, 1)
    ids = ids - STRIDE * (lax.broadcasted_iota(jnp.int32, band_rows.shape, 0) - ROW_MARGIN) + REACH
    band_rows[...] = band(taps, ids).astype(jnp.bfloat16)
    shape_8 = (8, band_cols.shape[1])
    ids = lax.broadcasted_iota(jnp.int32, shape_8, 0)
    ids = ids - STRIDE * (lax.broadcasted_iota(jnp.int32, shape_8, 1) - HALO_OUTS) + REACH
    initial = band(taps, ids)
    for pair in range(GROUP_COLS // 16):
        both = [pltpu.roll(initial, move, 1) if move else initial for move in (2 * pair, 2 * pair + 1)]
        band_cols[16 * pair : 16 * pair + 16, :] = jnp.concatenate(both, axis=0).astype(jnp.bfloat16)

    places = cut.shape[0]
    last = lax.broadcasted_iota(jnp.int32, (1, LANES), 1) == LANES - 1

    def finish(begin, count):
        rows = pl.ds(begin, count)
        middle = jnp.concatenate([total[1, rows, :], jnp.zeros((count, LANES), jnp.float32)], axis=1)
        middle = pltpu.roll(middle, 64, 1)
        joined = [
            total[0, rows, :LANES],
            total[0, rows, LANES:] + middle[:, :LANES],
            middle[:, LANES : 2 * LANES],
            middle[:, 2 * LANES :] + total[2, rows, :LANES],
            total[2, rows, LANES:],
        ]
        scale = row_scale(*joined)
        for place in range(places):
            code = encode(joined[place], scale)
            cut[place, rows, :] = jnp.where(last, scale, code) if place == places - 1 else code

    def step(turn, carry):
        for part in range(merged):
            copy(turn * merged + part).wait()
        stacked = [
            raw[turn * merged + part, :, group * GROUP_COLS : (group + 1) * GROUP_COLS]
            for group in range(groups)
            for part in range(merged)
        ]
        high, low = split(dot(jnp.concatenate(stacked, axis=0), band_cols[...]))
        rows = pl.ds(pl.multiple_of(turn * merged * block_outs, 8), band_rows.shape[0])
        for group in range(groups):
            own = slice(group * merged * block_rows, (group + 1) * merged * block_rows)
            total[group, rows, :] += dot(band_rows[...], high[own]) + dot(band_rows[...], low[own])
        return carry

    lax.fori_loop(0, chunks // merged, step, 0)
    finish(0, owners * own_rows + 2 * ROW_MARGIN)
    used = own_rows + 8
    sub = lax.broadcasted_iota(jnp.int32, (8, LANES), 0)
    if ordered.shape[0] > used:
        ordered[used:, :] = jnp.full((ordered.shape[0] - used, ordered.shape[1]), NONE_CODE, jnp.float32)
    for owner in range(owners):
        count = own_rows // fold
        begin_at = ROW_MARGIN + owner * own_rows
        edge = (ROW_MARGIN - 2, ROW_MARGIN - 1, ROW_MARGIN + owners * own_rows, ROW_MARGIN + owners * own_rows + 1)[owner]
        for place in range(places):
            lanes = slice(place * LANES, (place + 1) * LANES)
            for part in range(fold):
                picked = cut[pl.ds(place, 1), pl.ds(begin_at + part, count, stride=fold), :]
                ordered[part * count : (part + 1) * count, lanes] = picked[0]
            row = cut[place, edge : edge + 1, :]
            ordered[own_rows:used, lanes] = jnp.where(sub == 0, row, NONE_CODE)
        coded[owner] = ordered[...].astype(jnp.bfloat16)
    own_col = lax.axis_index("cols")
    for distance in range(owners):
        outs[distance][...] = coded[own_col ^ distance]


def cut_filter(field, owners, fold):
    _, raw_rows, raw_cols = field.shape
    block_rows = next(size for size in (256, 192, 128, 64) if raw_rows % size == 0)
    chunks = raw_rows // block_rows
    merged = 1
    groups = raw_cols // GROUP_COLS
    block_outs = block_rows // STRIDE
    own_rows = raw_rows // STRIDE // owners
    span = merged * block_outs + 2 * ROW_MARGIN
    count_rows = raw_rows // STRIDE + 2 * ROW_MARGIN
    out_cols = ceil_to(raw_cols // STRIDE + 2 * HALO_OUTS, LANES)
    taps = [float(tap) for tap in taps_host()]
    shape = (taps, chunks, merged, groups, block_outs, fold, owners, own_rows)
    out_rows = ceil_to(own_rows + 8, 16)
    return pl.pallas_call(
        functools.partial(cut_kernel, shape),
        out_shape=[jax.ShapeDtypeStruct((out_rows, out_cols), jnp.bfloat16)] * owners,
        in_specs=[pl.BlockSpec(memory_space=pl.ANY)],
        out_specs=[pl.BlockSpec(memory_space=pltpu.VMEM)] * owners,
        scratch_shapes=[
            pltpu.VMEM((chunks, block_rows, raw_cols), jnp.bfloat16),
            pltpu.SemaphoreType.DMA((chunks,)),
            pltpu.VMEM((span, merged * block_rows), jnp.bfloat16),
            pltpu.VMEM((GROUP_COLS, 2 * LANES), jnp.bfloat16),
            pltpu.VMEM((groups, count_rows, 2 * LANES), jnp.float32),
            pltpu.VMEM((out_cols // LANES, count_rows, LANES), jnp.float32),
            pltpu.VMEM((out_rows, out_cols), jnp.float32),
            pltpu.VMEM((owners, out_rows, out_cols), jnp.bfloat16),
        ],
        compiler_params=pltpu.CompilerParams(vmem_limit_bytes=40 * 2**20),
    )(field)


def column_kernel(shape, *refs):
    owners, rows, own_cols, fold = shape
    blocks, refs = refs[:owners], refs[owners:]
    weight, twiddle, table, out, held, joined, high_rows, low_rows = refs
    own_col = lax.axis_index("cols")
    joined[...] = jnp.zeros_like(joined)
    width = blocks[0].shape[1]
    inside = lax.broadcasted_iota(jnp.int32, (rows, width), 1) < own_cols + 2 * HALO_OUTS
    for distance in range(owners):
        code = blocks[distance][...].astype(jnp.float32)
        value = decode(code, code[:, width - 1 :])
        held[own_col ^ distance] = jnp.where(inside, value, 0.0)
    for owner in range(owners):
        first = LANES + own_cols * owner - HALO_OUTS
        block = jnp.concatenate([held[owner], jnp.zeros((rows, LANES), jnp.float32)], axis=1)
        base = first // LANES * LANES
        joined[:, base : base + width + LANES] += pltpu.roll(block, first - base, 1)
    points = [
        joined[:, LANES + INNER * i : LANES + INNER * (i + 1)] * weight[:, INNER * i : INNER * (i + 1)]
        for i in range(fold)
    ]
    half = fold // 2
    sums = [points[j] + points[fold - j] for j in range(1, half + 1)]
    differences = [points[j] - points[fold - j] for j in range(1, half + 1)]
    used = rows * fold
    if high_rows.shape[0] > used:
        rest = jnp.zeros((high_rows.shape[0] - used, 2 * INNER), jnp.bfloat16)
        high_rows[used:, :] = rest
        low_rows[used:, :] = rest

    def keep(freq, real, imag):
        for side, value in enumerate((real, imag)):
            high, low = split(value)
            place = (slice(freq * rows, (freq + 1) * rows), slice(side * INNER, (side + 1) * INNER))
            high_rows[place] = high
            low_rows[place] = low

    def turned(freq, real, imag):
        tc = twiddle[freq : freq + 1, :INNER]
        ts = twiddle[freq : freq + 1, INNER:]
        keep(freq, real * tc + imag * ts, imag * tc - real * ts)

    keep(0, functools.reduce(jnp.add, sums, points[0]), jnp.zeros((rows, INNER), jnp.float32))
    for freq in range(1, half + 1):
        real, imag = points[0], None
        for j in range(1, half + 1):
            angle = 2 * math.pi * ((j * freq) % fold) / fold
            real = real + math.cos(angle) * sums[j - 1]
            term = -math.sin(angle) * differences[j - 1]
            imag = term if imag is None else imag + term
        turned(freq, real, imag)
        turned(fold - freq, real, -imag)
    both = dot(high_rows[...], table[...])
    result = (both[:, :INNER] + both[:, INNER:] + dot(low_rows[...], table[:, :INNER])).T
    scale = row_scale(result)
    code = encode(result, scale)
    lane = lax.broadcasted_iota(jnp.int32, code.shape, 1)
    code = jnp.where(lane == code.shape[1] - 1, scale, code)
    devices, tall, wide = out.shape
    pieces = code.shape[1] // wide
    code = code.reshape(devices, tall // pieces, code.shape[1])
    code = [code[:, :, piece * wide : (piece + 1) * wide] for piece in range(pieces)]
    out[...] = jnp.concatenate(code, axis=1).astype(jnp.bfloat16)


def column_transform(blocks, length, devices):
    owners = len(blocks)
    rows, width = blocks[0].shape
    own_cols = length // owners
    fold = length // INNER
    kept = INNER // 2
    per_device = kept // devices
    angle = angles_host(np.arange(fold), np.arange(INNER), length)
    twiddle = np.concatenate([np.cos(angle), np.sin(angle)], axis=1).astype(np.float32)
    angle = angles_host(np.arange(kept), np.arange(INNER), INNER)
    table = np.stack(
        [
            np.concatenate([np.cos(angle), np.sin(angle)], axis=1),
            np.concatenate([-np.sin(angle), np.cos(angle)], axis=1),
        ]
    )
    table = table.reshape(2, devices, per_device, 2 * INNER).transpose(1, 0, 2, 3).reshape(INNER, 2 * INNER)
    table = np.concatenate([part.T for part in split_host(table)], axis=1)
    pieces = max(16 // (2 * per_device), 1)
    lanes = ceil_to(fold * rows + 1, pieces * LANES)
    return pl.pallas_call(
        functools.partial(column_kernel, (owners, rows, own_cols, fold)),
        out_shape=jax.ShapeDtypeStruct((devices, pieces * 2 * per_device, lanes // pieces), jnp.bfloat16),
        scratch_shapes=[
            pltpu.VMEM((owners, rows, width), jnp.float32),
            pltpu.VMEM((rows, length + 2 * LANES), jnp.float32),
            pltpu.VMEM((lanes, 2 * INNER), jnp.bfloat16),
            pltpu.VMEM((lanes, 2 * INNER), jnp.bfloat16),
        ],
        compiler_params=pltpu.CompilerParams(vmem_limit_bytes=48 * 2**20),
    )(*blocks, jnp.asarray(taper_host(length)[None, :]), jnp.asarray(twiddle), jnp.asarray(table))


def row_kernel(shape, arrived, weight, twiddle, high_table, low_table, out, blocks, spread, folded):
    length, fold, step, parts, packed, factor = shape
    devices, tall, wide = arrived.shape
    per_device = packed // 2
    pieces = tall // packed
    code = arrived[...].astype(jnp.float32)
    scale = code[:, tall - packed :, wide - 1 :]
    value = decode(code, jnp.concatenate([scale] * pieces, axis=1))
    for piece in range(pieces):
        blocks[:, :, piece * wide : (piece + 1) * wide] = value[:, piece * packed : (piece + 1) * packed]
    width = blocks.shape[2]
    slots = LANES // step
    lane = lax.broadcasted_iota(jnp.int32, (packed, LANES), 1) // step
    sign = jnp.where(lax.broadcasted_iota(jnp.int32, (packed, INNER), 0) < per_device, 1.0, -1.0)

    for column in range(width // LANES):
        for half in range(devices // slots):
            tiles = [
                blocks[half * slots + g, :, column * LANES : (column + 1) * LANES] for g in range(slots)
            ]
            bit = 1
            while bit < slots:
                upper = (lane & bit) != 0
                for g in range(slots):
                    if g & bit:
                        continue
                    a, b = tiles[g], tiles[g + bit]
                    tiles[g] = jnp.where(upper, pltpu.roll(b, bit * step, 1), a)
                    tiles[g + bit] = jnp.where(upper, b, pltpu.roll(a, LANES - bit * step, 1))
                bit *= 2
            for g in range(slots):
                q = column * slots + g
                if q < fold * parts:
                    spread[q, :, half * LANES : (half + 1) * LANES] = tiles[g]

    def quarter(value):
        return pltpu.roll(value, per_device, 0) * sign

    place = lax.broadcasted_iota(jnp.int32, (packed, INNER), 1)
    for freq in range(fold):
        halo = spread[freq * parts + fold]
        run = 4 * step
        extra = {}
        for owner, (target, shift) in enumerate(
            ((fold - 2, -1), (fold - 1, -1 - step), (0, 2 * step), (1, step))
        ):
            inside = place != owner * step if owner < 2 else place != INNER - run + owner * step
            only = jnp.where((place % run == owner * step) & inside, halo, 0.0)
            moved = pltpu.roll(only, shift % INNER, 1)
            extra[target] = extra[target] + moved if target in extra else moved
        for point in range(fold):
            value = spread[freq * parts + point]
            if point in extra:
                value = value + extra[point]
            folded[(point * fold + freq) * packed : (point * fold + freq + 1) * packed, :] = (
                value * weight[point : point + 1, :]
            )

    high, low = split(folded[...])
    both = dot(jnp.concatenate([high, low], axis=0), high_table[...])
    result = both[: high.shape[0]] + both[high.shape[0] :] + dot(high, low_table[...])
    for freq in range(fold):
        points = []
        for point in range(fold):
            begin = (point * fold + freq) * packed
            rows = slice(begin, begin + packed)
            value = result[rows, :INNER] + quarter(result[rows, INNER:])
            if point:
                tc = twiddle[point : point + 1, :INNER]
                ts = twiddle[point : point + 1, INNER:]
                value = value * tc + quarter(value) * ts
            points.append(value)
        half = fold // 2
        sums = [points[j] + points[fold - j] for j in range(1, half + 1)]
        differences = [quarter(points[j] - points[fold - j]) for j in range(1, half + 1)]

        def keep(index, value):
            power = value * value
            power = (power + pltpu.roll(power, per_device, 0)) * factor
            for side in range(INNER // LANES):
                row = (freq * length + index * INNER) // LANES + side
                rows = pl.ds(row, per_device, stride=fold * length // LANES)
                out[rows, :] = power[:per_device, side * LANES : (side + 1) * LANES]

        keep(0, functools.reduce(jnp.add, sums, points[0]))
        for index in range(1, half + 1):
            even, odd = points[0], None
            for j in range(1, half + 1):
                angle = 2 * math.pi * ((j * index) % fold) / fold
                even = even + math.cos(angle) * sums[j - 1]
                term = math.sin(angle) * differences[j - 1]
                odd = term if odd is None else odd + term
            keep(index, even + odd)
            keep(fold - index, even - odd)


def row_transform(arrived, length, rows):
    devices, tall, wide = arrived.shape
    packed = INNER // devices
    fold = length // INNER
    step = length // fold // devices
    angle = angles_host(np.arange(fold), np.arange(INNER), length)
    twiddle = np.concatenate([np.cos(angle), np.sin(angle)], axis=1).astype(np.float32)
    angle = angles_host(np.arange(INNER), np.arange(INNER), INNER)
    high_table, low_table = split_host(np.concatenate([np.cos(angle), np.sin(angle)], axis=1))
    parts = rows // step
    weight = np.ascontiguousarray(taper_host(length).reshape(INNER, fold).T)
    shape = (length, fold, step, parts, packed, STRIDE / (length * length))
    return pl.pallas_call(
        functools.partial(row_kernel, shape),
        out_shape=jax.ShapeDtypeStruct((fold * packed // 2 * length // LANES, LANES), jnp.float32),
        scratch_shapes=[
            pltpu.VMEM((devices, packed, tall * wide // packed), jnp.float32),
            pltpu.VMEM((fold * parts, packed, INNER), jnp.float32),
            pltpu.VMEM((fold * fold * packed, INNER), jnp.float32),
        ],
        compiler_params=pltpu.CompilerParams(vmem_limit_bytes=48 * 2**20),
    )(arrived, jnp.asarray(weight), jnp.asarray(twiddle), jnp.asarray(high_table), jnp.asarray(low_table))


def local(field):
    owners = lax.axis_size("cols")
    devices = lax.axis_size("rows") * owners
    length = field.shape[1] // STRIDE * lax.axis_size("rows")
    fold = length // INNER
    cut = cut_filter(field, owners, fold)
    grouped = [cut[0]] * owners
    for distance in reversed(range(1, owners)):
        pairs = [(col, col ^ distance) for col in range(owners)]
        grouped[distance] = lax.ppermute(cut[distance], "cols", pairs)
    partial = column_transform(grouped, length, devices)
    arrived = lax.all_to_all(partial, ("rows", "cols"), split_axis=0, concat_axis=0, tiled=True)
    return row_transform(arrived, length, grouped[0].shape[0]).reshape(1, -1, length)


def solution(mesh):
    return jax.shard_map(
        local,
        mesh=mesh,
        in_specs=(P(None, "rows", "cols"),),
        out_specs=P(None, ("rows", "cols"), None),
        check_vma=False,
    )
```
